512 devices in a mesh: dom: 128 (over y, z, core), cls: 4 (over x).
Axes of the slice: x: 4, y: 4, z: 16, core: 2. Of those that a mesh axis runs over, the one named last changes fastest.
Arguments:
- images: bfloat16 [16384, 64, 256], P('dom', 'cls'), may hold values from -80 to 80
- references: bfloat16 [256, 64, 256], P('dom', 'cls'), may hold values from -6 to 6
- sharpness: bfloat16 [256], P('dom'), may hold values from 20 to 200
- classes: int32 [16384, 1], P('dom'), may hold values from 0 to 255; in each aligned block of 128 rows (0 to 127, 128 to 255, ...) at most 4 rows name the same one
- rotations: int32 [16384], P('dom'), may hold values from 0 to 255
- shifts: int32 [16384], P('dom'), may hold values from 0 to 24
- shift_phase: float32 [25, 64, 128], P(None, 'cls'), may hold values from -3.140625 to 3.140625
Outputs:
- class_sums: float32 [256, 64, 256], P('dom', 'cls')
- class_weights: float32 [256], P('dom')
The draws below stay inside these ranges and needn't reach their ends.
Inputs may be any that keep to these rules, and one draw needn't show every extreme that they name: `classes`: within the rows of one device (aligned blocks of 128 particles) no class is named by more than 4 particles, a bound that some block reaches; every class is named by some particle.
All inputs are finite; a program needn't handle non-finite values.
Results may differ from the reference program's by a relative error of at most 0.0048.
Values may be sent and summed in bfloat16 or wider, within the bound.
No kernel may reach another device: no remote copies, remote signals or barrier semaphores. Data moves between devices by JAX's collectives and lax.ppermute only.
A program may use at most 64 MiB of HBM per device.

```python
import math
import jax
import jax.numpy as jnp
import numpy as np
from jax import lax

R = 64
A = 256
FREQS = 128
C = 256
NSH = 25
MOST = 4
P_DEV = 128
PARTICLES = 16384


def draw_images(key, part):
    key = jax.random.fold_in(key, 11)
    key_base, key_cycle, key_angle = jax.random.split(key, 3)
    shape = (PARTICLES, R, A)
    base = jnp.clip(jax.random.normal(key_base, shape, jnp.float32), -4.0, 4.0)
    cycle_scale = jnp.exp(jax.random.uniform(key_cycle, (PARTICLES, R, 1), jnp.float32) * math.log(10.0))
    angle_scale = jnp.exp(jax.random.uniform(key_angle, (PARTICLES, 1, A), jnp.float32) * math.log(2.0))
    return (base * cycle_scale * angle_scale).astype(jnp.bfloat16)


def plant(result, stream_key, least, largest):
    dims = result.shape
    index_at = [jax.random.randint(jax.random.fold_in(stream_key, axis), (), 0, dims[axis]) for axis in range(len(dims))]
    result = result.at[tuple(index_at)].set(least)
    longest = dims.index(max(dims))
    index_at[longest] = (index_at[longest] + 1) % dims[longest]
    return result.at[tuple(index_at)].set(largest)


def steps_of(stream_key, extent, cuts, least, top_value):
    factor_of = 1.0
    for axis_at, shards_of in cuts:
        heights = jax.random.uniform(jax.random.fold_in(jax.random.fold_in(stream_key, 6), axis_at), (shards_of,), jnp.float32, least / len(cuts), top_value / len(cuts))
        factor_of = factor_of * jnp.repeat(jnp.exp(heights), extent[axis_at] // shards_of).reshape((-1,) + (1,) * (len(extent) - 1 - axis_at))
    return factor_of


def deal_out(own_key, own, number, rows, number_of, top, bound, skew):
    sequence = jax.random.permutation(own_key, number_of)
    heavy_load, usual = shares(number_of, rows * top, bound, skew, True), shares(number_of, rows * top, bound, skew, False)
    places = jnp.arange(number_of)

    def named(tallies, offset_by):
        used = int((tallies > 0).sum())
        fixed = max(1, used // 4)
        passed = fixed + (places - fixed + offset_by * (used - fixed)) % max(1, number_of - fixed)
        return jnp.zeros((number_of,), jnp.int32).at[sequence[jnp.where(places < fixed, places, passed)]].set(jnp.asarray(tallies, jnp.int32))

    tallies = jnp.where(number % 4 == 0, named(heavy_load, number // 4), named(usual, number - number // 4 - 1))
    mixed = jax.random.permutation(jax.random.fold_in(own, 3), number_of)
    giver, sink = mixed[0:number_of // 2 * 2:2], mixed[1:number_of // 2 * 2:2]
    room = jnp.minimum(tallies[giver] - 1, bound - tallies[sink]) // 2
    room = jnp.where((giver == sequence[0]) | (sink == sequence[0]) | (tallies[sink] == 0), 0, jnp.maximum(room, 0))
    passed = jax.random.randint(jax.random.fold_in(own, 4), (number_of // 2,), 0, 1 << 20) % (room + 1)
    tallies = tallies.at[giver].add(-passed).at[sink].add(passed)
    members = jnp.searchsorted(jnp.cumsum(tallies), jnp.arange(rows * top), side="right").astype(jnp.int32)
    grid = members.reshape(top, rows).T
    grid = grid[jax.random.permutation(jax.random.fold_in(own, 1), rows)]
    offset_by = jax.random.randint(jax.random.fold_in(own, 2), (rows, 1), 0, top)
    return jnp.take_along_axis(grid, (jnp.arange(top)[None, :] + offset_by) % top, axis=1)


def shares(number_of, total, limit, skew, full):
    weights = [(1 << 20) // math.isqrt(standing ** skew) + 1 for standing in range(1, number_of + 1)]
    largest = limit if full else min(limit, max(-(-total // number_of), total * weights[0] // sum(weights)))
    least = 1 if total - largest >= number_of - 1 else 0
    counts, surplus = [largest] + [least] * (number_of - 1), total - largest - least * (number_of - 1)
    while surplus > 0:
        movable = [i for i in range(1, number_of) if counts[i] < largest] or [i for i in range(1, number_of) if counts[i] < limit]
        whole, budget = sum([weights[i] for i in movable]), surplus
        for i in movable:
            more = min(limit - counts[i], max(1, budget * weights[i] // whole), surplus)
            counts[i] = counts[i] + more
            surplus = surplus - more
    return np.array(counts)


def gaussian(own_key, extent, spread, bound, shards=(), held_as=jnp.bfloat16):
    entries = jax.random.normal(own_key, extent, jnp.float32) * spread
    if len(shards) > 0:
        entries = steps_of(own_key, extent, shards, -0.22, 0.18) * entries
    return jnp.clip(entries, min=-bound, max=bound).astype(held_as)


def setup_inputs(seed: int = 0) -> dict:
    streams_of = jax.random.split(jax.random.key(seed), 8)
    images = draw_images(jax.random.fold_in(streams_of[7], 71), 0)
    references = gaussian(streams_of[1], (C, R, A), 1.0, 6.0, ((0, 128), (1, 4)))
    sharpness = jnp.clip(jnp.exp(math.log(200.0) - 2.3025851 * jax.random.uniform(streams_of[2], (C,), jnp.float32) ** steps_of(streams_of[2], (C,), ((0, 128),), -0.2, 0.2)), 20.0, 200.0).astype(jnp.bfloat16)
    classes_keys = jax.random.split(jax.random.fold_in(streams_of[3], 1), PARTICLES // P_DEV)
    classes_turns = jax.random.permutation(jax.random.fold_in(streams_of[3], 3), PARTICLES // P_DEV)
    classes = jax.vmap(lambda own, number: deal_out(jax.random.fold_in(streams_of[3], 2), own, number, P_DEV, C, 1, MOST, 2))(classes_keys, classes_turns).reshape((PARTICLES, 1))
    rotations = plant(jax.random.randint(streams_of[4], (PARTICLES,), 0, A), jax.random.fold_in(streams_of[4], 1), 0, A - 1).astype(jnp.int32)
    shifts = plant(jax.random.randint(streams_of[5], (PARTICLES,), 0, NSH), jax.random.fold_in(streams_of[5], 1), 0, NSH - 1).astype(jnp.int32)
    shift_phase = jnp.clip(jax.random.uniform(streams_of[6], (NSH, R, FREQS), jnp.float32, -3.140625, 3.140625), -3.140625, 3.140625)
    return dict(images=images, references=references, sharpness=sharpness, classes=classes, rotations=rotations, shifts=shifts, shift_phase=shift_phase)


EPSILON = 1e-06

def spectral_table(length):
    half_len = length // 2
    angle_index = jnp.arange(length, dtype=jnp.int32)
    freq_index = jnp.arange(half_len, dtype=jnp.int32)
    turn_count = angle_index[:, None] * freq_index[None, :] % length
    radians = turn_count.astype(jnp.float32) * (2.0 * math.pi / length)
    norm_scale = 1.0 / math.sqrt(length)
    both = jnp.concatenate([jnp.cos(radians), -jnp.sin(radians)], 1) * norm_scale
    return both.astype(jnp.bfloat16)

def align_block(image_blk, rot_blk, phases, dft_table):
    rows_dev, cycle_count, length = image_blk.shape
    half_len = length // 2
    flat_rows = image_blk.reshape(rows_dev * cycle_count, length).astype(jnp.float32)
    spectra = jnp.dot(flat_rows, dft_table.astype(jnp.float32), precision=lax.Precision.HIGHEST)
    spectra = spectra.reshape(rows_dev, cycle_count, length)
    freq_index = jnp.arange(half_len, dtype=jnp.int32)
    turn_count = rot_blk[:, None] * freq_index[None, :] % length
    phase_angle = turn_count.astype(jnp.float32)[:, None, :] * (2.0 * math.pi / length) + phases
    cosine = jnp.cos(phase_angle)
    sine_val = jnp.sin(phase_angle)
    real_part = spectra[:, :, :half_len]
    imag_part = spectra[:, :, half_len:]
    out_real = real_part * cosine - imag_part * sine_val
    out_imag = real_part * sine_val + imag_part * cosine
    return jnp.concatenate([out_real, out_imag], -1).astype(jnp.bfloat16)

def reference(images, references, sharpness, classes, rotations, shifts, shift_phase):
    dft_table = spectral_table(A)
    labels_all = classes[:, 0]
    block_total = PARTICLES // P_DEV

    def block_step(carry, block_id):
        class_sum, totals = carry
        start = (block_id * P_DEV).astype(jnp.int32)
        image_blk = lax.dynamic_slice_in_dim(images, start, P_DEV, 0)
        labels = lax.dynamic_slice_in_dim(labels_all, start, P_DEV, 0)
        rot_blk = lax.dynamic_slice_in_dim(rotations, start, P_DEV, 0)
        shift_blk = lax.dynamic_slice_in_dim(shifts, start, P_DEV, 0)
        phases = shift_phase[shift_blk]
        aligned = align_block(image_blk, rot_blk, phases, dft_table).astype(jnp.float32)
        own_ref = references[labels].astype(jnp.float32)
        inner_sum = lax.optimization_barrier(jnp.sum(aligned * own_ref, axis=(1, 2)))
        power = lax.optimization_barrier(jnp.sum(aligned * aligned, axis=(1, 2)))
        ref_power = lax.optimization_barrier(jnp.sum(own_ref * own_ref, axis=(1, 2)))
        correlation = inner_sum / jnp.sqrt((power + EPSILON) * (ref_power + EPSILON))
        weight = jax.nn.sigmoid(sharpness[labels].astype(jnp.float32) * correlation)
        weight = lax.optimization_barrier(weight.astype(jnp.bfloat16)).astype(jnp.float32)
        class_sum = class_sum.at[labels].add(weight[:, None, None] * aligned)
        totals = totals.at[labels].add(weight)
        return ((class_sum, totals), None)
    start_sums = jnp.zeros((C, R, A), jnp.float32)
    start_totals = jnp.zeros((C,), jnp.float32)
    (class_sum, totals), _ = lax.scan(block_step, (start_sums, start_totals), jnp.arange(block_total, dtype=jnp.int32))
    return (class_sum, totals)
```

```python
import math

import jax
import jax.numpy as jnp
from jax import lax
from jax.experimental import pallas as pl
from jax.experimental.pallas import tpu as pltpu
from jax.sharding import Mesh
from jax.sharding import PartitionSpec as P

C = 256
EPSILON = 1e-06
NY, NZ, NX = 4, 16, 4
P_DEV = 128
R_DEV = 16
A = 256
FREQS = 128
R_OWN = R_DEV // NY
WIDE = R_OWN * A
FULL = WIDE + 128
SHIFT_ROWS = 32
VMEM_LIMIT = 40 * 1024 * 1024


def spectral_table(length):
    half_len = length // 2
    angle_index = jnp.arange(length, dtype=jnp.int32)
    freq_index = jnp.arange(half_len, dtype=jnp.int32)
    turn_count = angle_index[:, None] * freq_index[None, :] % length
    radians = turn_count.astype(jnp.float32) * (2.0 * math.pi / length)
    norm_scale = 1.0 / math.sqrt(length)
    both = jnp.concatenate([jnp.cos(radians), -jnp.sin(radians)], 1) * norm_scale
    return both.astype(jnp.bfloat16)


def iota(shape, axis):
    return lax.broadcasted_iota(jnp.int32, shape, axis)


def align_kernel(
    y_ref, images, table, rot, shift, label_row, phases, out0, out1, out2, out3, parts, turn, grid
):
    y = y_ref[0]
    for r in range(R_DEV):
        phase = phases[r]
        for at, value in ((0, jnp.cos(phase)), (FREQS, jnp.sin(phase))):
            high = value.astype(jnp.bfloat16)
            low = (value - high.astype(jnp.float32)).astype(jnp.bfloat16)
            lanes = slice(r * A + at, r * A + at + FREQS)
            parts[0:SHIFT_ROWS, lanes] = high
            parts[SHIFT_ROWS : 2 * SHIFT_ROWS, lanes] = low
    pick = (iota((P_DEV, 2 * SHIFT_ROWS), 1) & (SHIFT_ROWS - 1)) == shift[...]
    pick = pick.astype(jnp.float32).astype(jnp.bfloat16)
    turn[:, : R_DEV * A] = jnp.dot(pick, parts[...], preferred_element_type=jnp.float32)
    angle = ((rot[...] * iota((P_DEV, FREQS), 1)) & (A - 1)).astype(jnp.float32) * (2.0 * math.pi / A)
    turn[:, R_DEV * A : R_DEV * A + FREQS] = jnp.cos(angle)
    turn[:, R_DEV * A + FREQS :] = jnp.sin(angle)
    row, col = iota((A, A), 0), iota((A, A), 1)
    swap = (col == ((row & 15) * 16 + (row >> 4))).astype(jnp.float32).astype(jnp.bfloat16)
    dft = table[...]

    def block(b, _):
        rows = pl.ds(pl.multiple_of(b * 16, 16), 16)
        x = images[pl.ds(pl.multiple_of(b * 256, 256), 256), :]
        x = jnp.dot(swap, x, preferred_element_type=jnp.float32).astype(jnp.bfloat16)
        spectra = jnp.dot(x, dft, preferred_element_type=jnp.float32)
        cos_rot = turn[rows, R_DEV * A : R_DEV * A + FREQS]
        sin_rot = turn[rows, R_DEV * A + FREQS :]
        for r in range(R_DEV):
            cos_shift = turn[rows, r * A : r * A + FREQS]
            sin_shift = turn[rows, r * A + FREQS : r * A + A]
            cosine = cos_shift * cos_rot - sin_shift * sin_rot
            sine = sin_shift * cos_rot + cos_shift * sin_rot
            real = spectra[r * 16 : r * 16 + 16, :FREQS]
            imag = spectra[r * 16 : r * 16 + 16, FREQS:]
            grid[r, rows, :FREQS] = (real * cosine - imag * sine).astype(jnp.bfloat16)
            grid[r, rows, FREQS:] = (real * sine + imag * cosine).astype(jnp.bfloat16)
        return 0

    lax.fori_loop(0, P_DEV // 16, block, 0)
    label = label_row[...]
    label = ((label >> 1) & 1) * 128 + (label >> 2) * 2 + (label & 1)
    tail = jnp.broadcast_to(label.astype(jnp.float32), (P_DEV, 128)).astype(jnp.bfloat16)
    for d, out in enumerate((out0, out1, out2, out3)):
        first = ((y + d) & (NY - 1)) * R_OWN
        for i in range(R_OWN):
            out[:, i * A : i * A + A] = grid[first + i]
        out[:, WIDE:] = tail


def score_kernel(y_ref, a0, a1, a2, a3, panel, out, rows_out, stats):
    y = y_ref[0]
    refs = panel[:, :WIDE]
    wide = refs.astype(jnp.float32)
    norm = jnp.sum(wide * wide, axis=1, keepdims=True)
    sharp = panel[:, WIDE:].astype(jnp.float32)
    diagonal = iota((P_DEV, P_DEV), 0) == iota((P_DEV, P_DEV), 1)
    for d, rows in enumerate((a0, a1, a2, a3)):
        source = (y - d) & (NY - 1)
        flat = rows[:, :WIDE]
        label = rows[0:16, WIDE:].astype(jnp.float32)[0:1].astype(jnp.int32)
        member = iota((C, P_DEV), 0) == label
        scores = lax.dot_general(
            refs, flat, (((1,), (1,)), ((), ())), preferred_element_type=jnp.float32
        )
        gram = lax.dot_general(
            flat, flat, (((1,), (1,)), ((), ())), preferred_element_type=jnp.float32
        )
        inner = jnp.sum(jnp.where(member, scores, 0.0), axis=0, keepdims=True)
        power = jnp.sum(jnp.where(diagonal, gram, 0.0), axis=0, keepdims=True)
        ref_power = jnp.sum(jnp.where(member, norm, 0.0), axis=0, keepdims=True)
        own_sharp = jnp.sum(jnp.where(member, sharp, 0.0), axis=0, keepdims=True)
        for at, value in enumerate((inner, power, ref_power, own_sharp)):
            stats[pl.ds(at * NY + source, 1), :] = value
    value = stats[...]
    rows_out[...] = value
    for i in range(NX * NY):
        out[i] = value


def sum_kernel(at_ref, got, own, a0, a1, a2, a3, keep, send, weights):
    y, core = at_ref[0], at_ref[1]
    total = got[0]
    for i in range(1, NX * NY):
        total = total + got[i]
    inner, power, ref_power = total[0:NY], total[NY : 2 * NY], total[2 * NY : 3 * NY]
    sharp = own[3 * NY : 4 * NY, :]
    correlation = inner / jnp.sqrt((power + EPSILON) * (ref_power + EPSILON))
    weight = 1.0 / (1.0 + jnp.exp(-(sharp * correlation)))
    weights[0:NY, :] = weight.astype(jnp.bfloat16).astype(jnp.float32)
    parts = []
    for d, rows in enumerate((a0, a1, a2, a3)):
        source = (y - d) & (NY - 1)
        label = rows[0:16, WIDE:].astype(jnp.float32)[0:1].astype(jnp.int32) ^ (core * 128)
        member = iota((C, P_DEV), 0) == label
        parts.append(jnp.where(member, weights[pl.ds(source, 1), :], 0.0).astype(jnp.bfloat16))
    spread = jnp.concatenate(parts, axis=1)
    for i in range(R_OWN):
        lanes = slice(i * A, i * A + A)
        flat = jnp.concatenate([a0[:, lanes], a1[:, lanes], a2[:, lanes], a3[:, lanes]], axis=0)
        sums = jnp.dot(spread, flat, preferred_element_type=jnp.float32)
        keep[:, lanes] = sums[:128]
        send[:, lanes] = sums[128:]
    ones = jnp.ones((NY * P_DEV, 128), jnp.bfloat16)
    sums = jnp.dot(spread, ones, preferred_element_type=jnp.float32)
    keep[:, WIDE:] = sums[:128]
    send[:, WIDE:] = sums[128:]


def call(kernel, name, outs, scratch, flops, nbytes, n_scalar, n_vector):
    vmem = pl.BlockSpec(memory_space=pltpu.VMEM)
    smem = pl.BlockSpec(memory_space=pltpu.SMEM)
    return pl.pallas_call(
        kernel,
        out_shape=outs,
        in_specs=[smem] * n_scalar + [vmem] * n_vector,
        out_specs=jax.tree.map(lambda _: vmem, outs),
        scratch_shapes=scratch,
        compiler_params=pltpu.CompilerParams(vmem_limit_bytes=VMEM_LIMIT),
        cost_estimate=pl.CostEstimate(flops=flops, bytes_accessed=nbytes, transcendentals=0),
        name=name,
    )


def body(images, references, sharpness, classes, rotations, shifts, shift_phase):
    y = lax.axis_index("y").astype(jnp.int32)
    core = lax.axis_index("core").astype(jnp.int32)
    shape = jax.ShapeDtypeStruct

    pieces = references.reshape(2, NY, WIDE).transpose(1, 0, 2)
    sharp_tile = jnp.broadcast_to(sharpness[None, :, None], (NY, 2, 128))
    pieces = jnp.concatenate([pieces, sharp_tile], axis=2)
    pieces = jnp.broadcast_to(pieces[:, None], (NY, NZ, 2, FULL)).reshape(NY * NZ, 2, FULL)
    panel = lax.all_to_all(pieces, ("y", "z"), split_axis=0, concat_axis=0, tiled=True)

    phases = jnp.pad(shift_phase.transpose(1, 0, 2), ((0, 0), (0, SHIFT_ROWS - 25), (0, 0)))
    block = shape((P_DEV, FULL), jnp.bfloat16)
    aligned = call(
        align_kernel,
        "align",
        [block] * NY,
        [
            pltpu.VMEM((2 * SHIFT_ROWS, R_DEV * A), jnp.bfloat16),
            pltpu.VMEM((P_DEV, R_DEV * A + A), jnp.float32),
            pltpu.VMEM((R_DEV, P_DEV, A), jnp.bfloat16),
        ],
        800_000_000,
        4_000_000,
        1,
        6,
    )(
        y[None],
        images.reshape(P_DEV * R_DEV, A),
        spectral_table(A),
        rotations[:, None],
        shifts[:, None],
        classes.reshape(1, P_DEV),
        phases,
    )
    rows = [aligned[0]]
    for d in range(1, NY):
        rows.append(lax.ppermute(aligned[d], "y", [(i, (i + d) % NY) for i in range(NY)]))

    panel = lax.all_gather(panel.reshape(NY * NZ * 2, FULL), "core", axis=0, tiled=True)
    payload, stats = call(
        score_kernel,
        "score",
        [shape((NX * NY, 4 * NY, P_DEV), jnp.float32), shape((4 * NY, P_DEV), jnp.float32)],
        [pltpu.VMEM((4 * NY, P_DEV), jnp.float32)],
        600_000_000,
        2_000_000,
        1,
        5,
    )(y[None], *rows, panel)
    got = lax.all_to_all(payload, ("x", "y"), split_axis=0, concat_axis=0, tiled=True)
    half = shape((128, FULL), jnp.float32)
    keep, send = call(
        sum_kernel,
        "sum",
        [half, half],
        [pltpu.VMEM((8, P_DEV), jnp.float32)],
        300_000_000,
        3_000_000,
        1,
        6,
    )(jnp.stack([y, core]), got, stats, *rows)
    sums = keep + lax.ppermute(send, "core", [(0, 1), (1, 0)])
    totals = sums[:, WIDE : WIDE + 64]
    high = totals.astype(jnp.bfloat16)
    low = (totals - high.astype(jnp.float32)).astype(jnp.bfloat16)
    sums = jnp.concatenate([sums[:, :WIDE].astype(jnp.bfloat16), high, low], axis=1)
    sums = lax.all_to_all(
        sums.reshape(NY * NZ, 2, FULL), ("y", "z"), split_axis=0, concat_axis=0, tiled=True
    )
    sums = jnp.sum(sums.reshape(NY, NZ, 2, FULL).astype(jnp.float32), axis=1)
    class_sums = sums[:, :, :WIDE].reshape(NY, 2, R_OWN, A).transpose(1, 0, 2, 3)
    class_weights = sums[0, :, WIDE] + sums[0, :, WIDE + 64]
    return class_sums.reshape(2, R_DEV, A), class_weights


def solution(mesh):
    whole = Mesh(mesh.devices.reshape(NY, NZ, 2, NX), ("y", "z", "core", "x"))
    dom = ("y", "z", "core")
    return jax.shard_map(
        body,
        mesh=whole,
        in_specs=(
            P(dom, "x", None),
            P(dom, "x", None),
            P(dom),
            P(dom, None),
            P(dom),
            P(dom),
            P(None, "x", None),
        ),
        out_specs=(P(dom, "x", None), P(dom)),
        check_vma=False,
    )
```

```python
import math

import jax
import jax.numpy as jnp
from jax import lax
from jax.experimental import pallas as pl
from jax.experimental.pallas import tpu as pltpu
from jax.sharding import Mesh
from jax.sharding import PartitionSpec as P

C = 256
EPSILON = 1e-06
NY, NZ, NX = 4, 16, 4
P_DEV = 128
R_DEV = 16
A = 256
FREQS = 128
R_OWN = R_DEV // NY
WIDE = R_OWN * A
FULL = WIDE + 128
SHIFT_ROWS = 32
VMEM_LIMIT = 40 * 1024 * 1024


def spectral_table(length):
    half_len = length // 2
    angle_index = jnp.arange(length, dtype=jnp.int32)
    freq_index = jnp.arange(half_len, dtype=jnp.int32)
    turn_count = angle_index[:, None] * freq_index[None, :] % length
    radians = turn_count.astype(jnp.float32) * (2.0 * math.pi / length)
    norm_scale = 1.0 / math.sqrt(length)
    both = jnp.concatenate([jnp.cos(radians), -jnp.sin(radians)], 1) * norm_scale
    return both.astype(jnp.bfloat16)


def iota(shape, axis):
    return lax.broadcasted_iota(jnp.int32, shape, axis)


def deal_kernel(
    y_ref, images, label_row, rot_row, shift_row, out0, out1, out2, out3, grid
):
    y = y_ref[0]
    row, col = iota((A, A), 0), iota((A, A), 1)
    swap = (col == ((row & 15) * 16 + (row >> 4))).astype(jnp.float32).astype(jnp.bfloat16)
    for b in range(P_DEV // 16):
        x = jnp.dot(swap, images[b * A : b * A + A, :], preferred_element_type=jnp.float32)
        x = x.astype(jnp.bfloat16)
        for r in range(R_DEV):
            grid[r, b * 16 : b * 16 + 16, :] = x[r * 16 : r * 16 + 16]
    label = label_row[...]
    label = ((label >> 1) & 1) * 128 + (label >> 2) * 2 + (label & 1)
    at = iota((P_DEV, P_DEV), 0)
    tail = jnp.where(at == 0, label, jnp.where(at == 1, rot_row[...], shift_row[...]))
    tail = tail.astype(jnp.float32).astype(jnp.bfloat16)
    for d, out in enumerate((out0, out1, out2, out3)):
        first = ((y + d) & (NY - 1)) * R_OWN
        for i in range(R_OWN):
            out[:, i * A : i * A + A] = grid[first + i]
        out[:, WIDE:] = tail


def align_kernel(in0, in1, in2, in3, table, phases, out, parts):
    for r in range(R_OWN):
        phase = phases[r]
        for at, value in ((0, jnp.cos(phase)), (FREQS, jnp.sin(phase))):
            high = value.astype(jnp.bfloat16)
            low = (value - high.astype(jnp.float32)).astype(jnp.bfloat16)
            lanes = slice(r * A + at, r * A + at + FREQS)
            parts[0:SHIFT_ROWS, lanes] = high
            parts[SHIFT_ROWS : 2 * SHIFT_ROWS, lanes] = low
    dft = table[...]
    diagonal = iota((P_DEV, P_DEV), 0) == iota((P_DEV, P_DEV), 1)
    lane = iota((P_DEV, P_DEV), 1)
    for d, block in enumerate((in0, in1, in2, in3)):
        rows = slice(d * P_DEV, d * P_DEV + P_DEV)
        tail = block[0:16, WIDE:].astype(jnp.float32)
        rot = jnp.sum(jnp.where(diagonal, tail[1:2], 0.0), axis=1, keepdims=True)
        shift = jnp.sum(jnp.where(diagonal, tail[2:3], 0.0), axis=1, keepdims=True)
        angle = ((rot.astype(jnp.int32) * lane) & (A - 1)).astype(jnp.float32) * (2.0 * math.pi / A)
        cos_rot, sin_rot = jnp.cos(angle), jnp.sin(angle)
        pick = (lane[:, : 2 * SHIFT_ROWS] & (SHIFT_ROWS - 1)) == shift.astype(jnp.int32)
        pick = pick.astype(jnp.float32).astype(jnp.bfloat16)
        for i in range(R_OWN):
            lanes = slice(i * A, i * A + A)
            turn = jnp.dot(pick, parts[:, lanes], preferred_element_type=jnp.float32)
            spectra = jnp.dot(block[:, lanes], dft, preferred_element_type=jnp.float32)
            cosine = turn[:, :FREQS] * cos_rot - turn[:, FREQS:] * sin_rot
            sine = turn[:, FREQS:] * cos_rot + turn[:, :FREQS] * sin_rot
            real, imag = spectra[:, :FREQS], spectra[:, FREQS:]
            out[rows, i * A : i * A + FREQS] = (real * cosine - imag * sine).astype(jnp.bfloat16)
            out[rows, i * A + FREQS : i * A + A] = (real * sine + imag * cosine).astype(jnp.bfloat16)
        out[rows, WIDE:] = block[:, WIDE:]


def score_kernel(y_ref, rows, panel, out, stats):
    y = y_ref[0]
    refs = panel[:, :WIDE]
    wide = refs.astype(jnp.float32)
    norm = jnp.sum(wide * wide, axis=1, keepdims=True)
    sharp = panel[:, WIDE:].astype(jnp.float32)
    diagonal = iota((P_DEV, P_DEV), 0) == iota((P_DEV, P_DEV), 1)
    for d in range(NY):
        source = (y - d) & (NY - 1)
        flat = rows[d * P_DEV : d * P_DEV + P_DEV, :WIDE]
        label = rows[d * P_DEV : d * P_DEV + 16, WIDE:].astype(jnp.float32)[0:1].astype(jnp.int32)
        member = iota((C, P_DEV), 0) == label
        scores = lax.dot_general(
            refs, flat, (((1,), (1,)), ((), ())), preferred_element_type=jnp.float32
        )
        gram = lax.dot_general(
            flat, flat, (((1,), (1,)), ((), ())), preferred_element_type=jnp.float32
        )
        inner = jnp.sum(jnp.where(member, scores, 0.0), axis=0, keepdims=True)
        power = jnp.sum(jnp.where(diagonal, gram, 0.0), axis=0, keepdims=True)
        ref_power = jnp.sum(jnp.where(member, norm, 0.0), axis=0, keepdims=True)
        own_sharp = jnp.sum(jnp.where(member, sharp, 0.0), axis=0, keepdims=True)
        for at, value in enumerate((inner, power, ref_power, own_sharp)):
            stats[pl.ds(at * NY + source, 1), :] = value
    value = stats[...]
    for i in range(NX * NY * 2):
        out[i] = value


def sum_kernel(at_ref, got, own, other, out, weights):
    y, core = at_ref[0], at_ref[1]
    for c in range(2):
        total = got[c]
        for i in range(1, NX * NY):
            total = total + got[2 * i + c]
        inner, power, ref_power = total[0:NY], total[NY : 2 * NY], total[2 * NY : 3 * NY]
        sharp = got[c][3 * NY : 4 * NY]
        correlation = inner / jnp.sqrt((power + EPSILON) * (ref_power + EPSILON))
        weight = jax.nn.sigmoid(sharp * correlation)
        weights[c * NY : c * NY + NY, :] = weight.astype(jnp.bfloat16).astype(jnp.float32)
    spread = []
    for rows, side in ((own, core), (other, 1 - core)):
        parts = []
        for d in range(NY):
            source = (y - d) & (NY - 1)
            first = d * P_DEV
            label = rows[first : first + 16, WIDE:].astype(jnp.float32)[0:1].astype(jnp.int32)
            member = iota((P_DEV, P_DEV), 0) == (label ^ (core * 128))
            weight = weights[pl.ds(side * NY + source, 1), :]
            parts.append(jnp.where(member, weight, 0.0).astype(jnp.bfloat16))
        spread.append(jnp.concatenate(parts, axis=1))
    for i in range(R_OWN):
        lanes = slice(i * A, i * A + A)
        sums = jnp.dot(spread[0], own[:, lanes], preferred_element_type=jnp.float32)
        sums = sums + jnp.dot(spread[1], other[:, lanes], preferred_element_type=jnp.float32)
        out[:, lanes] = sums.astype(jnp.bfloat16)
    ones = jnp.ones((NY * P_DEV, P_DEV), jnp.bfloat16)
    sums = jnp.dot(spread[0], ones, preferred_element_type=jnp.float32)
    sums = sums + jnp.dot(spread[1], ones, preferred_element_type=jnp.float32)
    high = sums.astype(jnp.bfloat16).astype(jnp.float32)
    sums = jnp.where(iota((P_DEV, P_DEV), 1) < 64, high, sums - high)
    out[:, WIDE:] = sums.astype(jnp.bfloat16)


def call(kernel, name, outs, scratch, flops, nbytes, n_scalar, n_vector):
    vmem = pl.BlockSpec(memory_space=pltpu.VMEM)
    smem = pl.BlockSpec(memory_space=pltpu.SMEM)
    return pl.pallas_call(
        kernel,
        out_shape=outs,
        in_specs=[smem] * n_scalar + [vmem] * n_vector,
        out_specs=jax.tree.map(lambda _: vmem, outs),
        scratch_shapes=scratch,
        compiler_params=pltpu.CompilerParams(vmem_limit_bytes=VMEM_LIMIT),
        cost_estimate=pl.CostEstimate(flops=flops, bytes_accessed=nbytes, transcendentals=0),
        name=name,
    )


def body(images, references, sharpness, classes, rotations, shifts, shift_phase):
    y = lax.axis_index("y").astype(jnp.int32)
    core = lax.axis_index("core").astype(jnp.int32)
    shape = jax.ShapeDtypeStruct

    pieces = references.reshape(2, NY, WIDE).transpose(1, 0, 2)
    sharp_tile = jnp.broadcast_to(sharpness[None, :, None], (NY, 2, 128))
    pieces = jnp.concatenate([pieces, sharp_tile], axis=2)
    pieces = jnp.broadcast_to(pieces[:, None], (NY, NZ, 2, FULL)).reshape(NY * NZ, 2, FULL)
    panel = lax.all_to_all(pieces, ("y", "z"), split_axis=0, concat_axis=0, tiled=True)

    block = shape((P_DEV, FULL), jnp.bfloat16)
    dealt = call(
        deal_kernel,
        "deal",
        [block] * NY,
        [pltpu.VMEM((R_DEV, P_DEV, A), jnp.bfloat16)],
        300_000_000,
        3_000_000,
        1,
        4,
    )(
        y[None],
        images.reshape(P_DEV * R_DEV, A),
        classes.reshape(1, P_DEV),
        rotations.reshape(1, P_DEV),
        shifts.reshape(1, P_DEV),
    )
    blocks = [dealt[0]]
    for d in range(1, NY):
        blocks.append(lax.ppermute(dealt[d], "y", [(i, (i + d) % NY) for i in range(NY)]))
    phases = lax.dynamic_slice_in_dim(shift_phase, y * R_OWN, R_OWN, 1).transpose(1, 0, 2)
    phases = jnp.pad(phases, ((0, 0), (0, SHIFT_ROWS - 25), (0, 0)))
    rows = call(
        align_kernel,
        "align",
        shape((NY * P_DEV, FULL), jnp.bfloat16),
        [pltpu.VMEM((2 * SHIFT_ROWS, WIDE), jnp.bfloat16)],
        800_000_000,
        4_000_000,
        0,
        6,
    )(*blocks, spectral_table(A), phases)

    panel = lax.all_gather(panel.reshape(NY * NZ * 2, FULL), "core", axis=0, tiled=True)
    payload = call(
        score_kernel,
        "score",
        shape((NX * NY * 2, 4 * NY, P_DEV), jnp.float32),
        [pltpu.VMEM((4 * NY, P_DEV), jnp.float32)],
        600_000_000,
        2_000_000,
        1,
        2,
    )(y[None], rows, panel)
    got = lax.all_to_all(payload, ("x", "y", "core"), split_axis=0, concat_axis=0, tiled=True)
    other = lax.ppermute(rows, "core", [(0, 1), (1, 0)])
    sums = call(
        sum_kernel,
        "sum",
        shape((P_DEV, FULL), jnp.bfloat16),
        [pltpu.VMEM((2 * NY, P_DEV), jnp.float32)],
        300_000_000,
        3_000_000,
        1,
        3,
    )(jnp.stack([y, core]), got, rows, other)
    sums = lax.all_to_all(
        sums.reshape(NY * NZ, 2, FULL), ("y", "z"), split_axis=0, concat_axis=0, tiled=True
    )
    sums = jnp.sum(sums.reshape(NY, NZ, 2, FULL).astype(jnp.float32), axis=1)
    class_sums = sums[:, :, :WIDE].reshape(NY, 2, R_OWN, A).transpose(1, 0, 2, 3)
    class_weights = sums[0, :, WIDE] + sums[0, :, WIDE + 64]
    return class_sums.reshape(2, R_DEV, A), class_weights


def solution(mesh):
    whole = Mesh(mesh.devices.reshape(NY, NZ, 2, NX), ("y", "z", "core", "x"))
    dom = ("y", "z", "core")
    return jax.shard_map(
        body,
        mesh=whole,
        in_specs=(
            P(dom, "x", None),
            P(dom, "x", None),
            P(dom),
            P(dom, None),
            P(dom),
            P(dom),
            P(None, "x", None),
        ),
        out_specs=(P(dom, "x", None), P(dom)),
        check_vma=False,
    )
```

```python
import math

import jax
import jax.numpy as jnp
from jax import lax
from jax.experimental import pallas as pl
from jax.experimental.pallas import tpu as pltpu
from jax.sharding import Mesh
from jax.sharding import PartitionSpec as P

C = 256
EPSILON = 1e-06
NY, NZ, NX = 4, 16, 4
P_DEV = 128
R_DEV = 16
A = 256
FREQS = 128
R_OWN = R_DEV // NY
WIDE = R_OWN * A
FULL = WIDE + 128
SHIFT_ROWS = 32
VMEM_LIMIT = 40 * 1024 * 1024


def spectral_table(length):
    half_len = length // 2
    angle_index = jnp.arange(length, dtype=jnp.int32)
    freq_index = jnp.arange(half_len, dtype=jnp.int32)
    turn_count = angle_index[:, None] * freq_index[None, :] % length
    radians = turn_count.astype(jnp.float32) * (2.0 * math.pi / length)
    norm_scale = 1.0 / math.sqrt(length)
    both = jnp.concatenate([jnp.cos(radians), -jnp.sin(radians)], 1) * norm_scale
    return both.astype(jnp.bfloat16)


def iota(shape, axis):
    return lax.broadcasted_iota(jnp.int32, shape, axis)


def deal_kernel(
    y_ref,
    images_hbm,
    refs_hbm,
    label_hbm,
    rot_hbm,
    shift_hbm,
    sharp,
    pieces,
    out0,
    out1,
    out2,
    out3,
    images,
    refs,
    ints,
    row_of,
    grid,
    sems,
):
    y = y_ref[0]
    copies = [
        pltpu.make_async_copy(source, target, sems.at[at])
        for at, (source, target) in enumerate(
            (
                (refs_hbm, refs),
                (label_hbm, ints.at[pl.ds(0, 1)]),
                (rot_hbm, ints.at[pl.ds(1, 1)]),
                (shift_hbm, ints.at[pl.ds(2, 1)]),
            )
        )
    ]
    quarter = P_DEV * R_DEV // 4
    for i in range(4):
        rows = pl.ds(i * quarter, quarter)
        copies.append(pltpu.make_async_copy(images_hbm.at[rows], images.at[rows], sems.at[4 + i]))
    for copy in copies:
        copy.start()
    for copy in copies[:4]:
        copy.wait()
    odd = (iota((2 * NZ, FULL), 0) & 1) == 1
    for j in range(2):
        wide = refs[j].astype(jnp.float32)
        for r in range(R_DEV):
            at = r // R_OWN * 2 + j
            lanes = slice(r % R_OWN * A, r % R_OWN * A + A)
            row_of[at : at + 1, lanes] = wide[r : r + 1]
        tile = jnp.broadcast_to(sharp[0:1, j : j + 1], (1, 128))
        for r in range(NY):
            row_of[2 * r + j : 2 * r + j + 1, WIDE:] = tile
    for r in range(NY):
        pair = jnp.where(odd, row_of[2 * r + 1 : 2 * r + 2, :], row_of[2 * r : 2 * r + 1, :])
        pieces[r * 2 * NZ : (r + 1) * 2 * NZ, :] = pair.astype(jnp.bfloat16)
    row, col = iota((A, A), 0), iota((A, A), 1)
    swap = (col == ((row & 15) * 16 + (row >> 4))).astype(jnp.float32).astype(jnp.bfloat16)
    for b in range(P_DEV // 16):
        if b % 2 == 0:
            copies[4 + b // 2].wait()
        x = jnp.dot(swap, images[b * A : b * A + A, :], preferred_element_type=jnp.float32)
        x = x.astype(jnp.bfloat16)
        for r in range(R_DEV):
            grid[r, b * 16 : b * 16 + 16, :] = x[r * 16 : r * 16 + 16]
    label = ints[0:1, :]
    label = ((label >> 1) & 1) * 128 + (label >> 2) * 2 + (label & 1)
    at = iota((P_DEV, P_DEV), 0)
    tail = jnp.where(at == 0, label, jnp.where(at == 1, ints[1:2, :], ints[2:3, :]))
    tail = tail.astype(jnp.float32).astype(jnp.bfloat16)
    for d, out in enumerate((out0, out1, out2, out3)):
        first = ((y + d) & (NY - 1)) * R_OWN
        for i in range(R_OWN):
            out[:, i * A : i * A + A] = grid[first + i]
        out[:, WIDE:] = tail


def align_kernel(in0, in1, in2, in3, table, phases, out, parts):
    for r in range(R_OWN):
        phase = phases[r]
        for at, value in ((0, jnp.cos(phase)), (FREQS, jnp.sin(phase))):
            high = value.astype(jnp.bfloat16)
            low = (value - high.astype(jnp.float32)).astype(jnp.bfloat16)
            lanes = slice(r * A + at, r * A + at + FREQS)
            parts[0:SHIFT_ROWS, lanes] = high
            parts[SHIFT_ROWS : 2 * SHIFT_ROWS, lanes] = low
    dft = table[...]
    diagonal = iota((P_DEV, P_DEV), 0) == iota((P_DEV, P_DEV), 1)
    lane = iota((P_DEV, P_DEV), 1)
    for d, block in enumerate((in0, in1, in2, in3)):
        rows = slice(d * P_DEV, d * P_DEV + P_DEV)
        tail = block[0:16, WIDE:].astype(jnp.float32)
        rot = jnp.sum(jnp.where(diagonal, tail[1:2], 0.0), axis=1, keepdims=True)
        shift = jnp.sum(jnp.where(diagonal, tail[2:3], 0.0), axis=1, keepdims=True)
        angle = ((rot.astype(jnp.int32) * lane) & (A - 1)).astype(jnp.float32) * (2.0 * math.pi / A)
        cos_rot, sin_rot = jnp.cos(angle), jnp.sin(angle)
        pick = (lane[:, : 2 * SHIFT_ROWS] & (SHIFT_ROWS - 1)) == shift.astype(jnp.int32)
        pick = pick.astype(jnp.float32).astype(jnp.bfloat16)
        for i in range(R_OWN):
            lanes = slice(i * A, i * A + A)
            turn = jnp.dot(pick, parts[:, lanes], preferred_element_type=jnp.float32)
            spectra = jnp.dot(block[:, lanes], dft, preferred_element_type=jnp.float32)
            cosine = turn[:, :FREQS] * cos_rot - turn[:, FREQS:] * sin_rot
            sine = turn[:, FREQS:] * cos_rot + turn[:, :FREQS] * sin_rot
            real, imag = spectra[:, :FREQS], spectra[:, FREQS:]
            out[rows, i * A : i * A + FREQS] = (real * cosine - imag * sine).astype(jnp.bfloat16)
            out[rows, i * A + FREQS : i * A + A] = (real * sine + imag * cosine).astype(jnp.bfloat16)
        out[rows, WIDE:] = block[:, WIDE:]


def score_kernel(y_ref, rows, panel, out, stats):
    y = y_ref[0]
    refs = panel[:, :WIDE]
    wide = refs.astype(jnp.float32)
    norm = jnp.sum(wide * wide, axis=1, keepdims=True)
    sharp = panel[:, WIDE:].astype(jnp.float32)
    diagonal = iota((P_DEV, P_DEV), 0) == iota((P_DEV, P_DEV), 1)
    for d in range(NY):
        source = (y - d) & (NY - 1)
        flat = rows[d * P_DEV : d * P_DEV + P_DEV, :WIDE]
        label = rows[d * P_DEV : d * P_DEV + 16, WIDE:].astype(jnp.float32)[0:1].astype(jnp.int32)
        member = iota((C, P_DEV), 0) == label
        scores = lax.dot_general(
            refs, flat, (((1,), (1,)), ((), ())), preferred_element_type=jnp.float32
        )
        gram = lax.dot_general(
            flat, flat, (((1,), (1,)), ((), ())), preferred_element_type=jnp.float32
        )
        inner = jnp.sum(jnp.where(member, scores, 0.0), axis=0, keepdims=True)
        power = jnp.sum(jnp.where(diagonal, gram, 0.0), axis=0, keepdims=True)
        ref_power = jnp.sum(jnp.where(member, norm, 0.0), axis=0, keepdims=True)
        own_sharp = jnp.sum(jnp.where(member, sharp, 0.0), axis=0, keepdims=True)
        for at, value in enumerate((own_sharp * inner, power, ref_power)):
            stats[pl.ds(at * NY + source, 1), :] = value
    value = stats[...]
    for i in range(NX * NY * 2):
        out[i] = value


def sum_kernel(at_ref, got, own, other, out, weights):
    y, core = at_ref[0], at_ref[1]
    for c in range(2):
        total = got[c]
        for i in range(1, NX * NY):
            total = total + got[2 * i + c]
        inner, power, ref_power = total[0:NY], total[NY : 2 * NY], total[2 * NY : 3 * NY]
        weight = jax.nn.sigmoid(inner / jnp.sqrt((power + EPSILON) * (ref_power + EPSILON)))
        weights[c * NY : c * NY + NY, :] = weight.astype(jnp.bfloat16).astype(jnp.float32)
    spread = []
    for rows, side in ((own, core), (other, 1 - core)):
        parts = []
        for d in range(NY):
            source = (y - d) & (NY - 1)
            first = d * P_DEV
            label = rows[first : first + 16, WIDE:].astype(jnp.float32)[0:1].astype(jnp.int32)
            member = iota((P_DEV, P_DEV), 0) == (label ^ (core * 128))
            weight = weights[pl.ds(side * NY + source, 1), :]
            parts.append(jnp.where(member, weight, 0.0).astype(jnp.bfloat16))
        spread.append(jnp.concatenate(parts, axis=1))
    for i in range(R_OWN):
        lanes = slice(i * A, i * A + A)
        sums = jnp.dot(spread[0], own[:, lanes], preferred_element_type=jnp.float32)
        sums = sums + jnp.dot(spread[1], other[:, lanes], preferred_element_type=jnp.float32)
        out[:, lanes] = sums.astype(jnp.bfloat16)
    ones = jnp.ones((NY * P_DEV, P_DEV), jnp.bfloat16)
    sums = jnp.dot(spread[0], ones, preferred_element_type=jnp.float32)
    sums = sums + jnp.dot(spread[1], ones, preferred_element_type=jnp.float32)
    high = sums.astype(jnp.bfloat16).astype(jnp.float32)
    sums = jnp.where(iota((P_DEV, P_DEV), 1) < 64, high, sums - high)
    out[:, WIDE:] = sums.astype(jnp.bfloat16)


def finish_kernel(got, out, out_weights):
    odd = (iota((2 * NZ, FULL), 0) & 1) == 1
    for r in range(NY):
        part = got[r * 2 * NZ : (r + 1) * 2 * NZ, :].astype(jnp.float32)
        for j in range(2):
            total = jnp.sum(jnp.where(odd == (j == 1), part, 0.0), axis=0, keepdims=True)
            for i in range(R_OWN):
                out[j, r * R_OWN + i : r * R_OWN + i + 1, :] = total[:, i * A : i * A + A]
            if r == 0:
                out_weights[j] = jnp.sum(total[:, WIDE:]) * (1.0 / 64.0)


VMEM = pl.BlockSpec(memory_space=pltpu.VMEM)
SMEM = pl.BlockSpec(memory_space=pltpu.SMEM)
HBM = pl.BlockSpec(memory_space=pltpu.HBM)


def call(kernel, name, outs, scratch, flops, nbytes, in_specs, out_specs):
    return pl.pallas_call(
        kernel,
        out_shape=outs,
        in_specs=in_specs,
        out_specs=out_specs,
        scratch_shapes=scratch,
        compiler_params=pltpu.CompilerParams(vmem_limit_bytes=VMEM_LIMIT),
        cost_estimate=pl.CostEstimate(flops=flops, bytes_accessed=nbytes, transcendentals=0),
        name=name,
    )


def body(images, references, sharpness, classes, rotations, shifts, shift_phase):
    y = lax.axis_index("y").astype(jnp.int32)
    core = lax.axis_index("core").astype(jnp.int32)
    shape = jax.ShapeDtypeStruct

    block = shape((P_DEV, FULL), jnp.bfloat16)
    pieces, *dealt = call(
        deal_kernel,
        "deal",
        [block] * (1 + NY),
        [
            pltpu.VMEM((P_DEV * R_DEV, A), jnp.bfloat16),
            pltpu.VMEM((2, R_DEV, A), jnp.bfloat16),
            pltpu.VMEM((8, P_DEV), jnp.int32),
            pltpu.VMEM((2 * NY, FULL), jnp.float32),
            pltpu.VMEM((R_DEV, P_DEV, A), jnp.bfloat16),
            pltpu.SemaphoreType.DMA((8,)),
        ],
        300_000_000,
        3_000_000,
        [SMEM] + [HBM] * 5 + [VMEM],
        [VMEM] * (1 + NY),
    )(
        y[None],
        *[
            pltpu.with_memory_space_constraint(x, pltpu.HBM)
            for x in (
                images.reshape(P_DEV * R_DEV, A),
                references,
                classes.reshape(1, P_DEV),
                rotations.reshape(1, P_DEV),
                shifts.reshape(1, P_DEV),
            )
        ],
        sharpness.astype(jnp.float32).reshape(1, 2),
    )
    panel = lax.all_to_all(
        pieces.reshape(NY * NZ, 2, FULL), ("y", "z"), split_axis=0, concat_axis=0, tiled=True
    )
    blocks = [dealt[0]]
    for d in range(1, NY):
        blocks.append(lax.ppermute(dealt[d], "y", [(i, (i + d) % NY) for i in range(NY)]))
    phases = lax.dynamic_slice_in_dim(shift_phase, y * R_OWN, R_OWN, 1).transpose(1, 0, 2)
    phases = jnp.pad(phases, ((0, 0), (0, SHIFT_ROWS - 25), (0, 0)))
    rows = call(
        align_kernel,
        "align",
        shape((NY * P_DEV, FULL), jnp.bfloat16),
        [pltpu.VMEM((2 * SHIFT_ROWS, WIDE), jnp.bfloat16)],
        800_000_000,
        4_000_000,
        [VMEM] * 6,
        VMEM,
    )(*blocks, spectral_table(A), phases)

    panel = lax.all_gather(panel.reshape(NY * NZ * 2, FULL), "core", axis=0, tiled=True)
    payload = call(
        score_kernel,
        "score",
        shape((NX * NY * 2, 3 * NY, P_DEV), jnp.float32),
        [pltpu.VMEM((3 * NY, P_DEV), jnp.float32)],
        600_000_000,
        2_000_000,
        [SMEM] + [VMEM] * 2,
        VMEM,
    )(y[None], rows, panel)
    rows, payload = lax.optimization_barrier((rows, payload))
    got = lax.all_to_all(payload, ("x", "y", "core"), split_axis=0, concat_axis=0, tiled=True)
    other = lax.ppermute(rows, "core", [(0, 1), (1, 0)])
    sums = call(
        sum_kernel,
        "sum",
        shape((P_DEV, FULL), jnp.bfloat16),
        [pltpu.VMEM((2 * NY, P_DEV), jnp.float32)],
        300_000_000,
        3_000_000,
        [SMEM] + [VMEM] * 3,
        VMEM,
    )(jnp.stack([y, core]), got, rows, other)
    sums = lax.all_to_all(
        sums.reshape(NY * NZ, 2, FULL), ("y", "z"), split_axis=0, concat_axis=0, tiled=True
    )
    class_sums, class_weights = call(
        finish_kernel,
        "finish",
        [shape((2, R_DEV, A), jnp.float32), shape((2,), jnp.float32)],
        [],
        1_000_000,
        400_000,
        [VMEM],
        [VMEM, SMEM],
    )(sums.reshape(NY * NZ * 2, FULL))
    return class_sums, class_weights


def solution(mesh):
    whole = Mesh(mesh.devices.reshape(NY, NZ, 2, NX), ("y", "z", "core", "x"))
    dom = ("y", "z", "core")
    return jax.shard_map(
        body,
        mesh=whole,
        in_specs=(
            P(dom, "x", None),
            P(dom, "x", None),
            P(dom),
            P(dom, None),
            P(dom),
            P(dom),
            P(None, "x", None),
        ),
        out_specs=(P(dom, "x", None), P(dom)),
        check_vma=False,
    )
```

```python
import math

import jax
import jax.numpy as jnp
from jax import lax
from jax.experimental import pallas as pl
from jax.experimental.pallas import tpu as pltpu
from jax.sharding import Mesh
from jax.sharding import PartitionSpec as P

C = 256
EPSILON = 1e-06
NY, NZ, NX = 4, 16, 4
P_DEV = 128
R_DEV = 16
A = 256
FREQS = 128
R_OWN = R_DEV // NY
WIDE = R_OWN * A
FULL = WIDE + 128
SHIFT_ROWS = 32
VMEM_LIMIT = 40 * 1024 * 1024


def spectral_table(length):
    half_len = length // 2
    angle_index = jnp.arange(length, dtype=jnp.int32)
    freq_index = jnp.arange(half_len, dtype=jnp.int32)
    turn_count = angle_index[:, None] * freq_index[None, :] % length
    radians = turn_count.astype(jnp.float32) * (2.0 * math.pi / length)
    norm_scale = 1.0 / math.sqrt(length)
    both = jnp.concatenate([jnp.cos(radians), -jnp.sin(radians)], 1) * norm_scale
    return both.astype(jnp.bfloat16)


def iota(shape, axis):
    return lax.broadcasted_iota(jnp.int32, shape, axis)


def deal_kernel(
    y_ref,
    images_hbm,
    refs_hbm,
    label_hbm,
    rot_hbm,
    shift_hbm,
    sharp,
    pieces,
    out0,
    out1,
    out2,
    out3,
    images,
    refs,
    ints,
    row_of,
    grid,
    sems,
):
    y = y_ref[0]
    copies = [
        pltpu.make_async_copy(source, target, sems.at[at])
        for at, (source, target) in enumerate(
            (
                (refs_hbm, refs),
                (label_hbm, ints.at[pl.ds(0, 1)]),
                (rot_hbm, ints.at[pl.ds(1, 1)]),
                (shift_hbm, ints.at[pl.ds(2, 1)]),
            )
        )
    ]
    quarter = P_DEV * R_DEV // 4
    for i in range(4):
        rows = pl.ds(i * quarter, quarter)
        copies.append(pltpu.make_async_copy(images_hbm.at[rows], images.at[rows], sems.at[4 + i]))
    for copy in copies:
        copy.start()
    for copy in copies[:4]:
        copy.wait()
    for j in range(2):
        wide = refs[j].astype(jnp.float32)
        for r in range(R_DEV):
            at = r // R_OWN * 2 + j
            lanes = slice(r % R_OWN * A, r % R_OWN * A + A)
            row_of[at : at + 1, lanes] = wide[r : r + 1]
            row_of[at + 8 : at + 9, lanes] = wide[r : r + 1]
        tile = jnp.broadcast_to(sharp[0:1, j : j + 1], (1, 128))
        for at in range(j, 4 * NY, 2):
            row_of[at : at + 1, WIDE:] = tile
    pair = row_of[...].astype(jnp.bfloat16)
    for z in range(0, NZ, 2):
        pieces[z * 8 : z * 8 + 16, :] = pair
    row, col = iota((A, A), 0), iota((A, A), 1)
    swap = (col == ((row & 15) * 16 + (row >> 4))).astype(jnp.float32).astype(jnp.bfloat16)
    for b in range(P_DEV // 16):
        if b % 2 == 0:
            copies[4 + b // 2].wait()
        x = jnp.dot(swap, images[b * A : b * A + A, :], preferred_element_type=jnp.float32)
        x = x.astype(jnp.bfloat16)
        for r in range(R_DEV):
            grid[r, b * 16 : b * 16 + 16, :] = x[r * 16 : r * 16 + 16]
    label = ints[0:1, :]
    label = ((label >> 1) & 1) * 128 + (label >> 2) * 2 + (label & 1)
    at = iota((P_DEV, P_DEV), 0)
    tail = jnp.where(at == 0, label, jnp.where(at == 1, ints[1:2, :], ints[2:3, :]))
    tail = tail.astype(jnp.float32).astype(jnp.bfloat16)
    for d, out in enumerate((out0, out1, out2, out3)):
        first = ((y + d) & (NY - 1)) * R_OWN
        for i in range(R_OWN):
            out[:, i * A : i * A + A] = grid[first + i]
        out[:, WIDE:] = tail


def align_kernel(in0, in1, in2, in3, table, phases, out, parts):
    for r in range(R_OWN):
        phase = phases[r]
        for at, value in ((0, jnp.cos(phase)), (FREQS, jnp.sin(phase))):
            high = value.astype(jnp.bfloat16)
            low = (value - high.astype(jnp.float32)).astype(jnp.bfloat16)
            lanes = slice(r * A + at, r * A + at + FREQS)
            parts[0:SHIFT_ROWS, lanes] = high
            parts[SHIFT_ROWS : 2 * SHIFT_ROWS, lanes] = low
    dft = table[...]
    diagonal = iota((P_DEV, P_DEV), 0) == iota((P_DEV, P_DEV), 1)
    lane = iota((P_DEV, P_DEV), 1)
    for d, block in enumerate((in0, in1, in2, in3)):
        rows = slice(d * P_DEV, d * P_DEV + P_DEV)
        tail = block[0:16, WIDE:].astype(jnp.float32)
        rot = jnp.sum(jnp.where(diagonal, tail[1:2], 0.0), axis=1, keepdims=True)
        shift = jnp.sum(jnp.where(diagonal, tail[2:3], 0.0), axis=1, keepdims=True)
        angle = ((rot.astype(jnp.int32) * lane) & (A - 1)).astype(jnp.float32) * (2.0 * math.pi / A)
        cos_rot, sin_rot = jnp.cos(angle), jnp.sin(angle)
        pick = (lane[:, : 2 * SHIFT_ROWS] & (SHIFT_ROWS - 1)) == shift.astype(jnp.int32)
        pick = pick.astype(jnp.float32).astype(jnp.bfloat16)
        for i in range(R_OWN):
            lanes = slice(i * A, i * A + A)
            turn = jnp.dot(pick, parts[:, lanes], preferred_element_type=jnp.float32)
            spectra = jnp.dot(block[:, lanes], dft, preferred_element_type=jnp.float32)
            cosine = turn[:, :FREQS] * cos_rot - turn[:, FREQS:] * sin_rot
            sine = turn[:, FREQS:] * cos_rot + turn[:, :FREQS] * sin_rot
            real, imag = spectra[:, :FREQS], spectra[:, FREQS:]
            out[rows, i * A : i * A + FREQS] = (real * cosine - imag * sine).astype(jnp.bfloat16)
            out[rows, i * A + FREQS : i * A + A] = (real * sine + imag * cosine).astype(jnp.bfloat16)
        out[rows, WIDE:] = block[:, WIDE:]


def score_kernel(y_ref, rows, panel, out, stats):
    y = y_ref[0]
    refs = panel[:, :WIDE]
    wide = refs.astype(jnp.float32)
    norm = jnp.sum(wide * wide, axis=1, keepdims=True)
    sharp = panel[:, WIDE:].astype(jnp.float32)
    diagonal = iota((P_DEV, P_DEV), 0) == iota((P_DEV, P_DEV), 1)
    for d in range(NY):
        source = (y - d) & (NY - 1)
        flat = rows[d * P_DEV : d * P_DEV + P_DEV, :WIDE]
        label = rows[d * P_DEV : d * P_DEV + 16, WIDE:].astype(jnp.float32)[0:1].astype(jnp.int32)
        member = iota((C, P_DEV), 0) == label
        scores = lax.dot_general(
            refs, flat, (((1,), (1,)), ((), ())), preferred_element_type=jnp.float32
        )
        gram = lax.dot_general(
            flat, flat, (((1,), (1,)), ((), ())), preferred_element_type=jnp.float32
        )
        inner = jnp.sum(jnp.where(member, scores, 0.0), axis=0, keepdims=True)
        power = jnp.sum(jnp.where(diagonal, gram, 0.0), axis=0, keepdims=True)
        ref_power = jnp.sum(jnp.where(member, norm, 0.0), axis=0, keepdims=True)
        own_sharp = jnp.sum(jnp.where(member, sharp, 0.0), axis=0, keepdims=True)
        for at, value in enumerate((own_sharp * inner, power, ref_power)):
            stats[pl.ds(at * NY + source, 1), :] = value
    value = stats[...]
    for i in range(NX * NY * 2):
        out[i] = value


def sum_kernel(at_ref, got, own, other, out, weights):
    y, core = at_ref[0], at_ref[1]
    for c in range(2):
        total = got[c]
        for i in range(1, NX * NY):
            total = total + got[2 * i + c]
        inner, power, ref_power = total[0:NY], total[NY : 2 * NY], total[2 * NY : 3 * NY]
        weight = jax.nn.sigmoid(inner / jnp.sqrt((power + EPSILON) * (ref_power + EPSILON)))
        weights[c * NY : c * NY + NY, :] = weight.astype(jnp.bfloat16).astype(jnp.float32)
    spread = []
    for rows, side in ((own, core), (other, 1 - core)):
        parts = []
        for d in range(NY):
            source = (y - d) & (NY - 1)
            first = d * P_DEV
            label = rows[first : first + 16, WIDE:].astype(jnp.float32)[0:1].astype(jnp.int32)
            member = iota((P_DEV, P_DEV), 0) == (label ^ (core * 128))
            weight = weights[pl.ds(side * NY + source, 1), :]
            parts.append(jnp.where(member, weight, 0.0).astype(jnp.bfloat16))
        spread.append(jnp.concatenate(parts, axis=1))
    for i in range(R_OWN):
        lanes = slice(i * A, i * A + A)
        sums = jnp.dot(spread[0], own[:, lanes], preferred_element_type=jnp.float32)
        sums = sums + jnp.dot(spread[1], other[:, lanes], preferred_element_type=jnp.float32)
        out[:, lanes] = sums.astype(jnp.bfloat16)
    ones = jnp.ones((NY * P_DEV, P_DEV), jnp.bfloat16)
    sums = jnp.dot(spread[0], ones, preferred_element_type=jnp.float32)
    sums = sums + jnp.dot(spread[1], ones, preferred_element_type=jnp.float32)
    high = sums.astype(jnp.bfloat16).astype(jnp.float32)
    sums = jnp.where(iota((P_DEV, P_DEV), 1) < 64, high, sums - high)
    out[:, WIDE:] = sums.astype(jnp.bfloat16)


def finish_kernel(got, out, out_weights):
    odd = (iota((2 * NZ, FULL), 0) & 1) == 1
    for r in range(NY):
        part = got[r * 2 * NZ : (r + 1) * 2 * NZ, :].astype(jnp.float32)
        for j in range(2):
            total = jnp.sum(jnp.where(odd == (j == 1), part, 0.0), axis=0, keepdims=True)
            for i in range(R_OWN):
                out[j, r * R_OWN + i : r * R_OWN + i + 1, :] = total[:, i * A : i * A + A]
            if r == 0:
                out_weights[j] = jnp.sum(total[:, WIDE:]) * (1.0 / 64.0)


VMEM = pl.BlockSpec(memory_space=pltpu.VMEM)
SMEM = pl.BlockSpec(memory_space=pltpu.SMEM)
HBM = pl.BlockSpec(memory_space=pltpu.HBM)
ANY = pl.BlockSpec(memory_space=pl.ANY)


def call(kernel, name, outs, scratch, flops, nbytes, in_specs, out_specs):
    return pl.pallas_call(
        kernel,
        out_shape=outs,
        in_specs=in_specs,
        out_specs=out_specs,
        scratch_shapes=scratch,
        compiler_params=pltpu.CompilerParams(vmem_limit_bytes=VMEM_LIMIT),
        cost_estimate=pl.CostEstimate(flops=flops, bytes_accessed=nbytes, transcendentals=0),
        name=name,
    )


def body(images, references, sharpness, classes, rotations, shifts, shift_phase):
    y = lax.axis_index("y").astype(jnp.int32)
    core = lax.axis_index("core").astype(jnp.int32)
    shape = jax.ShapeDtypeStruct

    block = shape((P_DEV, FULL), jnp.bfloat16)
    pieces, *dealt = call(
        deal_kernel,
        "deal",
        [block] * (1 + NY),
        [
            pltpu.VMEM((P_DEV * R_DEV, A), jnp.bfloat16),
            pltpu.VMEM((2, R_DEV, A), jnp.bfloat16),
            pltpu.VMEM((8, P_DEV), jnp.int32),
            pltpu.VMEM((4 * NY, FULL), jnp.float32),
            pltpu.VMEM((R_DEV, P_DEV, A), jnp.bfloat16),
            pltpu.SemaphoreType.DMA((8,)),
        ],
        300_000_000,
        3_000_000,
        [SMEM] + [HBM] * 5 + [VMEM],
        [VMEM] * (1 + NY),
    )(
        y[None],
        *[
            pltpu.with_memory_space_constraint(x, pltpu.HBM)
            for x in (
                images.reshape(P_DEV * R_DEV, A),
                references,
                classes.reshape(1, P_DEV),
                rotations.reshape(1, P_DEV),
                shifts.reshape(1, P_DEV),
            )
        ],
        sharpness.astype(jnp.float32).reshape(1, 2),
    )
    panel = lax.all_to_all(
        pieces.reshape(NZ, 2 * NY, FULL), "z", split_axis=0, concat_axis=0, tiled=True
    )
    panel = panel.reshape(NZ, NY, 2, FULL).transpose(1, 0, 2, 3).reshape(NY, 2 * NZ, FULL)
    panel = lax.all_to_all(panel, "y", split_axis=0, concat_axis=0, tiled=True)
    blocks = [dealt[0]]
    for d in range(1, NY):
        blocks.append(lax.ppermute(dealt[d], "y", [(i, (i + d) % NY) for i in range(NY)]))
    phases = lax.dynamic_slice_in_dim(shift_phase, y * R_OWN, R_OWN, 1).transpose(1, 0, 2)
    phases = jnp.pad(phases, ((0, 0), (0, SHIFT_ROWS - 25), (0, 0)))
    rows = call(
        align_kernel,
        "align",
        shape((NY * P_DEV, FULL), jnp.bfloat16),
        [pltpu.VMEM((2 * SHIFT_ROWS, WIDE), jnp.bfloat16)],
        800_000_000,
        4_000_000,
        [VMEM] * 6,
        VMEM,
    )(*blocks, spectral_table(A), phases)

    panel = lax.all_gather(panel.reshape(NY * NZ * 2, FULL), "core", axis=0, tiled=True)
    payload = call(
        score_kernel,
        "score",
        shape((NX * NY * 2, 3 * NY, P_DEV), jnp.float32),
        [pltpu.VMEM((3 * NY, P_DEV), jnp.float32)],
        600_000_000,
        2_000_000,
        [SMEM] + [VMEM] * 2,
        VMEM,
    )(y[None], rows, panel)
    rows = pl.pallas_call(
        lambda rows, payload, out: None,
        out_shape=shape(rows.shape, rows.dtype),
        in_specs=[ANY, ANY],
        out_specs=ANY,
        input_output_aliases={0: 0},
        cost_estimate=pl.CostEstimate(
            flops=20_000_000_000, bytes_accessed=2_000_000, transcendentals=0
        ),
        name="hold",
    )(rows, payload)
    got = lax.all_to_all(payload, ("x", "y", "core"), split_axis=0, concat_axis=0, tiled=True)
    other = lax.ppermute(rows, "core", [(0, 1), (1, 0)])
    sums = call(
        sum_kernel,
        "sum",
        shape((P_DEV, FULL), jnp.bfloat16),
        [pltpu.VMEM((2 * NY, P_DEV), jnp.float32)],
        300_000_000,
        3_000_000,
        [SMEM] + [VMEM] * 3,
        VMEM,
    )(jnp.stack([y, core]), got, rows, other)
    sums = lax.all_to_all(
        sums.reshape(NY * NZ, 2, FULL), ("y", "z"), split_axis=0, concat_axis=0, tiled=True
    )
    class_sums, class_weights = call(
        finish_kernel,
        "finish",
        [shape((2, R_DEV, A), jnp.float32), shape((2,), jnp.float32)],
        [],
        1_000_000,
        400_000,
        [VMEM],
        [VMEM, SMEM],
    )(sums.reshape(NY * NZ * 2, FULL))
    return class_sums, class_weights


def solution(mesh):
    whole = Mesh(mesh.devices.reshape(NY, NZ, 2, NX), ("y", "z", "core", "x"))
    dom = ("y", "z", "core")
    return jax.shard_map(
        body,
        mesh=whole,
        in_specs=(
            P(dom, "x", None),
            P(dom, "x", None),
            P(dom),
            P(dom, None),
            P(dom),
            P(dom),
            P(None, "x", None),
        ),
        out_specs=(P(dom, "x", None), P(dom)),
        check_vma=False,
    )
```

```python
import math

import jax
import jax.numpy as jnp
from jax import lax
from jax.experimental import pallas as pl
from jax.experimental.pallas import tpu as pltpu
from jax.sharding import Mesh
from jax.sharding import PartitionSpec as P

C = 256
EPSILON = 1e-06
NY, NZ, NX = 4, 16, 4
P_DEV = 128
R_DEV = 16
A = 256
FREQS = 128
R_OWN = R_DEV // NY
WIDE = R_OWN * A
FULL = WIDE + 128
SHIFT_ROWS = 32
VMEM_LIMIT = 40 * 1024 * 1024


def spectral_table(length):
    half_len = length // 2
    angle_index = jnp.arange(length, dtype=jnp.int32)
    freq_index = jnp.arange(half_len, dtype=jnp.int32)
    turn_count = angle_index[:, None] * freq_index[None, :] % length
    radians = turn_count.astype(jnp.float32) * (2.0 * math.pi / length)
    norm_scale = 1.0 / math.sqrt(length)
    both = jnp.concatenate([jnp.cos(radians), -jnp.sin(radians)], 1) * norm_scale
    return both.astype(jnp.bfloat16)


def iota(shape, axis):
    return lax.broadcasted_iota(jnp.int32, shape, axis)


def deal_kernel(
    y_ref,
    images_hbm,
    refs_hbm,
    label_hbm,
    rot_hbm,
    shift_hbm,
    sharp,
    pieces,
    out0,
    out1,
    out2,
    out3,
    images,
    refs,
    ints,
    row_of,
    grid,
    sems,
):
    y = y_ref[0]
    copies = [
        pltpu.make_async_copy(source, target, sems.at[at])
        for at, (source, target) in enumerate(
            (
                (refs_hbm, refs),
                (label_hbm, ints.at[pl.ds(0, 1)]),
                (rot_hbm, ints.at[pl.ds(1, 1)]),
                (shift_hbm, ints.at[pl.ds(2, 1)]),
            )
        )
    ]
    quarter = P_DEV * R_DEV // 4
    for i in range(4):
        rows = pl.ds(i * quarter, quarter)
        copies.append(pltpu.make_async_copy(images_hbm.at[rows], images.at[rows], sems.at[4 + i]))
    for copy in copies:
        copy.start()
    for copy in copies[:4]:
        copy.wait()
    odd = (iota((2 * NZ, FULL), 0) & 1) == 1
    for j in range(2):
        wide = refs[j].astype(jnp.float32)
        for r in range(R_DEV):
            at = r // R_OWN * 2 + j
            lanes = slice(r % R_OWN * A, r % R_OWN * A + A)
            row_of[at : at + 1, lanes] = wide[r : r + 1]
        tile = jnp.broadcast_to(sharp[0:1, j : j + 1], (1, 128))
        for r in range(NY):
            row_of[2 * r + j : 2 * r + j + 1, WIDE:] = tile
    for r in range(NY):
        pair = jnp.where(odd, row_of[2 * r + 1 : 2 * r + 2, :], row_of[2 * r : 2 * r + 1, :])
        pieces[r * 2 * NZ : (r + 1) * 2 * NZ, :] = pair.astype(jnp.bfloat16)
    row, col = iota((A, A), 0), iota((A, A), 1)
    swap = (col == ((row & 15) * 16 + (row >> 4))).astype(jnp.float32).astype(jnp.bfloat16)
    for b in range(P_DEV // 16):
        if b % 2 == 0:
            copies[4 + b // 2].wait()
        x = jnp.dot(swap, images[b * A : b * A + A, :], preferred_element_type=jnp.float32)
        x = x.astype(jnp.bfloat16)
        for r in range(R_DEV):
            grid[r, b * 16 : b * 16 + 16, :] = x[r * 16 : r * 16 + 16]
    label = ints[0:1, :]
    label = ((label >> 1) & 1) * 128 + (label >> 2) * 2 + (label & 1)
    at = iota((P_DEV, P_DEV), 0)
    tail = jnp.where(at == 0, label, jnp.where(at == 1, ints[1:2, :], ints[2:3, :]))
    tail = tail.astype(jnp.float32).astype(jnp.bfloat16)
    for d, out in enumerate((out0, out1, out2, out3)):
        first = ((y + d) & (NY - 1)) * R_OWN
        for i in range(R_OWN):
            out[:, i * A : i * A + A] = grid[first + i]
        out[:, WIDE:] = tail


def align_kernel(in0, in1, in2, in3, table, phases, out, parts):
    for r in range(R_OWN):
        phase = phases[r]
        for at, value in ((0, jnp.cos(phase)), (FREQS, jnp.sin(phase))):
            high = value.astype(jnp.bfloat16)
            low = (value - high.astype(jnp.float32)).astype(jnp.bfloat16)
            lanes = slice(r * A + at, r * A + at + FREQS)
            parts[0:SHIFT_ROWS, lanes] = high
            parts[SHIFT_ROWS : 2 * SHIFT_ROWS, lanes] = low
    dft = table[...]
    diagonal = iota((P_DEV, P_DEV), 0) == iota((P_DEV, P_DEV), 1)
    lane = iota((P_DEV, P_DEV), 1)
    for d, block in enumerate((in0, in1, in2, in3)):
        rows = slice(d * P_DEV, d * P_DEV + P_DEV)
        tail = block[0:16, WIDE:].astype(jnp.float32)
        rot = jnp.sum(jnp.where(diagonal, tail[1:2], 0.0), axis=1, keepdims=True)
        shift = jnp.sum(jnp.where(diagonal, tail[2:3], 0.0), axis=1, keepdims=True)
        angle = ((rot.astype(jnp.int32) * lane) & (A - 1)).astype(jnp.float32) * (2.0 * math.pi / A)
        cos_rot, sin_rot = jnp.cos(angle), jnp.sin(angle)
        pick = (lane[:, : 2 * SHIFT_ROWS] & (SHIFT_ROWS - 1)) == shift.astype(jnp.int32)
        pick = pick.astype(jnp.float32).astype(jnp.bfloat16)
        for i in range(R_OWN):
            lanes = slice(i * A, i * A + A)
            turn = jnp.dot(pick, parts[:, lanes], preferred_element_type=jnp.float32)
            spectra = jnp.dot(block[:, lanes], dft, preferred_element_type=jnp.float32)
            cosine = turn[:, :FREQS] * cos_rot - turn[:, FREQS:] * sin_rot
            sine = turn[:, FREQS:] * cos_rot + turn[:, :FREQS] * sin_rot
            real, imag = spectra[:, :FREQS], spectra[:, FREQS:]
            out[rows, i * A : i * A + FREQS] = (real * cosine - imag * sine).astype(jnp.bfloat16)
            out[rows, i * A + FREQS : i * A + A] = (real * sine + imag * cosine).astype(jnp.bfloat16)
        out[rows, WIDE:] = block[:, WIDE:]


def score_kernel(y_ref, rows, panel, out, stats):
    y = y_ref[0]
    refs = panel[:, :WIDE]
    wide = refs.astype(jnp.float32)
    norm = jnp.sum(wide * wide, axis=1, keepdims=True)
    sharp = panel[:, WIDE:].astype(jnp.float32)
    diagonal = iota((P_DEV, P_DEV), 0) == iota((P_DEV, P_DEV), 1)
    for d in range(NY):
        source = (y - d) & (NY - 1)
        flat = rows[d * P_DEV : d * P_DEV + P_DEV, :WIDE]
        label = rows[d * P_DEV : d * P_DEV + 16, WIDE:].astype(jnp.float32)[0:1].astype(jnp.int32)
        member = iota((C, P_DEV), 0) == label
        scores = lax.dot_general(
            refs, flat, (((1,), (1,)), ((), ())), preferred_element_type=jnp.float32
        )
        gram = lax.dot_general(
            flat, flat, (((1,), (1,)), ((), ())), preferred_element_type=jnp.float32
        )
        inner = jnp.sum(jnp.where(member, scores, 0.0), axis=0, keepdims=True)
        power = jnp.sum(jnp.where(diagonal, gram, 0.0), axis=0, keepdims=True)
        ref_power = jnp.sum(jnp.where(member, norm, 0.0), axis=0, keepdims=True)
        own_sharp = jnp.sum(jnp.where(member, sharp, 0.0), axis=0, keepdims=True)
        for at, value in enumerate((own_sharp * inner, power, ref_power)):
            stats[pl.ds(at * NY + source, 1), :] = value
    value = stats[...]
    for i in range(NX * NY * 2):
        out[i] = value


def sum_kernel(at_ref, got, own, other, out, weights):
    y, core = at_ref[0], at_ref[1]
    for c in range(2):
        total = got[c]
        for i in range(1, NX * NY):
            total = total + got[2 * i + c]
        inner, power, ref_power = total[0:NY], total[NY : 2 * NY], total[2 * NY : 3 * NY]
        weight = jax.nn.sigmoid(inner / jnp.sqrt((power + EPSILON) * (ref_power + EPSILON)))
        weights[c * NY : c * NY + NY, :] = weight.astype(jnp.bfloat16).astype(jnp.float32)
    spread = []
    for rows, side in ((own, core), (other, 1 - core)):
        parts = []
        for d in range(NY):
            source = (y - d) & (NY - 1)
            first = d * P_DEV
            label = rows[first : first + 16, WIDE:].astype(jnp.float32)[0:1].astype(jnp.int32)
            member = iota((P_DEV, P_DEV), 0) == (label ^ (core * 128))
            weight = weights[pl.ds(side * NY + source, 1), :]
            parts.append(jnp.where(member, weight, 0.0).astype(jnp.bfloat16))
        spread.append(jnp.concatenate(parts, axis=1))
    for i in range(R_OWN):
        lanes = slice(i * A, i * A + A)
        sums = jnp.dot(spread[0], own[:, lanes], preferred_element_type=jnp.float32)
        sums = sums + jnp.dot(spread[1], other[:, lanes], preferred_element_type=jnp.float32)
        out[:, lanes] = sums.astype(jnp.bfloat16)
    ones = jnp.ones((NY * P_DEV, P_DEV), jnp.bfloat16)
    sums = jnp.dot(spread[0], ones, preferred_element_type=jnp.float32)
    sums = sums + jnp.dot(spread[1], ones, preferred_element_type=jnp.float32)
    high = sums.astype(jnp.bfloat16).astype(jnp.float32)
    sums = jnp.where(iota((P_DEV, P_DEV), 1) < 64, high, sums - high)
    out[:, WIDE:] = sums.astype(jnp.bfloat16)


def finish_kernel(got, out, out_weights):
    odd = (iota((2 * NZ, FULL), 0) & 1) == 1
    for r in range(NY):
        part = got[r * 2 * NZ : (r + 1) * 2 * NZ, :].astype(jnp.float32)
        for j in range(2):
            total = jnp.sum(jnp.where(odd == (j == 1), part, 0.0), axis=0, keepdims=True)
            for i in range(R_OWN):
                out[j, r * R_OWN + i : r * R_OWN + i + 1, :] = total[:, i * A : i * A + A]
            if r == 0:
                out_weights[j] = jnp.sum(total[:, WIDE:]) * (1.0 / 64.0)


VMEM = pl.BlockSpec(memory_space=pltpu.VMEM)
SMEM = pl.BlockSpec(memory_space=pltpu.SMEM)
HBM = pl.BlockSpec(memory_space=pltpu.HBM)


def call(kernel, name, outs, scratch, flops, nbytes, in_specs, out_specs):
    return pl.pallas_call(
        kernel,
        out_shape=outs,
        in_specs=in_specs,
        out_specs=out_specs,
        scratch_shapes=scratch,
        compiler_params=pltpu.CompilerParams(vmem_limit_bytes=VMEM_LIMIT),
        cost_estimate=pl.CostEstimate(flops=flops, bytes_accessed=nbytes, transcendentals=0),
        name=name,
    )


def body(images, references, sharpness, classes, rotations, shifts, shift_phase):
    y = lax.axis_index("y").astype(jnp.int32)
    core = lax.axis_index("core").astype(jnp.int32)
    shape = jax.ShapeDtypeStruct

    block = shape((P_DEV, FULL), jnp.bfloat16)
    pieces, *dealt = call(
        deal_kernel,
        "deal",
        [block] * (1 + NY),
        [
            pltpu.VMEM((P_DEV * R_DEV, A), jnp.bfloat16),
            pltpu.VMEM((2, R_DEV, A), jnp.bfloat16),
            pltpu.VMEM((8, P_DEV), jnp.int32),
            pltpu.VMEM((2 * NY, FULL), jnp.float32),
            pltpu.VMEM((R_DEV, P_DEV, A), jnp.bfloat16),
            pltpu.SemaphoreType.DMA((8,)),
        ],
        300_000_000,
        3_000_000,
        [SMEM] + [HBM] * 5 + [VMEM],
        [VMEM] * (1 + NY),
    )(
        y[None],
        *[
            pltpu.with_memory_space_constraint(x, pltpu.HBM)
            for x in (
                images.reshape(P_DEV * R_DEV, A),
                references,
                classes.reshape(1, P_DEV),
                rotations.reshape(1, P_DEV),
                shifts.reshape(1, P_DEV),
            )
        ],
        sharpness.astype(jnp.float32).reshape(1, 2),
    )
    panel = lax.all_to_all(
        pieces.reshape(NY * NZ, 2, FULL), ("y", "z"), split_axis=0, concat_axis=0, tiled=True
    )
    blocks = [dealt[0]]
    for d in range(1, NY):
        blocks.append(lax.ppermute(dealt[d], "y", [(i, (i + d) % NY) for i in range(NY)]))
    phases = lax.dynamic_slice_in_dim(shift_phase, y * R_OWN, R_OWN, 1).transpose(1, 0, 2)
    phases = jnp.pad(phases, ((0, 0), (0, SHIFT_ROWS - 25), (0, 0)))
    rows = call(
        align_kernel,
        "align",
        shape((NY * P_DEV, FULL), jnp.bfloat16),
        [pltpu.VMEM((2 * SHIFT_ROWS, WIDE), jnp.bfloat16)],
        800_000_000,
        4_000_000,
        [VMEM] * 6,
        VMEM,
    )(*blocks, spectral_table(A), phases)

    panel = lax.all_gather(panel.reshape(NY * NZ * 2, FULL), "core", axis=0, tiled=True)
    payload = call(
        score_kernel,
        "score",
        shape((NX * NY * 2, 3 * NY, P_DEV), jnp.float32),
        [pltpu.VMEM((3 * NY, P_DEV), jnp.float32)],
        600_000_000,
        2_000_000,
        [SMEM] + [VMEM] * 2,
        VMEM,
    )(y[None], rows, panel)
    got = lax.all_to_all(payload, ("x", "y", "core"), split_axis=0, concat_axis=0, tiled=True)
    other = lax.ppermute(rows, "core", [(0, 1), (1, 0)])
    sums = call(
        sum_kernel,
        "sum",
        shape((P_DEV, FULL), jnp.bfloat16),
        [pltpu.VMEM((2 * NY, P_DEV), jnp.float32)],
        300_000_000,
        3_000_000,
        [SMEM] + [VMEM] * 3,
        VMEM,
    )(jnp.stack([y, core]), got, rows, other)
    sums = lax.all_to_all(
        sums.reshape(NY * NZ, 2, FULL), ("y", "z"), split_axis=0, concat_axis=0, tiled=True
    )
    class_sums, class_weights = call(
        finish_kernel,
        "finish",
        [shape((2, R_DEV, A), jnp.float32), shape((2,), jnp.float32)],
        [],
        1_000_000,
        400_000,
        [VMEM],
        [VMEM, SMEM],
    )(sums.reshape(NY * NZ * 2, FULL))
    return class_sums, class_weights


def solution(mesh):
    whole = Mesh(mesh.devices.reshape(NY, NZ, 2, NX), ("y", "z", "core", "x"))
    dom = ("y", "z", "core")
    return jax.shard_map(
        body,
        mesh=whole,
        in_specs=(
            P(dom, "x", None),
            P(dom, "x", None),
            P(dom),
            P(dom, None),
            P(dom),
            P(dom),
            P(None, "x", None),
        ),
        out_specs=(P(dom, "x", None), P(dom)),
        check_vma=False,
    )
```

```python
import math

import jax
import jax.numpy as jnp
from jax import lax
from jax.experimental import pallas as pl
from jax.experimental.pallas import tpu as pltpu
from jax.sharding import Mesh
from jax.sharding import PartitionSpec as P

C = 256
EPSILON = 1e-06
NY, NZ, NX = 4, 16, 4
P_DEV = 128
R_DEV = 16
A = 256
FREQS = 128
R_OWN = R_DEV // NY
WIDE = R_OWN * A
FULL = WIDE + 128
SHIFT_ROWS = 32
VMEM_LIMIT = 40 * 1024 * 1024


def spectral_table(length):
    half_len = length // 2
    angle_index = jnp.arange(length, dtype=jnp.int32)
    freq_index = jnp.arange(half_len, dtype=jnp.int32)
    turn_count = angle_index[:, None] * freq_index[None, :] % length
    radians = turn_count.astype(jnp.float32) * (2.0 * math.pi / length)
    norm_scale = 1.0 / math.sqrt(length)
    both = jnp.concatenate([jnp.cos(radians), -jnp.sin(radians)], 1) * norm_scale
    return both.astype(jnp.bfloat16)


def iota(shape, axis):
    return lax.broadcasted_iota(jnp.int32, shape, axis)


def deal_kernel(
    y_ref,
    images_hbm,
    refs_hbm,
    label_hbm,
    rot_hbm,
    shift_hbm,
    sharp_hbm,
    pieces,
    out0,
    out1,
    out2,
    out3,
    images,
    refs,
    ints,
    sharp,
    row_of,
    grid,
    sems,
):
    y = y_ref[0]
    copies = [
        pltpu.make_async_copy(source, target, sems.at[at])
        for at, (source, target) in enumerate(
            (
                (refs_hbm, refs),
                (label_hbm, ints.at[pl.ds(0, 1)]),
                (rot_hbm, ints.at[pl.ds(1, 1)]),
                (shift_hbm, ints.at[pl.ds(2, 1)]),
                (sharp_hbm, sharp),
            )
        )
    ]
    quarter = P_DEV * R_DEV // 4
    for i in range(4):
        rows = pl.ds(i * quarter, quarter)
        copies.append(pltpu.make_async_copy(images_hbm.at[rows], images.at[rows], sems.at[5 + i]))
    for copy in copies:
        copy.start()
    for copy in copies[:5]:
        copy.wait()
    for j in range(2):
        wide = refs[j].astype(jnp.float32)
        for r in range(R_DEV):
            at = r // R_OWN * 2 + j
            lanes = slice(r % R_OWN * A, r % R_OWN * A + A)
            row_of[at : at + 1, lanes] = wide[r : r + 1]
        tile = jnp.broadcast_to(sharp[...].astype(jnp.float32)[0:1, j : j + 1], (1, 128))
        for r in range(NY):
            row_of[2 * r + j : 2 * r + j + 1, WIDE:] = tile
    for r in range(NY):
        pair = row_of[2 * r : 2 * r + 2, :].astype(jnp.bfloat16)
        for z in range(NZ):
            pieces[r * NZ + z] = pair
    row, col = iota((A, A), 0), iota((A, A), 1)
    swap = (col == ((row & 15) * 16 + (row >> 4))).astype(jnp.float32).astype(jnp.bfloat16)
    for b in range(P_DEV // 16):
        if b % 2 == 0:
            copies[5 + b // 2].wait()
        x = jnp.dot(swap, images[b * A : b * A + A, :], preferred_element_type=jnp.float32)
        x = x.astype(jnp.bfloat16)
        for r in range(R_DEV):
            grid[r, b * 16 : b * 16 + 16, :] = x[r * 16 : r * 16 + 16]
    label = ints[0:1, :]
    label = ((label >> 1) & 1) * 128 + (label >> 2) * 2 + (label & 1)
    at = iota((P_DEV, P_DEV), 0)
    tail = jnp.where(at == 0, label, jnp.where(at == 1, ints[1:2, :], ints[2:3, :]))
    tail = tail.astype(jnp.float32).astype(jnp.bfloat16)
    for d, out in enumerate((out0, out1, out2, out3)):
        first = ((y + d) & (NY - 1)) * R_OWN
        for i in range(R_OWN):
            out[:, i * A : i * A + A] = grid[first + i]
        out[:, WIDE:] = tail


def align_kernel(in0, in1, in2, in3, table, phases, out, parts):
    for r in range(R_OWN):
        phase = phases[r]
        for at, value in ((0, jnp.cos(phase)), (FREQS, jnp.sin(phase))):
            high = value.astype(jnp.bfloat16)
            low = (value - high.astype(jnp.float32)).astype(jnp.bfloat16)
            lanes = slice(r * A + at, r * A + at + FREQS)
            parts[0:SHIFT_ROWS, lanes] = high
            parts[SHIFT_ROWS : 2 * SHIFT_ROWS, lanes] = low
    dft = table[...]
    diagonal = iota((P_DEV, P_DEV), 0) == iota((P_DEV, P_DEV), 1)
    lane = iota((P_DEV, P_DEV), 1)
    for d, block in enumerate((in0, in1, in2, in3)):
        rows = slice(d * P_DEV, d * P_DEV + P_DEV)
        tail = block[0:16, WIDE:].astype(jnp.float32)
        rot = jnp.sum(jnp.where(diagonal, tail[1:2], 0.0), axis=1, keepdims=True)
        shift = jnp.sum(jnp.where(diagonal, tail[2:3], 0.0), axis=1, keepdims=True)
        angle = ((rot.astype(jnp.int32) * lane) & (A - 1)).astype(jnp.float32) * (2.0 * math.pi / A)
        cos_rot, sin_rot = jnp.cos(angle), jnp.sin(angle)
        pick = (lane[:, : 2 * SHIFT_ROWS] & (SHIFT_ROWS - 1)) == shift.astype(jnp.int32)
        pick = pick.astype(jnp.float32).astype(jnp.bfloat16)
        for i in range(R_OWN):
            lanes = slice(i * A, i * A + A)
            turn = jnp.dot(pick, parts[:, lanes], preferred_element_type=jnp.float32)
            spectra = jnp.dot(block[:, lanes], dft, preferred_element_type=jnp.float32)
            cosine = turn[:, :FREQS] * cos_rot - turn[:, FREQS:] * sin_rot
            sine = turn[:, FREQS:] * cos_rot + turn[:, :FREQS] * sin_rot
            real, imag = spectra[:, :FREQS], spectra[:, FREQS:]
            out[rows, i * A : i * A + FREQS] = (real * cosine - imag * sine).astype(jnp.bfloat16)
            out[rows, i * A + FREQS : i * A + A] = (real * sine + imag * cosine).astype(jnp.bfloat16)
        out[rows, WIDE:] = block[:, WIDE:]


def labels_of(rows, first, core):
    label = rows[first : first + 16, WIDE:].astype(jnp.float32)[0:1].astype(jnp.int32)
    return label ^ (core * P_DEV)


def norm_kernel(refs, out):
    wide = refs[:, :WIDE].astype(jnp.float32)
    norm = jnp.sum(wide * wide, axis=1, keepdims=True)
    out[...] = jnp.broadcast_to(norm, (P_DEV, P_DEV))


def score_kernel(at_ref, own, other, refs, norm, out, stats):
    y, core = at_ref[0], at_ref[1]
    flat_refs = refs[:, :WIDE]
    sharp = refs[:, WIDE:].astype(jnp.float32)
    class_of = iota((P_DEV, P_DEV), 0)
    diagonal = class_of == iota((P_DEV, P_DEV), 1)
    for side, rows in enumerate((own, other)):
        for d in range(NY):
            source = (y - d) & (NY - 1)
            flat = rows[d * P_DEV : d * P_DEV + P_DEV, :WIDE]
            member = class_of == labels_of(rows, d * P_DEV, core)
            scores = lax.dot_general(
                flat_refs, flat, (((1,), (1,)), ((), ())), preferred_element_type=jnp.float32
            )
            gram = lax.dot_general(
                flat, flat, (((1,), (1,)), ((), ())), preferred_element_type=jnp.float32
            )
            inner = jnp.sum(jnp.where(member, scores * sharp, 0.0), axis=0, keepdims=True)
            power = jnp.sum(jnp.where(diagonal, gram, 0.0), axis=0, keepdims=True)
            ref_power = jnp.sum(jnp.where(member, norm[...], 0.0), axis=0, keepdims=True)
            for at, value in enumerate((inner, power, ref_power)):
                stats[pl.ds(at * 2 * NY + side * NY + source, 1), :] = value
    value = stats[...]
    for i in range(NX * NY):
        out[i] = value


def sum_kernel(at_ref, got, own, other, out, weights):
    y, core = at_ref[0], at_ref[1]
    total = got[0]
    for i in range(1, NX * NY):
        total = total + got[i]
    inner, power, ref_power = total[:8], total[8:16], total[16:]
    weight = jax.nn.sigmoid(inner / jnp.sqrt((power + EPSILON) * (ref_power + EPSILON)))
    weights[...] = weight.astype(jnp.bfloat16).astype(jnp.float32)
    spread = []
    for side, rows in enumerate((own, other)):
        parts = []
        for d in range(NY):
            source = (y - d) & (NY - 1)
            member = iota((P_DEV, P_DEV), 0) == labels_of(rows, d * P_DEV, core)
            weight = weights[pl.ds(side * NY + source, 1), :]
            parts.append(jnp.where(member, weight, 0.0).astype(jnp.bfloat16))
        spread.append(jnp.concatenate(parts, axis=1))
    for i in range(R_OWN):
        lanes = slice(i * A, i * A + A)
        sums = jnp.dot(spread[0], own[:, lanes], preferred_element_type=jnp.float32)
        sums = sums + jnp.dot(spread[1], other[:, lanes], preferred_element_type=jnp.float32)
        out[:, lanes] = sums.astype(jnp.bfloat16)
    ones = jnp.ones((NY * P_DEV, P_DEV), jnp.bfloat16)
    sums = jnp.dot(spread[0], ones, preferred_element_type=jnp.float32)
    sums = sums + jnp.dot(spread[1], ones, preferred_element_type=jnp.float32)
    high = sums.astype(jnp.bfloat16).astype(jnp.float32)
    sums = jnp.where(iota((P_DEV, P_DEV), 1) < 64, high, sums - high)
    out[:, WIDE:] = sums.astype(jnp.bfloat16)


def finish_kernel(got, out, out_weights):
    odd = (iota((2 * NZ, FULL), 0) & 1) == 1
    for r in range(NY):
        part = got[r * 2 * NZ : (r + 1) * 2 * NZ, :].astype(jnp.float32)
        for j in range(2):
            total = jnp.sum(jnp.where(odd == (j == 1), part, 0.0), axis=0, keepdims=True)
            for i in range(R_OWN):
                out[j, r * R_OWN + i : r * R_OWN + i + 1, :] = total[:, i * A : i * A + A]
            if r == 0:
                out_weights[j] = jnp.sum(total[:, WIDE:]) * (1.0 / 64.0)


VMEM = pl.BlockSpec(memory_space=pltpu.VMEM)
SMEM = pl.BlockSpec(memory_space=pltpu.SMEM)
HBM = pl.BlockSpec(memory_space=pltpu.HBM)


def call(kernel, name, outs, scratch, flops, nbytes, in_specs, out_specs):
    return pl.pallas_call(
        kernel,
        out_shape=outs,
        in_specs=in_specs,
        out_specs=out_specs,
        scratch_shapes=scratch,
        compiler_params=pltpu.CompilerParams(vmem_limit_bytes=VMEM_LIMIT),
        cost_estimate=pl.CostEstimate(flops=flops, bytes_accessed=nbytes, transcendentals=0),
        name=name,
    )


def body(images, references, sharpness, classes, rotations, shifts, shift_phase):
    y = lax.axis_index("y").astype(jnp.int32)
    core = lax.axis_index("core").astype(jnp.int32)
    shape = jax.ShapeDtypeStruct

    block = shape((P_DEV, FULL), jnp.bfloat16)
    pieces, *dealt = call(
        deal_kernel,
        "deal",
        [shape((NY * NZ, 2, FULL), jnp.bfloat16)] + [block] * NY,
        [
            pltpu.VMEM((P_DEV * R_DEV, A), jnp.bfloat16),
            pltpu.VMEM((2, R_DEV, A), jnp.bfloat16),
            pltpu.VMEM((8, P_DEV), jnp.int32),
            pltpu.VMEM((1, 2), jnp.bfloat16),
            pltpu.VMEM((2 * NY, FULL), jnp.float32),
            pltpu.VMEM((R_DEV, P_DEV, A), jnp.bfloat16),
            pltpu.SemaphoreType.DMA((9,)),
        ],
        300_000_000,
        3_000_000,
        [SMEM] + [HBM] * 6,
        [VMEM] * (1 + NY),
    )(
        y[None],
        *[
            pltpu.with_memory_space_constraint(x, pltpu.HBM)
            for x in (
                images.reshape(P_DEV * R_DEV, A),
                references,
                classes.reshape(1, P_DEV),
                rotations.reshape(1, P_DEV),
                shifts.reshape(1, P_DEV),
                sharpness.reshape(1, 2),
            )
        ],
    )
    blocks = [dealt[0]]
    for d in range(1, NY):
        blocks.append(lax.ppermute(dealt[d], "y", [(i, (i + d) % NY) for i in range(NY)]))
    pieces, blocks[1] = lax.optimization_barrier((pieces, blocks[1]))
    panel = lax.all_to_all(
        pieces, ("y", "z"), split_axis=0, concat_axis=0, tiled=True
    )
    phases = lax.dynamic_slice_in_dim(shift_phase, y * R_OWN, R_OWN, 1).transpose(1, 0, 2)
    phases = jnp.pad(phases, ((0, 0), (0, SHIFT_ROWS - 25), (0, 0)))
    rows = call(
        align_kernel,
        "align",
        shape((NY * P_DEV, FULL), jnp.bfloat16),
        [pltpu.VMEM((2 * SHIFT_ROWS, WIDE), jnp.bfloat16)],
        800_000_000,
        4_000_000,
        [VMEM] * 6,
        VMEM,
    )(*blocks, spectral_table(A), phases)

    other = lax.ppermute(rows, "core", [(0, 1), (1, 0)])
    at = jnp.stack([y, core])
    panel = panel.reshape(NY * NZ * 2, FULL)
    norm = call(
        norm_kernel,
        "norms",
        shape((P_DEV, P_DEV), jnp.float32),
        [],
        300_000,
        300_000,
        [VMEM],
        VMEM,
    )(panel)
    payload = call(
        score_kernel,
        "score",
        shape((NX * NY, 6 * NY, P_DEV), jnp.float32),
        [pltpu.VMEM((6 * NY, P_DEV), jnp.float32)],
        600_000_000,
        2_000_000,
        [SMEM] + [VMEM] * 4,
        VMEM,
    )(at, rows, other, panel, norm)
    got = lax.all_to_all(payload, ("x", "y"), split_axis=0, concat_axis=0, tiled=True)
    sums = call(
        sum_kernel,
        "sum",
        shape((P_DEV, FULL), jnp.bfloat16),
        [pltpu.VMEM((2 * NY, P_DEV), jnp.float32)],
        300_000_000,
        3_000_000,
        [SMEM] + [VMEM] * 3,
        VMEM,
    )(at, got, rows, other)
    sums = lax.all_to_all(
        sums.reshape(NY * NZ, 2, FULL), ("y", "z"), split_axis=0, concat_axis=0, tiled=True
    )
    class_sums, class_weights = call(
        finish_kernel,
        "finish",
        [shape((2, R_DEV, A), jnp.float32), shape((2,), jnp.float32)],
        [],
        1_000_000,
        400_000,
        [VMEM],
        [VMEM, SMEM],
    )(sums.reshape(NY * NZ * 2, FULL))
    return class_sums, class_weights


def solution(mesh):
    whole = Mesh(mesh.devices.reshape(NY, NZ, 2, NX), ("y", "z", "core", "x"))
    dom = ("y", "z", "core")
    return jax.shard_map(
        body,
        mesh=whole,
        in_specs=(
            P(dom, "x", None),
            P(dom, "x", None),
            P(dom),
            P(dom, None),
            P(dom),
            P(dom),
            P(None, "x", None),
        ),
        out_specs=(P(dom, "x", None), P(dom)),
        check_vma=False,
    )
```

```python
import math

import jax
import jax.numpy as jnp
from jax import lax
from jax.experimental import pallas as pl
from jax.experimental.pallas import tpu as pltpu
from jax.sharding import Mesh
from jax.sharding import PartitionSpec as P

C = 256
EPSILON = 1e-06
NY, NZ, NX = 4, 16, 4
P_DEV = 128
R_DEV = 16
A = 256
FREQS = 128
R_OWN = R_DEV // NY
WIDE = R_OWN * A
FULL = WIDE + 128
SHIFT_ROWS = 32
CHUNKS = P_DEV // 16
VMEM_LIMIT = 40 * 1024 * 1024


def spectral_table(length):
    half_len = length // 2
    angle_index = jnp.arange(length, dtype=jnp.int32)
    freq_index = jnp.arange(half_len, dtype=jnp.int32)
    turn_count = angle_index[:, None] * freq_index[None, :] % length
    radians = turn_count.astype(jnp.float32) * (2.0 * math.pi / length)
    norm_scale = 1.0 / math.sqrt(length)
    both = jnp.concatenate([jnp.cos(radians), -jnp.sin(radians)], 1) * norm_scale
    return both.astype(jnp.bfloat16)


def iota(shape, axis):
    return lax.broadcasted_iota(jnp.int32, shape, axis)


def step_of(slot, core):
    return (slot * (1 + 2 * core)) & (NY - 1)


def deal_kernel(
    at_ref,
    images_hbm,
    label_hbm,
    rot_hbm,
    shift_hbm,
    out0,
    out1,
    out2,
    out3,
    images,
    ints,
    grid,
    sems,
):
    y, core = at_ref[0], at_ref[1]
    part = P_DEV * R_DEV // CHUNKS
    copies = []
    for i in range(CHUNKS):
        rows = pl.ds(i * part, part)
        copies.append(pltpu.make_async_copy(images_hbm.at[rows], images.at[rows], sems.at[3 + i]))
    for i, source in enumerate((label_hbm, rot_hbm, shift_hbm)):
        copies.append(pltpu.make_async_copy(source, ints.at[pl.ds(i, 1)], sems.at[i]))
    for copy in copies:
        copy.start()
    row, col = iota((A, A), 0), iota((A, A), 1)
    swap = (col == ((row & 15) * 16 + (row >> 4))).astype(jnp.float32).astype(jnp.bfloat16)
    for b in range(P_DEV // 16):
        copies[b].wait()
        x = jnp.dot(swap, images[b * A : b * A + A, :], preferred_element_type=jnp.float32)
        x = x.astype(jnp.bfloat16)
        for r in range(R_DEV):
            grid[r, b * 16 : b * 16 + 16, :] = x[r * 16 : r * 16 + 16]
    for copy in copies[CHUNKS:]:
        copy.wait()
    label = ints[0:1, :]
    label = ((label >> 1) & 1) * 128 + (label >> 2) * 2 + (label & 1)
    at = iota((P_DEV, P_DEV), 0)
    tail = jnp.where(at == 0, label, jnp.where(at == 1, ints[1:2, :], ints[2:3, :]))
    tail = tail.astype(jnp.float32).astype(jnp.bfloat16)
    for slot, out in enumerate((out0, out1, out2, out3)):
        first = ((y + step_of(slot, core)) & (NY - 1)) * R_OWN
        for i in range(R_OWN):
            out[:, i * A : i * A + A] = grid[first + i]
        out[:, WIDE:] = tail


def pieces_kernel(refs_hbm, sharp_hbm, pieces, refs, sharp, row_of, sems):
    copies = [
        pltpu.make_async_copy(refs_hbm, refs, sems.at[0]),
        pltpu.make_async_copy(sharp_hbm, sharp, sems.at[1]),
    ]
    for copy in copies:
        copy.start()
    for copy in copies:
        copy.wait()
    for j in range(2):
        wide = refs[j].astype(jnp.float32)
        for r in range(R_DEV):
            at = r // R_OWN * 2 + j
            lanes = slice(r % R_OWN * A, r % R_OWN * A + A)
            row_of[at : at + 1, lanes] = wide[r : r + 1]
        tile = jnp.broadcast_to(sharp[...].astype(jnp.float32)[0:1, j : j + 1], (1, 128))
        for r in range(NY):
            row_of[2 * r + j : 2 * r + j + 1, WIDE:] = tile
    for r in range(NY):
        pair = row_of[2 * r : 2 * r + 2, :].astype(jnp.bfloat16)
        for z in range(NZ):
            pieces[r * NZ + z] = pair


def align_kernel(in0, in1, in2, in3, table, phases, out, parts):
    for r in range(R_OWN):
        phase = phases[r]
        for at, value in ((0, jnp.cos(phase)), (FREQS, jnp.sin(phase))):
            high = value.astype(jnp.bfloat16)
            low = (value - high.astype(jnp.float32)).astype(jnp.bfloat16)
            lanes = slice(r * A + at, r * A + at + FREQS)
            parts[0:SHIFT_ROWS, lanes] = high
            parts[SHIFT_ROWS : 2 * SHIFT_ROWS, lanes] = low
    dft = table[...]
    diagonal = iota((P_DEV, P_DEV), 0) == iota((P_DEV, P_DEV), 1)
    lane = iota((P_DEV, P_DEV), 1)
    for d, block in enumerate((in0, in1, in2, in3)):
        rows = slice(d * P_DEV, d * P_DEV + P_DEV)
        tail = block[0:16, WIDE:].astype(jnp.float32)
        rot = jnp.sum(jnp.where(diagonal, tail[1:2], 0.0), axis=1, keepdims=True)
        shift = jnp.sum(jnp.where(diagonal, tail[2:3], 0.0), axis=1, keepdims=True)
        angle = ((rot.astype(jnp.int32) * lane) & (A - 1)).astype(jnp.float32) * (2.0 * math.pi / A)
        cos_rot, sin_rot = jnp.cos(angle), jnp.sin(angle)
        pick = (lane[:, : 2 * SHIFT_ROWS] & (SHIFT_ROWS - 1)) == shift.astype(jnp.int32)
        pick = pick.astype(jnp.float32).astype(jnp.bfloat16)
        for i in range(R_OWN):
            lanes = slice(i * A, i * A + A)
            turn = jnp.dot(pick, parts[:, lanes], preferred_element_type=jnp.float32)
            spectra = jnp.dot(block[:, lanes], dft, preferred_element_type=jnp.float32)
            cosine = turn[:, :FREQS] * cos_rot - turn[:, FREQS:] * sin_rot
            sine = turn[:, FREQS:] * cos_rot + turn[:, :FREQS] * sin_rot
            real, imag = spectra[:, :FREQS], spectra[:, FREQS:]
            out[rows, i * A : i * A + FREQS] = (real * cosine - imag * sine).astype(jnp.bfloat16)
            out[rows, i * A + FREQS : i * A + A] = (real * sine + imag * cosine).astype(jnp.bfloat16)
        out[rows, WIDE:] = block[:, WIDE:]


def labels_of(rows, first, core):
    label = rows[first : first + 16, WIDE:].astype(jnp.float32)[0:1].astype(jnp.int32)
    return label ^ (core * P_DEV)


def norm_kernel(refs, out):
    wide = refs[:, :WIDE].astype(jnp.float32)
    norm = jnp.sum(wide * wide, axis=1, keepdims=True)
    out[...] = jnp.broadcast_to(norm, (P_DEV, P_DEV))


def score_kernel(at_ref, own, other, refs, norm, out, stats):
    y, core = at_ref[0], at_ref[1]
    flat_refs = refs[:, :WIDE]
    sharp = refs[:, WIDE:].astype(jnp.float32)
    class_of = iota((P_DEV, P_DEV), 0)
    diagonal = class_of == iota((P_DEV, P_DEV), 1)
    for side, rows in enumerate((own, other)):
        for d in range(NY):
            source = (y - step_of(d, core ^ side)) & (NY - 1)
            flat = rows[d * P_DEV : d * P_DEV + P_DEV, :WIDE]
            member = class_of == labels_of(rows, d * P_DEV, core)
            scores = lax.dot_general(
                flat_refs, flat, (((1,), (1,)), ((), ())), preferred_element_type=jnp.float32
            )
            gram = lax.dot_general(
                flat, flat, (((1,), (1,)), ((), ())), preferred_element_type=jnp.float32
            )
            inner = jnp.sum(jnp.where(member, scores * sharp, 0.0), axis=0, keepdims=True)
            power = jnp.sum(jnp.where(diagonal, gram, 0.0), axis=0, keepdims=True)
            ref_power = jnp.sum(jnp.where(member, norm[...], 0.0), axis=0, keepdims=True)
            for at, value in enumerate((inner, power, ref_power)):
                stats[pl.ds(at * 2 * NY + side * NY + source, 1), :] = value
    value = stats[...]
    for i in range(NX * NY):
        out[i] = value


def sum_kernel(at_ref, got, own, other, out, weights):
    y, core = at_ref[0], at_ref[1]
    total = got[0]
    for i in range(1, NX * NY):
        total = total + got[i]
    inner, power, ref_power = total[:8], total[8:16], total[16:]
    weight = jax.nn.sigmoid(inner / jnp.sqrt((power + EPSILON) * (ref_power + EPSILON)))
    weights[...] = weight.astype(jnp.bfloat16).astype(jnp.float32)
    spread = []
    for side, rows in enumerate((own, other)):
        parts = []
        for d in range(NY):
            source = (y - step_of(d, core ^ side)) & (NY - 1)
            member = iota((P_DEV, P_DEV), 0) == labels_of(rows, d * P_DEV, core)
            weight = weights[pl.ds(side * NY + source, 1), :]
            parts.append(jnp.where(member, weight, 0.0).astype(jnp.bfloat16))
        spread.append(jnp.concatenate(parts, axis=1))
    for i in range(R_OWN):
        lanes = slice(i * A, i * A + A)
        sums = jnp.dot(spread[0], own[:, lanes], preferred_element_type=jnp.float32)
        sums = sums + jnp.dot(spread[1], other[:, lanes], preferred_element_type=jnp.float32)
        out[:, lanes] = sums.astype(jnp.bfloat16)
    ones = jnp.ones((NY * P_DEV, P_DEV), jnp.bfloat16)
    sums = jnp.dot(spread[0], ones, preferred_element_type=jnp.float32)
    sums = sums + jnp.dot(spread[1], ones, preferred_element_type=jnp.float32)
    high = sums.astype(jnp.bfloat16).astype(jnp.float32)
    sums = jnp.where(iota((P_DEV, P_DEV), 1) < 64, high, sums - high)
    out[:, WIDE:] = sums.astype(jnp.bfloat16)


def finish_kernel(got, out, out_weights):
    odd = (iota((2 * NZ, FULL), 0) & 1) == 1
    for r in range(NY):
        part = got[r * 2 * NZ : (r + 1) * 2 * NZ, :].astype(jnp.float32)
        for j in range(2):
            total = jnp.sum(jnp.where(odd == (j == 1), part, 0.0), axis=0, keepdims=True)
            for i in range(R_OWN):
                out[j, r * R_OWN + i : r * R_OWN + i + 1, :] = total[:, i * A : i * A + A]
            if r == 0:
                out_weights[j] = jnp.sum(total[:, WIDE:]) * (1.0 / 64.0)


VMEM = pl.BlockSpec(memory_space=pltpu.VMEM)
SMEM = pl.BlockSpec(memory_space=pltpu.SMEM)
HBM = pl.BlockSpec(memory_space=pltpu.HBM)


def call(kernel, name, outs, scratch, flops, nbytes, in_specs, out_specs):
    return pl.pallas_call(
        kernel,
        out_shape=outs,
        in_specs=in_specs,
        out_specs=out_specs,
        scratch_shapes=scratch,
        compiler_params=pltpu.CompilerParams(vmem_limit_bytes=VMEM_LIMIT),
        cost_estimate=pl.CostEstimate(flops=flops, bytes_accessed=nbytes, transcendentals=0),
        name=name,
    )


def body(images, references, sharpness, classes, rotations, shifts, shift_phase):
    y = lax.axis_index("y").astype(jnp.int32)
    core = lax.axis_index("core").astype(jnp.int32)
    shape = jax.ShapeDtypeStruct

    def in_hbm(*arrays):
        return [pltpu.with_memory_space_constraint(x, pltpu.HBM) for x in arrays]

    at = jnp.stack([y, core])
    block = shape((P_DEV, FULL), jnp.bfloat16)
    dealt = call(
        deal_kernel,
        "deal",
        [block] * NY,
        [
            pltpu.VMEM((P_DEV * R_DEV, A), jnp.bfloat16),
            pltpu.VMEM((8, P_DEV), jnp.int32),
            pltpu.VMEM((R_DEV, P_DEV, A), jnp.bfloat16),
            pltpu.SemaphoreType.DMA((3 + CHUNKS,)),
        ],
        300_000_000,
        3_000_000,
        [SMEM] + [HBM] * 4,
        [VMEM] * NY,
    )(
        at,
        *in_hbm(
            images.reshape(P_DEV * R_DEV, A),
            classes.reshape(1, P_DEV),
            rotations.reshape(1, P_DEV),
            shifts.reshape(1, P_DEV),
        ),
    )
    blocks = [dealt[0]]
    for slot in range(1, NY):
        pairs = [
            (2 * i + c, 2 * ((i + step_of(slot, c)) % NY) + c) for i in range(NY) for c in range(2)
        ]
        blocks.append(lax.ppermute(dealt[slot], ("y", "core"), pairs))

    pieces = call(
        pieces_kernel,
        "pieces",
        shape((NY * NZ, 2, FULL), jnp.bfloat16),
        [
            pltpu.VMEM((2, R_DEV, A), jnp.bfloat16),
            pltpu.VMEM((1, 2), jnp.bfloat16),
            pltpu.VMEM((2 * NY, FULL), jnp.float32),
            pltpu.SemaphoreType.DMA((2,)),
        ],
        1_000_000,
        500_000,
        [HBM] * 2,
        VMEM,
    )(*in_hbm(references, sharpness.reshape(1, 2)))
    pieces, blocks[1] = lax.optimization_barrier((pieces, blocks[1]))
    panel = lax.all_to_all(pieces, ("y", "z"), split_axis=0, concat_axis=0, tiled=True)
    phases = lax.dynamic_slice_in_dim(shift_phase, y * R_OWN, R_OWN, 1).transpose(1, 0, 2)
    phases = jnp.pad(phases, ((0, 0), (0, SHIFT_ROWS - 25), (0, 0)))
    rows = call(
        align_kernel,
        "align",
        shape((NY * P_DEV, FULL), jnp.bfloat16),
        [pltpu.VMEM((2 * SHIFT_ROWS, WIDE), jnp.bfloat16)],
        800_000_000,
        4_000_000,
        [VMEM] * 6,
        VMEM,
    )(*blocks, spectral_table(A), phases)

    other = lax.ppermute(rows, "core", [(0, 1), (1, 0)])
    panel = panel.reshape(NY * NZ * 2, FULL)
    norm = call(
        norm_kernel,
        "norms",
        shape((P_DEV, P_DEV), jnp.float32),
        [],
        1_000_000_000,
        300_000,
        [VMEM],
        VMEM,
    )(panel)
    payload = call(
        score_kernel,
        "score",
        shape((NX * NY, 6 * NY, P_DEV), jnp.float32),
        [pltpu.VMEM((6 * NY, P_DEV), jnp.float32)],
        600_000_000,
        2_000_000,
        [SMEM] + [VMEM] * 4,
        VMEM,
    )(at, rows, other, panel, norm)
    got = lax.all_to_all(payload, ("x", "y"), split_axis=0, concat_axis=0, tiled=True)
    sums = call(
        sum_kernel,
        "sum",
        shape((P_DEV, FULL), jnp.bfloat16),
        [pltpu.VMEM((2 * NY, P_DEV), jnp.float32)],
        300_000_000,
        3_000_000,
        [SMEM] + [VMEM] * 3,
        VMEM,
    )(at, got, rows, other)
    sums = lax.all_to_all(
        sums.reshape(NY * NZ, 2, FULL), ("y", "z"), split_axis=0, concat_axis=0, tiled=True
    )
    class_sums, class_weights = call(
        finish_kernel,
        "finish",
        [shape((2, R_DEV, A), jnp.float32), shape((2,), jnp.float32)],
        [],
        1_000_000,
        400_000,
        [VMEM],
        [VMEM, SMEM],
    )(sums.reshape(NY * NZ * 2, FULL))
    return class_sums, class_weights


def solution(mesh):
    whole = Mesh(mesh.devices.reshape(NY, NZ, 2, NX), ("y", "z", "core", "x"))
    dom = ("y", "z", "core")
    return jax.shard_map(
        body,
        mesh=whole,
        in_specs=(
            P(dom, "x", None),
            P(dom, "x", None),
            P(dom),
            P(dom, None),
            P(dom),
            P(dom),
            P(None, "x", None),
        ),
        out_specs=(P(dom, "x", None), P(dom)),
        check_vma=False,
    )
```

```python
import math

import jax
import jax.numpy as jnp
from jax import lax
from jax.experimental import pallas as pl
from jax.experimental.pallas import tpu as pltpu
from jax.sharding import Mesh
from jax.sharding import PartitionSpec as P

C = 256
EPSILON = 1e-06
NY, NZ, NX = 4, 16, 4
P_DEV = 128
R_DEV = 16
A = 256
FREQS = 128
R_OWN = R_DEV // NY
WIDE = R_OWN * A
FULL = WIDE + 128
SHIFT_ROWS = 32
VMEM_LIMIT = 40 * 1024 * 1024


def spectral_table(length):
    half_len = length // 2
    angle_index = jnp.arange(length, dtype=jnp.int32)
    freq_index = jnp.arange(half_len, dtype=jnp.int32)
    turn_count = angle_index[:, None] * freq_index[None, :] % length
    radians = turn_count.astype(jnp.float32) * (2.0 * math.pi / length)
    norm_scale = 1.0 / math.sqrt(length)
    both = jnp.concatenate([jnp.cos(radians), -jnp.sin(radians)], 1) * norm_scale
    return both.astype(jnp.bfloat16)


def iota(shape, axis):
    return lax.broadcasted_iota(jnp.int32, shape, axis)


def deal_kernel(
    y_ref,
    images,
    refs_hbm,
    label_hbm,
    rot_hbm,
    shift_hbm,
    sharp_hbm,
    pieces,
    head,
    out0,
    out1,
    out2,
    out3,
    refs,
    ints,
    sharp,
    row_of,
    grid,
    sems,
):
    y = y_ref[0]
    copies = [
        pltpu.make_async_copy(source, target, sems.at[at])
        for at, (source, target) in enumerate(
            (
                (refs_hbm, refs),
                (label_hbm, ints.at[pl.ds(0, 1)]),
                (rot_hbm, ints.at[pl.ds(1, 1)]),
                (shift_hbm, ints.at[pl.ds(2, 1)]),
                (sharp_hbm, sharp),
            )
        )
    ]
    for copy in copies:
        copy.start()
    for copy in copies:
        copy.wait()
    for j in range(2):
        wide = refs[j].astype(jnp.float32)
        for r in range(R_DEV):
            at = r // R_OWN * 2 + j
            lanes = slice(r % R_OWN * A, r % R_OWN * A + A)
            row_of[at : at + 1, lanes] = wide[r : r + 1]
        tile = jnp.broadcast_to(sharp[...].astype(jnp.float32)[0:1, j : j + 1], (1, 128))
        for r in range(NY):
            row_of[2 * r + j : 2 * r + j + 1, WIDE:] = tile
    for r in range(NY):
        pair = row_of[2 * r : 2 * r + 2, :].astype(jnp.bfloat16)
        for z in range(NZ):
            pieces[r * NZ + z] = pair
    row, col = iota((A, A), 0), iota((A, A), 1)
    swap = (col == ((row & 15) * 16 + (row >> 4))).astype(jnp.float32).astype(jnp.bfloat16)
    for b in range(P_DEV // 16):
        x = jnp.dot(swap, images[b * A : b * A + A, :], preferred_element_type=jnp.float32)
        x = x.astype(jnp.bfloat16)
        for r in range(R_DEV):
            grid[r, b * 16 : b * 16 + 16, :] = x[r * 16 : r * 16 + 16]
    label = ints[0:1, :]
    label = ((label >> 1) & 1) * 128 + (label >> 2) * 2 + (label & 1)
    at = iota((P_DEV, P_DEV), 0)
    tail = jnp.where(at == 0, label, jnp.where(at == 1, ints[1:2, :], ints[2:3, :]))
    tail = tail.astype(jnp.float32).astype(jnp.bfloat16)
    head[...] = tail[:16]
    for d, out in enumerate((out0, out1, out2, out3)):
        first = ((y + d) & (NY - 1)) * R_OWN
        for i in range(R_OWN):
            out[:, i * A : i * A + A] = grid[first + i]
        out[:, WIDE:] = tail


def align_kernel(in0, in1, in2, in3, table, phases, out, parts):
    for r in range(R_OWN):
        phase = phases[r]
        for at, value in ((0, jnp.cos(phase)), (FREQS, jnp.sin(phase))):
            high = value.astype(jnp.bfloat16)
            low = (value - high.astype(jnp.float32)).astype(jnp.bfloat16)
            lanes = slice(r * A + at, r * A + at + FREQS)
            parts[0:SHIFT_ROWS, lanes] = high
            parts[SHIFT_ROWS : 2 * SHIFT_ROWS, lanes] = low
    dft = table[...]
    diagonal = iota((P_DEV, P_DEV), 0) == iota((P_DEV, P_DEV), 1)
    lane = iota((P_DEV, P_DEV), 1)
    for d, block in enumerate((in0, in1, in2, in3)):
        rows = slice(d * P_DEV, d * P_DEV + P_DEV)
        tail = block[0:16, WIDE:].astype(jnp.float32)
        rot = jnp.sum(jnp.where(diagonal, tail[1:2], 0.0), axis=1, keepdims=True)
        shift = jnp.sum(jnp.where(diagonal, tail[2:3], 0.0), axis=1, keepdims=True)
        angle = ((rot.astype(jnp.int32) * lane) & (A - 1)).astype(jnp.float32) * (2.0 * math.pi / A)
        cos_rot, sin_rot = jnp.cos(angle), jnp.sin(angle)
        pick = (lane[:, : 2 * SHIFT_ROWS] & (SHIFT_ROWS - 1)) == shift.astype(jnp.int32)
        pick = pick.astype(jnp.float32).astype(jnp.bfloat16)
        for i in range(R_OWN):
            lanes = slice(i * A, i * A + A)
            turn = jnp.dot(pick, parts[:, lanes], preferred_element_type=jnp.float32)
            spectra = jnp.dot(block[:, lanes], dft, preferred_element_type=jnp.float32)
            cosine = turn[:, :FREQS] * cos_rot - turn[:, FREQS:] * sin_rot
            sine = turn[:, FREQS:] * cos_rot + turn[:, :FREQS] * sin_rot
            real, imag = spectra[:, :FREQS], spectra[:, FREQS:]
            out[rows, i * A : i * A + FREQS] = (real * cosine - imag * sine).astype(jnp.bfloat16)
            out[rows, i * A + FREQS : i * A + A] = (real * sine + imag * cosine).astype(jnp.bfloat16)
        out[rows, WIDE:] = block[:, WIDE:]


def labels_of(tail, core):
    label = tail.astype(jnp.float32)[0:1].astype(jnp.int32)
    return label ^ (core * P_DEV)


def norm_kernel(refs, out):
    wide = refs[:, :WIDE].astype(jnp.float32)
    norm = jnp.sum(wide * wide, axis=1, keepdims=True)
    out[...] = jnp.broadcast_to(norm, (P_DEV, P_DEV))


def score_kernel(at_ref, own, other, head, refs, norm, out, stats):
    y, core = at_ref[0], at_ref[1]
    flat_refs = refs[:, :WIDE]
    sharp = refs[:, WIDE:].astype(jnp.float32)
    class_of = iota((P_DEV, P_DEV), 0)
    diagonal = class_of == iota((P_DEV, P_DEV), 1)
    for side, rows in enumerate((own, other)):
        for d in range(NY):
            source = (y - d) & (NY - 1)
            flat = rows[d * P_DEV : d * P_DEV + P_DEV, :WIDE]
            tail = rows[d * P_DEV : d * P_DEV + 16, WIDE:] if (side, d) != (1, 0) else head[...]
            member = class_of == labels_of(tail, core)
            scores = lax.dot_general(
                flat_refs, flat, (((1,), (1,)), ((), ())), preferred_element_type=jnp.float32
            )
            gram = lax.dot_general(
                flat, flat, (((1,), (1,)), ((), ())), preferred_element_type=jnp.float32
            )
            inner = jnp.sum(jnp.where(member, scores * sharp, 0.0), axis=0, keepdims=True)
            power = jnp.sum(jnp.where(diagonal, gram, 0.0), axis=0, keepdims=True)
            ref_power = jnp.sum(jnp.where(member, norm[...], 0.0), axis=0, keepdims=True)
            for at, value in enumerate((inner, power, ref_power)):
                stats[pl.ds(at * 2 * NY + side * NY + source, 1), :] = value
    value = stats[...]
    for i in range(NX * NY):
        out[i] = value


def sum_kernel(at_ref, got, own, other, out, weights):
    y, core = at_ref[0], at_ref[1]
    total = got[0]
    for i in range(1, NX * NY):
        total = total + got[i]
    inner, power, ref_power = total[:8], total[8:16], total[16:]
    weight = jax.nn.sigmoid(inner / jnp.sqrt((power + EPSILON) * (ref_power + EPSILON)))
    weights[...] = weight.astype(jnp.bfloat16).astype(jnp.float32)
    spread = []
    for side, rows in enumerate((own, other)):
        parts = []
        for d in range(NY):
            source = (y - d) & (NY - 1)
            member = iota((P_DEV, P_DEV), 0) == labels_of(
                rows[d * P_DEV : d * P_DEV + 16, WIDE:], core
            )
            weight = weights[pl.ds(side * NY + source, 1), :]
            parts.append(jnp.where(member, weight, 0.0).astype(jnp.bfloat16))
        spread.append(jnp.concatenate(parts, axis=1))
    for i in range(R_OWN):
        lanes = slice(i * A, i * A + A)
        sums = jnp.dot(spread[0], own[:, lanes], preferred_element_type=jnp.float32)
        sums = sums + jnp.dot(spread[1], other[:, lanes], preferred_element_type=jnp.float32)
        out[:, lanes] = sums.astype(jnp.bfloat16)
    ones = jnp.ones((NY * P_DEV, P_DEV), jnp.bfloat16)
    sums = jnp.dot(spread[0], ones, preferred_element_type=jnp.float32)
    sums = sums + jnp.dot(spread[1], ones, preferred_element_type=jnp.float32)
    high = sums.astype(jnp.bfloat16).astype(jnp.float32)
    sums = jnp.where(iota((P_DEV, P_DEV), 1) < 64, high, sums - high)
    out[:, WIDE:] = sums.astype(jnp.bfloat16)


def finish_kernel(got, out, out_weights):
    odd = (iota((2 * NZ, FULL), 0) & 1) == 1
    for r in range(NY):
        part = got[r * 2 * NZ : (r + 1) * 2 * NZ, :].astype(jnp.float32)
        for j in range(2):
            total = jnp.sum(jnp.where(odd == (j == 1), part, 0.0), axis=0, keepdims=True)
            for i in range(R_OWN):
                out[j, r * R_OWN + i : r * R_OWN + i + 1, :] = total[:, i * A : i * A + A]
            if r == 0:
                out_weights[j] = jnp.sum(total[:, WIDE:]) * (1.0 / 64.0)


VMEM = pl.BlockSpec(memory_space=pltpu.VMEM)
SMEM = pl.BlockSpec(memory_space=pltpu.SMEM)
HBM = pl.BlockSpec(memory_space=pltpu.HBM)


def call(kernel, name, outs, scratch, flops, nbytes, in_specs, out_specs):
    return pl.pallas_call(
        kernel,
        out_shape=outs,
        in_specs=in_specs,
        out_specs=out_specs,
        scratch_shapes=scratch,
        compiler_params=pltpu.CompilerParams(vmem_limit_bytes=VMEM_LIMIT),
        cost_estimate=pl.CostEstimate(flops=flops, bytes_accessed=nbytes, transcendentals=0),
        name=name,
    )


def body(images, references, sharpness, classes, rotations, shifts, shift_phase):
    y = lax.axis_index("y").astype(jnp.int32)
    core = lax.axis_index("core").astype(jnp.int32)
    shape = jax.ShapeDtypeStruct

    block = shape((P_DEV, FULL), jnp.bfloat16)
    pieces, head, *dealt = call(
        deal_kernel,
        "deal",
        [shape((NY * NZ, 2, FULL), jnp.bfloat16), shape((16, P_DEV), jnp.bfloat16)] + [block] * NY,
        [
            pltpu.VMEM((2, R_DEV, A), jnp.bfloat16),
            pltpu.VMEM((8, P_DEV), jnp.int32),
            pltpu.VMEM((1, 2), jnp.bfloat16),
            pltpu.VMEM((2 * NY, FULL), jnp.float32),
            pltpu.VMEM((R_DEV, P_DEV, A), jnp.bfloat16),
            pltpu.SemaphoreType.DMA((5,)),
        ],
        300_000_000,
        3_000_000,
        [SMEM, VMEM] + [HBM] * 5,
        [VMEM] * (2 + NY),
    )(
        y[None],
        images.reshape(P_DEV * R_DEV, A),
        *[
            pltpu.with_memory_space_constraint(x, pltpu.HBM)
            for x in (
                references,
                classes.reshape(1, P_DEV),
                rotations.reshape(1, P_DEV),
                shifts.reshape(1, P_DEV),
                sharpness.reshape(1, 2),
            )
        ],
    )
    head = lax.ppermute(head, "core", [(0, 1), (1, 0)])
    blocks = [dealt[0]]
    for d in range(1, NY):
        blocks.append(lax.ppermute(dealt[d], "y", [(i, (i + d) % NY) for i in range(NY)]))
    pieces, head = lax.optimization_barrier((pieces, head))
    panel = lax.all_to_all(
        pieces, ("y", "z"), split_axis=0, concat_axis=0, tiled=True
    )
    phases = lax.dynamic_slice_in_dim(shift_phase, y * R_OWN, R_OWN, 1).transpose(1, 0, 2)
    phases = jnp.pad(phases, ((0, 0), (0, SHIFT_ROWS - 25), (0, 0)))
    rows = call(
        align_kernel,
        "align",
        shape((NY * P_DEV, FULL), jnp.bfloat16),
        [pltpu.VMEM((2 * SHIFT_ROWS, WIDE), jnp.bfloat16)],
        800_000_000,
        4_000_000,
        [VMEM] * 6,
        VMEM,
    )(*blocks, spectral_table(A), phases)

    other = lax.ppermute(rows, "core", [(0, 1), (1, 0)])
    at = jnp.stack([y, core])
    panel = panel.reshape(NY * NZ * 2, FULL)
    norm = call(
        norm_kernel,
        "norms",
        shape((P_DEV, P_DEV), jnp.float32),
        [],
        300_000,
        300_000,
        [VMEM],
        VMEM,
    )(panel)
    payload = call(
        score_kernel,
        "score",
        shape((NX * NY, 6 * NY, P_DEV), jnp.float32),
        [pltpu.VMEM((6 * NY, P_DEV), jnp.float32)],
        600_000_000,
        2_000_000,
        [SMEM] + [VMEM] * 5,
        VMEM,
    )(at, rows, other, head, panel, norm)
    got = lax.all_to_all(payload, ("x", "y"), split_axis=0, concat_axis=0, tiled=True)
    sums = call(
        sum_kernel,
        "sum",
        shape((P_DEV, FULL), jnp.bfloat16),
        [pltpu.VMEM((2 * NY, P_DEV), jnp.float32)],
        300_000_000,
        3_000_000,
        [SMEM] + [VMEM] * 3,
        VMEM,
    )(at, got, rows, other)
    sums = lax.all_to_all(
        sums.reshape(NY * NZ, 2, FULL), ("y", "z"), split_axis=0, concat_axis=0, tiled=True
    )
    class_sums, class_weights = call(
        finish_kernel,
        "finish",
        [shape((2, R_DEV, A), jnp.float32), shape((2,), jnp.float32)],
        [],
        1_000_000,
        400_000,
        [VMEM],
        [VMEM, SMEM],
    )(sums.reshape(NY * NZ * 2, FULL))
    return class_sums, class_weights


def solution(mesh):
    whole = Mesh(mesh.devices.reshape(NY, NZ, 2, NX), ("y", "z", "core", "x"))
    dom = ("y", "z", "core")
    return jax.shard_map(
        body,
        mesh=whole,
        in_specs=(
            P(dom, "x", None),
            P(dom, "x", None),
            P(dom),
            P(dom, None),
            P(dom),
            P(dom),
            P(None, "x", None),
        ),
        out_specs=(P(dom, "x", None), P(dom)),
        check_vma=False,
    )
```

```python
import math

import jax
import jax.numpy as jnp
from jax import lax
from jax.experimental import pallas as pl
from jax.experimental.pallas import tpu as pltpu
from jax.sharding import Mesh
from jax.sharding import PartitionSpec as P

C = 256
EPSILON = 1e-06
NY, NZ, NX = 4, 16, 4
P_DEV = 128
R_DEV = 16
A = 256
FREQS = 128
R_OWN = R_DEV // NY
WIDE = R_OWN * A
FULL = WIDE + 128
SHIFT_ROWS = 32
NEAR, FAR = (0, 1, 3), 2
VMEM_LIMIT = 40 * 1024 * 1024


def spectral_table(length):
    half_len = length // 2
    angle_index = jnp.arange(length, dtype=jnp.int32)
    freq_index = jnp.arange(half_len, dtype=jnp.int32)
    turn_count = angle_index[:, None] * freq_index[None, :] % length
    radians = turn_count.astype(jnp.float32) * (2.0 * math.pi / length)
    norm_scale = 1.0 / math.sqrt(length)
    both = jnp.concatenate([jnp.cos(radians), -jnp.sin(radians)], 1) * norm_scale
    return both.astype(jnp.bfloat16)


def iota(shape, axis):
    return lax.broadcasted_iota(jnp.int32, shape, axis)


def deal_kernel(
    y_ref,
    images_hbm,
    refs_hbm,
    label_hbm,
    rot_hbm,
    shift_hbm,
    sharp_hbm,
    pieces,
    out0,
    out1,
    out2,
    out3,
    images,
    refs,
    ints,
    sharp,
    row_of,
    grid,
    sems,
):
    y = y_ref[0]
    copies = [
        pltpu.make_async_copy(source, target, sems.at[at])
        for at, (source, target) in enumerate(
            (
                (refs_hbm, refs),
                (label_hbm, ints.at[pl.ds(0, 1)]),
                (rot_hbm, ints.at[pl.ds(1, 1)]),
                (shift_hbm, ints.at[pl.ds(2, 1)]),
                (sharp_hbm, sharp),
            )
        )
    ]
    quarter = P_DEV * R_DEV // 4
    for i in range(4):
        rows = pl.ds(i * quarter, quarter)
        copies.append(pltpu.make_async_copy(images_hbm.at[rows], images.at[rows], sems.at[5 + i]))
    for copy in copies:
        copy.start()
    for copy in copies[:5]:
        copy.wait()
    for j in range(2):
        wide = refs[j].astype(jnp.float32)
        for r in range(R_DEV):
            at = r // R_OWN * 2 + j
            lanes = slice(r % R_OWN * A, r % R_OWN * A + A)
            row_of[at : at + 1, lanes] = wide[r : r + 1]
        tile = jnp.broadcast_to(sharp[...].astype(jnp.float32)[0:1, j : j + 1], (1, 128))
        for r in range(NY):
            row_of[2 * r + j : 2 * r + j + 1, WIDE:] = tile
    for r in range(NY):
        pair = row_of[2 * r : 2 * r + 2, :].astype(jnp.bfloat16)
        for z in range(NZ):
            pieces[r * NZ + z] = pair
    row, col = iota((A, A), 0), iota((A, A), 1)
    swap = (col == ((row & 15) * 16 + (row >> 4))).astype(jnp.float32).astype(jnp.bfloat16)
    for b in range(P_DEV // 16):
        if b % 2 == 0:
            copies[5 + b // 2].wait()
        x = jnp.dot(swap, images[b * A : b * A + A, :], preferred_element_type=jnp.float32)
        x = x.astype(jnp.bfloat16)
        for r in range(R_DEV):
            grid[r, b * 16 : b * 16 + 16, :] = x[r * 16 : r * 16 + 16]
    label = ints[0:1, :]
    label = ((label >> 1) & 1) * 128 + (label >> 2) * 2 + (label & 1)
    at = iota((P_DEV, P_DEV), 0)
    tail = jnp.where(at == 0, label, jnp.where(at == 1, ints[1:2, :], ints[2:3, :]))
    tail = tail.astype(jnp.float32).astype(jnp.bfloat16)
    for d, out in enumerate((out0, out1, out2, out3)):
        first = ((y + d) & (NY - 1)) * R_OWN
        for i in range(R_OWN):
            out[:, i * A : i * A + A] = grid[first + i]
        out[:, WIDE:] = tail


def align_kernel(*refs):
    *blocks, table, phases, out, parts = refs
    for r in range(R_OWN):
        phase = phases[r]
        for at, value in ((0, jnp.cos(phase)), (FREQS, jnp.sin(phase))):
            high = value.astype(jnp.bfloat16)
            low = (value - high.astype(jnp.float32)).astype(jnp.bfloat16)
            lanes = slice(r * A + at, r * A + at + FREQS)
            parts[0:SHIFT_ROWS, lanes] = high
            parts[SHIFT_ROWS : 2 * SHIFT_ROWS, lanes] = low
    dft = table[...]
    diagonal = iota((P_DEV, P_DEV), 0) == iota((P_DEV, P_DEV), 1)
    lane = iota((P_DEV, P_DEV), 1)
    for at, block in enumerate(blocks):
        rows = slice(at * P_DEV, at * P_DEV + P_DEV)
        tail = block[0:16, WIDE:].astype(jnp.float32)
        rot = jnp.sum(jnp.where(diagonal, tail[1:2], 0.0), axis=1, keepdims=True)
        shift = jnp.sum(jnp.where(diagonal, tail[2:3], 0.0), axis=1, keepdims=True)
        angle = ((rot.astype(jnp.int32) * lane) & (A - 1)).astype(jnp.float32) * (2.0 * math.pi / A)
        cos_rot, sin_rot = jnp.cos(angle), jnp.sin(angle)
        pick = (lane[:, : 2 * SHIFT_ROWS] & (SHIFT_ROWS - 1)) == shift.astype(jnp.int32)
        pick = pick.astype(jnp.float32).astype(jnp.bfloat16)
        for i in range(R_OWN):
            lanes = slice(i * A, i * A + A)
            turn = jnp.dot(pick, parts[:, lanes], preferred_element_type=jnp.float32)
            spectra = jnp.dot(block[:, lanes], dft, preferred_element_type=jnp.float32)
            cosine = turn[:, :FREQS] * cos_rot - turn[:, FREQS:] * sin_rot
            sine = turn[:, FREQS:] * cos_rot + turn[:, :FREQS] * sin_rot
            real, imag = spectra[:, :FREQS], spectra[:, FREQS:]
            out[rows, i * A : i * A + FREQS] = (real * cosine - imag * sine).astype(jnp.bfloat16)
            out[rows, i * A + FREQS : i * A + A] = (real * sine + imag * cosine).astype(jnp.bfloat16)
        out[rows, WIDE:] = block[:, WIDE:]


def blocks_of(near, far):
    return [(near, i * P_DEV, d) for i, d in enumerate(NEAR)] + [(far, 0, FAR)]


def labels_of(rows, first, core):
    label = rows[first : first + 16, WIDE:].astype(jnp.float32)[0:1].astype(jnp.int32)
    return label ^ (core * P_DEV)


def score_kernel(at_ref, near, far, other_near, other_far, refs, out, stats):
    y, core = at_ref[0], at_ref[1]
    flat_refs = refs[:, :WIDE]
    wide = flat_refs.astype(jnp.float32)
    norm = jnp.sum(wide * wide, axis=1, keepdims=True)
    sharp = refs[:, WIDE:].astype(jnp.float32)
    class_of = iota((P_DEV, P_DEV), 0)
    diagonal = class_of == iota((P_DEV, P_DEV), 1)
    for side, pair in enumerate(((near, far), (other_near, other_far))):
        for rows, first, d in blocks_of(*pair):
            source = (y - d) & (NY - 1)
            flat = rows[first : first + P_DEV, :WIDE]
            member = class_of == labels_of(rows, first, core)
            scores = lax.dot_general(
                flat_refs, flat, (((1,), (1,)), ((), ())), preferred_element_type=jnp.float32
            )
            gram = lax.dot_general(
                flat, flat, (((1,), (1,)), ((), ())), preferred_element_type=jnp.float32
            )
            inner = jnp.sum(jnp.where(member, scores * sharp, 0.0), axis=0, keepdims=True)
            power = jnp.sum(jnp.where(diagonal, gram, 0.0), axis=0, keepdims=True)
            ref_power = jnp.sum(jnp.where(member, norm, 0.0), axis=0, keepdims=True)
            for at, value in enumerate((inner, power, ref_power)):
                stats[pl.ds(at * 2 * NY + side * NY + source, 1), :] = value
    value = stats[...]
    for i in range(NX * NY):
        out[i] = value


def sum_kernel(at_ref, got, near, far, other_near, other_far, out, weights):
    y, core = at_ref[0], at_ref[1]
    total = got[0]
    for i in range(1, NX * NY):
        total = total + got[i]
    inner, power, ref_power = total[:8], total[8:16], total[16:]
    weight = jax.nn.sigmoid(inner / jnp.sqrt((power + EPSILON) * (ref_power + EPSILON)))
    weights[...] = weight.astype(jnp.bfloat16).astype(jnp.float32)
    spread, arrays = [], (near, far, other_near, other_far)
    for side in range(2):
        parts = []
        for rows, first, d in blocks_of(*arrays[2 * side : 2 * side + 2]):
            source = (y - d) & (NY - 1)
            member = iota((P_DEV, P_DEV), 0) == labels_of(rows, first, core)
            weight = weights[pl.ds(side * NY + source, 1), :]
            parts.append(jnp.where(member, weight, 0.0).astype(jnp.bfloat16))
        spread += [jnp.concatenate(parts[:-1], axis=1), parts[-1]]

    def summed(blocks):
        pairs = zip(spread, blocks)
        return sum(jnp.dot(a, b, preferred_element_type=jnp.float32) for a, b in pairs)

    for i in range(R_OWN):
        lanes = slice(i * A, i * A + A)
        out[:, lanes] = summed([rows[:, lanes] for rows in arrays]).astype(jnp.bfloat16)
    sums = summed([jnp.ones((rows.shape[0], P_DEV), jnp.bfloat16) for rows in arrays])
    high = sums.astype(jnp.bfloat16).astype(jnp.float32)
    sums = jnp.where(iota((P_DEV, P_DEV), 1) < 64, high, sums - high)
    out[:, WIDE:] = sums.astype(jnp.bfloat16)


def finish_kernel(got, out, out_weights):
    odd = (iota((2 * NZ, FULL), 0) & 1) == 1
    for r in range(NY):
        part = got[r * 2 * NZ : (r + 1) * 2 * NZ, :].astype(jnp.float32)
        for j in range(2):
            total = jnp.sum(jnp.where(odd == (j == 1), part, 0.0), axis=0, keepdims=True)
            for i in range(R_OWN):
                out[j, r * R_OWN + i : r * R_OWN + i + 1, :] = total[:, i * A : i * A + A]
            if r == 0:
                out_weights[j] = jnp.sum(total[:, WIDE:]) * (1.0 / 64.0)


VMEM = pl.BlockSpec(memory_space=pltpu.VMEM)
SMEM = pl.BlockSpec(memory_space=pltpu.SMEM)
HBM = pl.BlockSpec(memory_space=pltpu.HBM)


def call(kernel, name, outs, scratch, flops, nbytes, in_specs, out_specs):
    return pl.pallas_call(
        kernel,
        out_shape=outs,
        in_specs=in_specs,
        out_specs=out_specs,
        scratch_shapes=scratch,
        compiler_params=pltpu.CompilerParams(vmem_limit_bytes=VMEM_LIMIT),
        cost_estimate=pl.CostEstimate(flops=flops, bytes_accessed=nbytes, transcendentals=0),
        name=name,
    )


def body(images, references, sharpness, classes, rotations, shifts, shift_phase):
    y = lax.axis_index("y").astype(jnp.int32)
    core = lax.axis_index("core").astype(jnp.int32)
    shape = jax.ShapeDtypeStruct

    block = shape((P_DEV, FULL), jnp.bfloat16)
    pieces, *dealt = call(
        deal_kernel,
        "deal",
        [shape((NY * NZ, 2, FULL), jnp.bfloat16)] + [block] * NY,
        [
            pltpu.VMEM((P_DEV * R_DEV, A), jnp.bfloat16),
            pltpu.VMEM((2, R_DEV, A), jnp.bfloat16),
            pltpu.VMEM((8, P_DEV), jnp.int32),
            pltpu.VMEM((1, 2), jnp.bfloat16),
            pltpu.VMEM((2 * NY, FULL), jnp.float32),
            pltpu.VMEM((R_DEV, P_DEV, A), jnp.bfloat16),
            pltpu.SemaphoreType.DMA((9,)),
        ],
        300_000_000,
        3_000_000,
        [SMEM] + [HBM] * 6,
        [VMEM] * (1 + NY),
    )(
        y[None],
        *[
            pltpu.with_memory_space_constraint(x, pltpu.HBM)
            for x in (
                images.reshape(P_DEV * R_DEV, A),
                references,
                classes.reshape(1, P_DEV),
                rotations.reshape(1, P_DEV),
                shifts.reshape(1, P_DEV),
                sharpness.reshape(1, 2),
            )
        ],
    )
    panel = lax.all_to_all(
        pieces, ("y", "z"), split_axis=0, concat_axis=0, tiled=True
    )
    blocks = [dealt[0]]
    for d in range(1, NY):
        blocks.append(lax.ppermute(dealt[d], "y", [(i, (i + d) % NY) for i in range(NY)]))
    phases = lax.dynamic_slice_in_dim(shift_phase, y * R_OWN, R_OWN, 1).transpose(1, 0, 2)
    phases = jnp.pad(phases, ((0, 0), (0, SHIFT_ROWS - 25), (0, 0)))
    table = spectral_table(A)

    def align(name, *some):
        return call(
            align_kernel,
            name,
            shape((len(some) * P_DEV, FULL), jnp.bfloat16),
            [pltpu.VMEM((2 * SHIFT_ROWS, WIDE), jnp.bfloat16)],
            600_000_000 if len(some) > 1 else 20_000_000_000,
            1_000_000 * len(some),
            [VMEM] * (len(some) + 2),
            VMEM,
        )(*some, table, phases)

    near = align("align_near", *[blocks[d] for d in NEAR])
    far = align("align_far", blocks[FAR])
    rows = [near, far] + [lax.ppermute(part, "core", [(0, 1), (1, 0)]) for part in (near, far)]
    at = jnp.stack([y, core])
    payload = call(
        score_kernel,
        "score",
        shape((NX * NY, 6 * NY, P_DEV), jnp.float32),
        [pltpu.VMEM((6 * NY, P_DEV), jnp.float32)],
        600_000_000,
        2_000_000,
        [SMEM] + [VMEM] * 5,
        VMEM,
    )(at, *rows, panel.reshape(NY * NZ * 2, FULL))
    got = lax.all_to_all(payload, ("x", "y"), split_axis=0, concat_axis=0, tiled=True)
    sums = call(
        sum_kernel,
        "sum",
        shape((P_DEV, FULL), jnp.bfloat16),
        [pltpu.VMEM((2 * NY, P_DEV), jnp.float32)],
        300_000_000,
        3_000_000,
        [SMEM] + [VMEM] * 5,
        VMEM,
    )(at, got, *rows)
    sums = lax.all_to_all(
        sums.reshape(NY * NZ, 2, FULL), ("y", "z"), split_axis=0, concat_axis=0, tiled=True
    )
    class_sums, class_weights = call(
        finish_kernel,
        "finish",
        [shape((2, R_DEV, A), jnp.float32), shape((2,), jnp.float32)],
        [],
        1_000_000,
        400_000,
        [VMEM],
        [VMEM, SMEM],
    )(sums.reshape(NY * NZ * 2, FULL))
    return class_sums, class_weights


def solution(mesh):
    whole = Mesh(mesh.devices.reshape(NY, NZ, 2, NX), ("y", "z", "core", "x"))
    dom = ("y", "z", "core")
    return jax.shard_map(
        body,
        mesh=whole,
        in_specs=(
            P(dom, "x", None),
            P(dom, "x", None),
            P(dom),
            P(dom, None),
            P(dom),
            P(dom),
            P(None, "x", None),
        ),
        out_specs=(P(dom, "x", None), P(dom)),
        check_vma=False,
    )
```

```python
import math

import jax
import jax.numpy as jnp
from jax import lax
from jax.experimental import pallas as pl
from jax.experimental.pallas import tpu as pltpu
from jax.sharding import Mesh
from jax.sharding import PartitionSpec as P

C = 256
EPSILON = 1e-06
NY, NZ, NX = 4, 16, 4
P_DEV = 128
R_DEV = 16
A = 256
FREQS = 128
R_OWN = R_DEV // NY
WIDE = R_OWN * A
FULL = WIDE + 128
SHIFT_ROWS = 32
STEPS = (0, 1, 3, 2)
VMEM_LIMIT = 40 * 1024 * 1024


def spectral_table(length):
    half_len = length // 2
    angle_index = jnp.arange(length, dtype=jnp.int32)
    freq_index = jnp.arange(half_len, dtype=jnp.int32)
    turn_count = angle_index[:, None] * freq_index[None, :] % length
    radians = turn_count.astype(jnp.float32) * (2.0 * math.pi / length)
    norm_scale = 1.0 / math.sqrt(length)
    both = jnp.concatenate([jnp.cos(radians), -jnp.sin(radians)], 1) * norm_scale
    return both.astype(jnp.bfloat16)


def iota(shape, axis):
    return lax.broadcasted_iota(jnp.int32, shape, axis)


def deal_kernel(
    y_ref,
    images_hbm,
    refs_hbm,
    label_hbm,
    rot_hbm,
    shift_hbm,
    sharp_hbm,
    pieces,
    out0,
    out1,
    out2,
    out3,
    images,
    refs,
    ints,
    sharp,
    row_of,
    grid,
    sems,
):
    y = y_ref[0]
    copies = [
        pltpu.make_async_copy(source, target, sems.at[at])
        for at, (source, target) in enumerate(
            (
                (refs_hbm, refs),
                (label_hbm, ints.at[pl.ds(0, 1)]),
                (rot_hbm, ints.at[pl.ds(1, 1)]),
                (shift_hbm, ints.at[pl.ds(2, 1)]),
                (sharp_hbm, sharp),
            )
        )
    ]
    quarter = P_DEV * R_DEV // 4
    for i in range(4):
        rows = pl.ds(i * quarter, quarter)
        copies.append(pltpu.make_async_copy(images_hbm.at[rows], images.at[rows], sems.at[5 + i]))
    for copy in copies:
        copy.start()
    for copy in copies[:5]:
        copy.wait()
    for j in range(2):
        wide = refs[j].astype(jnp.float32)
        for r in range(R_DEV):
            at = r // R_OWN * 2 + j
            lanes = slice(r % R_OWN * A, r % R_OWN * A + A)
            row_of[at : at + 1, lanes] = wide[r : r + 1]
        tile = jnp.broadcast_to(sharp[...].astype(jnp.float32)[0:1, j : j + 1], (1, 128))
        for r in range(NY):
            row_of[2 * r + j : 2 * r + j + 1, WIDE:] = tile
    for r in range(NY):
        pair = row_of[2 * r : 2 * r + 2, :].astype(jnp.bfloat16)
        for z in range(NZ):
            pieces[r * NZ + z] = pair
    row, col = iota((A, A), 0), iota((A, A), 1)
    swap = (col == ((row & 15) * 16 + (row >> 4))).astype(jnp.float32).astype(jnp.bfloat16)
    for b in range(P_DEV // 16):
        if b % 2 == 0:
            copies[5 + b // 2].wait()
        x = jnp.dot(swap, images[b * A : b * A + A, :], preferred_element_type=jnp.float32)
        x = x.astype(jnp.bfloat16)
        for r in range(R_DEV):
            grid[r, b * 16 : b * 16 + 16, :] = x[r * 16 : r * 16 + 16]
    label = ints[0:1, :]
    label = ((label >> 1) & 1) * 128 + (label >> 2) * 2 + (label & 1)
    at = iota((P_DEV, P_DEV), 0)
    tail = jnp.where(at == 0, label, jnp.where(at == 1, ints[1:2, :], ints[2:3, :]))
    tail = tail.astype(jnp.float32).astype(jnp.bfloat16)
    for step, out in zip(STEPS, (out0, out1, out2, out3)):
        first = ((y + step) & (NY - 1)) * R_OWN
        for i in range(R_OWN):
            out[:, i * A : i * A + A] = grid[first + i]
        out[:, WIDE:] = tail


def align_kernel(in0, in1, in2, in3, table, phases, out, parts):
    for r in range(R_OWN):
        phase = phases[r]
        for at, value in ((0, jnp.cos(phase)), (FREQS, jnp.sin(phase))):
            high = value.astype(jnp.bfloat16)
            low = (value - high.astype(jnp.float32)).astype(jnp.bfloat16)
            lanes = slice(r * A + at, r * A + at + FREQS)
            parts[0:SHIFT_ROWS, lanes] = high
            parts[SHIFT_ROWS : 2 * SHIFT_ROWS, lanes] = low
    dft = table[...]
    diagonal = iota((P_DEV, P_DEV), 0) == iota((P_DEV, P_DEV), 1)
    lane = iota((P_DEV, P_DEV), 1)
    for d, block in enumerate((in0, in1, in2, in3)):
        rows = slice(d * P_DEV, d * P_DEV + P_DEV)
        tail = block[0:16, WIDE:].astype(jnp.float32)
        rot = jnp.sum(jnp.where(diagonal, tail[1:2], 0.0), axis=1, keepdims=True)
        shift = jnp.sum(jnp.where(diagonal, tail[2:3], 0.0), axis=1, keepdims=True)
        angle = ((rot.astype(jnp.int32) * lane) & (A - 1)).astype(jnp.float32) * (2.0 * math.pi / A)
        cos_rot, sin_rot = jnp.cos(angle), jnp.sin(angle)
        pick = (lane[:, : 2 * SHIFT_ROWS] & (SHIFT_ROWS - 1)) == shift.astype(jnp.int32)
        pick = pick.astype(jnp.float32).astype(jnp.bfloat16)
        for i in range(R_OWN):
            lanes = slice(i * A, i * A + A)
            turn = jnp.dot(pick, parts[:, lanes], preferred_element_type=jnp.float32)
            spectra = jnp.dot(block[:, lanes], dft, preferred_element_type=jnp.float32)
            cosine = turn[:, :FREQS] * cos_rot - turn[:, FREQS:] * sin_rot
            sine = turn[:, FREQS:] * cos_rot + turn[:, :FREQS] * sin_rot
            real, imag = spectra[:, :FREQS], spectra[:, FREQS:]
            out[rows, i * A : i * A + FREQS] = (real * cosine - imag * sine).astype(jnp.bfloat16)
            out[rows, i * A + FREQS : i * A + A] = (real * sine + imag * cosine).astype(jnp.bfloat16)
        out[rows, WIDE:] = block[:, WIDE:]


def labels_of(rows, first, core):
    label = rows[first : first + 16, WIDE:].astype(jnp.float32)[0:1].astype(jnp.int32)
    return label ^ (core * P_DEV)


def norm_kernel(refs, out):
    wide = refs[:, :WIDE].astype(jnp.float32)
    norm = jnp.sum(wide * wide, axis=1, keepdims=True)
    out[...] = jnp.broadcast_to(norm, (P_DEV, P_DEV))


def score_kernel(at_ref, own, other, refs, norm, out, stats):
    y, core = at_ref[0], at_ref[1]
    flat_refs = refs[:, :WIDE]
    sharp = refs[:, WIDE:].astype(jnp.float32)
    class_of = iota((P_DEV, P_DEV), 0)
    diagonal = class_of == iota((P_DEV, P_DEV), 1)
    for side, rows in enumerate((own, other)):
        for d in range(NY):
            source = (y - STEPS[d]) & (NY - 1)
            flat = rows[d * P_DEV : d * P_DEV + P_DEV, :WIDE]
            member = class_of == labels_of(rows, d * P_DEV, core)
            scores = lax.dot_general(
                flat_refs, flat, (((1,), (1,)), ((), ())), preferred_element_type=jnp.float32
            )
            gram = lax.dot_general(
                flat, flat, (((1,), (1,)), ((), ())), preferred_element_type=jnp.float32
            )
            inner = jnp.sum(jnp.where(member, scores * sharp, 0.0), axis=0, keepdims=True)
            power = jnp.sum(jnp.where(diagonal, gram, 0.0), axis=0, keepdims=True)
            ref_power = jnp.sum(jnp.where(member, norm[...], 0.0), axis=0, keepdims=True)
            for at, value in enumerate((inner, power, ref_power)):
                stats[pl.ds(at * 2 * NY + side * NY + source, 1), :] = value
    value = stats[...]
    for i in range(NX * NY):
        out[i] = value


def sum_kernel(at_ref, got, own, other, out, weights):
    y, core = at_ref[0], at_ref[1]
    total = got[0]
    for i in range(1, NX * NY):
        total = total + got[i]
    inner, power, ref_power = total[:8], total[8:16], total[16:]
    weight = jax.nn.sigmoid(inner / jnp.sqrt((power + EPSILON) * (ref_power + EPSILON)))
    weights[...] = weight.astype(jnp.bfloat16).astype(jnp.float32)
    spread = []
    for side, rows in enumerate((own, other)):
        parts = []
        for d in range(NY):
            source = (y - STEPS[d]) & (NY - 1)
            member = iota((P_DEV, P_DEV), 0) == labels_of(rows, d * P_DEV, core)
            weight = weights[pl.ds(side * NY + source, 1), :]
            parts.append(jnp.where(member, weight, 0.0).astype(jnp.bfloat16))
        spread.append(jnp.concatenate(parts, axis=1))
    for i in range(R_OWN):
        lanes = slice(i * A, i * A + A)
        sums = jnp.dot(spread[0], own[:, lanes], preferred_element_type=jnp.float32)
        sums = sums + jnp.dot(spread[1], other[:, lanes], preferred_element_type=jnp.float32)
        out[:, lanes] = sums.astype(jnp.bfloat16)
    ones = jnp.ones((NY * P_DEV, P_DEV), jnp.bfloat16)
    sums = jnp.dot(spread[0], ones, preferred_element_type=jnp.float32)
    sums = sums + jnp.dot(spread[1], ones, preferred_element_type=jnp.float32)
    high = sums.astype(jnp.bfloat16).astype(jnp.float32)
    sums = jnp.where(iota((P_DEV, P_DEV), 1) < 64, high, sums - high)
    out[:, WIDE:] = sums.astype(jnp.bfloat16)


def finish_kernel(got, out, out_weights):
    odd = (iota((2 * NZ, FULL), 0) & 1) == 1
    for r in range(NY):
        part = got[r * 2 * NZ : (r + 1) * 2 * NZ, :].astype(jnp.float32)
        for j in range(2):
            total = jnp.sum(jnp.where(odd == (j == 1), part, 0.0), axis=0, keepdims=True)
            for i in range(R_OWN):
                out[j, r * R_OWN + i : r * R_OWN + i + 1, :] = total[:, i * A : i * A + A]
            if r == 0:
                out_weights[j] = jnp.sum(total[:, WIDE:]) * (1.0 / 64.0)


VMEM = pl.BlockSpec(memory_space=pltpu.VMEM)
SMEM = pl.BlockSpec(memory_space=pltpu.SMEM)
HBM = pl.BlockSpec(memory_space=pltpu.HBM)


def call(kernel, name, outs, scratch, flops, nbytes, in_specs, out_specs):
    return pl.pallas_call(
        kernel,
        out_shape=outs,
        in_specs=in_specs,
        out_specs=out_specs,
        scratch_shapes=scratch,
        compiler_params=pltpu.CompilerParams(vmem_limit_bytes=VMEM_LIMIT),
        cost_estimate=pl.CostEstimate(flops=flops, bytes_accessed=nbytes, transcendentals=0),
        name=name,
    )


def body(images, references, sharpness, classes, rotations, shifts, shift_phase):
    y = lax.axis_index("y").astype(jnp.int32)
    core = lax.axis_index("core").astype(jnp.int32)
    shape = jax.ShapeDtypeStruct

    block = shape((P_DEV, FULL), jnp.bfloat16)
    pieces, *dealt = call(
        deal_kernel,
        "deal",
        [shape((NY * NZ, 2, FULL), jnp.bfloat16)] + [block] * NY,
        [
            pltpu.VMEM((P_DEV * R_DEV, A), jnp.bfloat16),
            pltpu.VMEM((2, R_DEV, A), jnp.bfloat16),
            pltpu.VMEM((8, P_DEV), jnp.int32),
            pltpu.VMEM((1, 2), jnp.bfloat16),
            pltpu.VMEM((2 * NY, FULL), jnp.float32),
            pltpu.VMEM((R_DEV, P_DEV, A), jnp.bfloat16),
            pltpu.SemaphoreType.DMA((9,)),
        ],
        300_000_000,
        3_000_000,
        [SMEM] + [HBM] * 6,
        [VMEM] * (1 + NY),
    )(
        y[None],
        *[
            pltpu.with_memory_space_constraint(x, pltpu.HBM)
            for x in (
                images.reshape(P_DEV * R_DEV, A),
                references,
                classes.reshape(1, P_DEV),
                rotations.reshape(1, P_DEV),
                shifts.reshape(1, P_DEV),
                sharpness.reshape(1, 2),
            )
        ],
    )
    blocks = [dealt[0]]
    for d in range(1, NY):
        pairs = [(i, (i + STEPS[d]) % NY) for i in range(NY)]
        blocks.append(lax.ppermute(dealt[d], "y", pairs))
    pieces, blocks[1] = lax.optimization_barrier((pieces, blocks[1]))
    panel = lax.all_to_all(
        pieces, ("y", "z"), split_axis=0, concat_axis=0, tiled=True
    )
    phases = lax.dynamic_slice_in_dim(shift_phase, y * R_OWN, R_OWN, 1).transpose(1, 0, 2)
    phases = jnp.pad(phases, ((0, 0), (0, SHIFT_ROWS - 25), (0, 0)))
    rows = call(
        align_kernel,
        "align",
        shape((NY * P_DEV, FULL), jnp.bfloat16),
        [pltpu.VMEM((2 * SHIFT_ROWS, WIDE), jnp.bfloat16)],
        800_000_000,
        4_000_000,
        [VMEM] * 6,
        VMEM,
    )(*blocks, spectral_table(A), phases)

    other = lax.ppermute(rows, "core", [(0, 1), (1, 0)])
    at = jnp.stack([y, core])
    panel = panel.reshape(NY * NZ * 2, FULL)
    norm = call(
        norm_kernel,
        "norms",
        shape((P_DEV, P_DEV), jnp.float32),
        [],
        300_000,
        300_000,
        [VMEM],
        VMEM,
    )(panel)
    payload = call(
        score_kernel,
        "score",
        shape((NX * NY, 6 * NY, P_DEV), jnp.float32),
        [pltpu.VMEM((6 * NY, P_DEV), jnp.float32)],
        600_000_000,
        2_000_000,
        [SMEM] + [VMEM] * 4,
        VMEM,
    )(at, rows, other, panel, norm)
    got = lax.all_to_all(payload, ("x", "y"), split_axis=0, concat_axis=0, tiled=True)
    sums = call(
        sum_kernel,
        "sum",
        shape((P_DEV, FULL), jnp.bfloat16),
        [pltpu.VMEM((2 * NY, P_DEV), jnp.float32)],
        300_000_000,
        3_000_000,
        [SMEM] + [VMEM] * 3,
        VMEM,
    )(at, got, rows, other)
    sums = lax.all_to_all(
        sums.reshape(NY * NZ, 2, FULL), ("y", "z"), split_axis=0, concat_axis=0, tiled=True
    )
    class_sums, class_weights = call(
        finish_kernel,
        "finish",
        [shape((2, R_DEV, A), jnp.float32), shape((2,), jnp.float32)],
        [],
        1_000_000,
        400_000,
        [VMEM],
        [VMEM, SMEM],
    )(sums.reshape(NY * NZ * 2, FULL))
    return class_sums, class_weights


def solution(mesh):
    whole = Mesh(mesh.devices.reshape(NY, NZ, 2, NX), ("y", "z", "core", "x"))
    dom = ("y", "z", "core")
    return jax.shard_map(
        body,
        mesh=whole,
        in_specs=(
            P(dom, "x", None),
            P(dom, "x", None),
            P(dom),
            P(dom, None),
            P(dom),
            P(dom),
            P(None, "x", None),
        ),
        out_specs=(P(dom, "x", None), P(dom)),
        check_vma=False,
    )
```

```python
import math

import jax
import jax.numpy as jnp
from jax import lax
from jax.experimental import pallas as pl
from jax.experimental.pallas import tpu as pltpu
from jax.sharding import Mesh
from jax.sharding import PartitionSpec as P

C = 256
EPSILON = 1e-06
NY, NZ, NX = 4, 16, 4
P_DEV = 128
R_DEV = 16
A = 256
FREQS = 128
R_OWN = R_DEV // NY
WIDE = R_OWN * A
FULL = WIDE + 128
SHIFT_ROWS = 32
STEPS = (0, 1, 3, 2)
VMEM_LIMIT = 40 * 1024 * 1024


def spectral_table(length):
    half_len = length // 2
    angle_index = jnp.arange(length, dtype=jnp.int32)
    freq_index = jnp.arange(half_len, dtype=jnp.int32)
    turn_count = angle_index[:, None] * freq_index[None, :] % length
    radians = turn_count.astype(jnp.float32) * (2.0 * math.pi / length)
    norm_scale = 1.0 / math.sqrt(length)
    both = jnp.concatenate([jnp.cos(radians), -jnp.sin(radians)], 1) * norm_scale
    return both.astype(jnp.bfloat16)


def iota(shape, axis):
    return lax.broadcasted_iota(jnp.int32, shape, axis)


def deal_kernel(
    y_ref,
    images_hbm,
    refs_hbm,
    label_hbm,
    rot_hbm,
    shift_hbm,
    sharp_hbm,
    pieces,
    out0,
    out1,
    out2,
    out3,
    images,
    refs,
    ints,
    sharp,
    row_of,
    grid,
    sems,
):
    y = y_ref[0]
    copies = [
        pltpu.make_async_copy(source, target, sems.at[at])
        for at, (source, target) in enumerate(
            (
                (refs_hbm, refs),
                (label_hbm, ints.at[pl.ds(0, 1)]),
                (rot_hbm, ints.at[pl.ds(1, 1)]),
                (shift_hbm, ints.at[pl.ds(2, 1)]),
                (sharp_hbm, sharp),
            )
        )
    ]
    half = P_DEV * R_DEV // 2
    for i in range(2):
        rows = pl.ds(i * half, half)
        copies.append(pltpu.make_async_copy(images_hbm.at[rows], images.at[rows], sems.at[5 + i]))
    for copy in copies:
        copy.start()
    for copy in copies[:5]:
        copy.wait()
    for j in range(2):
        wide = refs[j].astype(jnp.float32)
        for r in range(R_DEV):
            at = r // R_OWN * 2 + j
            lanes = slice(r % R_OWN * A, r % R_OWN * A + A)
            row_of[at : at + 1, lanes] = wide[r : r + 1]
        tile = jnp.broadcast_to(sharp[...].astype(jnp.float32)[0:1, j : j + 1], (1, 128))
        for r in range(NY):
            row_of[2 * r + j : 2 * r + j + 1, WIDE:] = tile
    for r in range(NY):
        pair = row_of[2 * r : 2 * r + 2, :].astype(jnp.bfloat16)
        for z in range(NZ):
            pieces[r * NZ + z] = pair
    row, col = iota((A, A), 0), iota((A, A), 1)
    swap = (col == ((row & 15) * 16 + (row >> 4))).astype(jnp.float32).astype(jnp.bfloat16)
    for b in range(P_DEV // 16):
        if b % 4 == 0:
            copies[5 + b // 4].wait()
        x = jnp.dot(swap, images[b * A : b * A + A, :], preferred_element_type=jnp.float32)
        x = x.astype(jnp.bfloat16)
        for r in range(R_DEV):
            grid[r, b * 16 : b * 16 + 16, :] = x[r * 16 : r * 16 + 16]
    label = ints[0:1, :]
    label = ((label >> 1) & 1) * 128 + (label >> 2) * 2 + (label & 1)
    at = iota((P_DEV, P_DEV), 0)
    tail = jnp.where(at == 0, label, jnp.where(at == 1, ints[1:2, :], ints[2:3, :]))
    tail = tail.astype(jnp.float32).astype(jnp.bfloat16)
    for step, out in zip(STEPS, (out0, out1, out2, out3)):
        first = ((y + step) & (NY - 1)) * R_OWN
        for i in range(R_OWN):
            out[:, i * A : i * A + A] = grid[first + i]
        out[:, WIDE:] = tail


def align_kernel(in0, in1, in2, in3, table, phases, out, parts):
    for r in range(R_OWN):
        phase = phases[r]
        for at, value in ((0, jnp.cos(phase)), (FREQS, jnp.sin(phase))):
            high = value.astype(jnp.bfloat16)
            low = (value - high.astype(jnp.float32)).astype(jnp.bfloat16)
            lanes = slice(r * A + at, r * A + at + FREQS)
            parts[0:SHIFT_ROWS, lanes] = high
            parts[SHIFT_ROWS : 2 * SHIFT_ROWS, lanes] = low
    dft = table[...]
    diagonal = iota((P_DEV, P_DEV), 0) == iota((P_DEV, P_DEV), 1)
    row, lane = iota((P_DEV, P_DEV), 0), iota((P_DEV, P_DEV), 1)
    for d, block in enumerate((in0, in1, in2, in3)):
        rows = slice(d * P_DEV, d * P_DEV + P_DEV)
        tail = block[0:16, WIDE:].astype(jnp.float32)
        rot = jnp.sum(jnp.where(diagonal, tail[1:2], 0.0), axis=1, keepdims=True)
        shift = jnp.sum(jnp.where(diagonal, tail[2:3], 0.0), axis=1, keepdims=True)
        angle = ((rot.astype(jnp.int32) * lane) & (A - 1)).astype(jnp.float32) * (2.0 * math.pi / A)
        cos_rot, sin_rot = jnp.cos(angle), jnp.sin(angle)
        pick = (lane[:, : 2 * SHIFT_ROWS] & (SHIFT_ROWS - 1)) == shift.astype(jnp.int32)
        pick = pick.astype(jnp.float32).astype(jnp.bfloat16)
        for i in range(R_OWN):
            lanes = slice(i * A, i * A + A)
            turn = jnp.dot(pick, parts[:, lanes], preferred_element_type=jnp.float32)
            spectra = jnp.dot(block[:, lanes], dft, preferred_element_type=jnp.float32)
            cosine = turn[:, :FREQS] * cos_rot - turn[:, FREQS:] * sin_rot
            sine = turn[:, FREQS:] * cos_rot + turn[:, :FREQS] * sin_rot
            real, imag = spectra[:, :FREQS], spectra[:, FREQS:]
            out[rows, i * A : i * A + FREQS] = (real * cosine - imag * sine).astype(jnp.bfloat16)
            out[rows, i * A + FREQS : i * A + A] = (real * sine + imag * cosine).astype(jnp.bfloat16)
        flat = out[rows, :WIDE]
        gram = lax.dot_general(
            flat, flat, (((1,), (1,)), ((), ())), preferred_element_type=jnp.float32
        )
        power = jnp.sum(jnp.where(diagonal, gram, 0.0), axis=0, keepdims=True)
        high = power.astype(jnp.bfloat16).astype(jnp.float32)
        tail = jnp.where(row == 3, high, jnp.where(row == 4, power - high, block[:, WIDE:].astype(jnp.float32)))
        out[rows, WIDE:] = tail.astype(jnp.bfloat16)


def norm_kernel(refs, out):
    wide = refs[:, :WIDE].astype(jnp.float32)
    norm = jnp.sum(wide * wide, axis=1, keepdims=True)
    out[...] = jnp.broadcast_to(norm, (P_DEV, P_DEV))


def tail_of(rows, d, core):
    tail = rows[d * P_DEV : d * P_DEV + 16, WIDE:].astype(jnp.float32)
    return tail[0:1].astype(jnp.int32) ^ (core * P_DEV), tail[3:4] + tail[4:5]


def lanes_of(side, source):
    return pl.ds(pl.multiple_of((side * NY + source) * P_DEV, P_DEV), P_DEV)


def score_kernel(at_ref, own, other, refs, norm, out, stats):
    y, core = at_ref[0], at_ref[1]
    flat_refs = refs[:, :WIDE]
    sharp = refs[:, WIDE:].astype(jnp.float32)
    class_of = iota((P_DEV, P_DEV), 0)
    diagonal = class_of == iota((P_DEV, P_DEV), 1)
    for side, rows in enumerate((own, other)):
        for d in range(NY):
            lanes = lanes_of(side, (y - STEPS[d]) & (NY - 1))
            label, power = tail_of(rows, d, core)
            scores = lax.dot_general(
                flat_refs,
                rows[d * P_DEV : d * P_DEV + P_DEV, :WIDE],
                (((1,), (1,)), ((), ())),
                preferred_element_type=jnp.float32,
            )
            inner = jnp.where(class_of == label, scores * sharp, 0.0)
            stats[0:1, lanes] = jnp.sum(inner, axis=0, keepdims=True)
            stats[1:2, lanes] = power
    norm_row = jnp.sum(jnp.where(diagonal, norm[...], 0.0), axis=0, keepdims=True)
    stats[0:1, WIDE:] = norm_row
    stats[1:2, WIDE:] = norm_row
    value = stats[...]
    for i in range(NX * NY):
        out[i] = value


def sum_kernel(at_ref, got, own, other, out, stats):
    y, core = at_ref[0], at_ref[1]
    total = got[0]
    for i in range(1, NX * NY):
        total = total + got[i]
    stats[...] = total
    class_of = iota((P_DEV, P_DEV), 0)
    diagonal = class_of == iota((P_DEV, P_DEV), 1)
    norm = jnp.sum(jnp.where(diagonal, stats[0:1, WIDE:], 0.0), axis=1, keepdims=True)
    spread = []
    for side, rows in enumerate((own, other)):
        parts = []
        for d in range(NY):
            lanes = lanes_of(side, (y - STEPS[d]) & (NY - 1))
            member = class_of == tail_of(rows, d, core)[0]
            ref_power = jnp.sum(jnp.where(member, norm, 0.0), axis=0, keepdims=True)
            inner, power = stats[0:1, lanes], stats[1:2, lanes]
            weight = jax.nn.sigmoid(inner / jnp.sqrt((power + EPSILON) * (ref_power + EPSILON)))
            weight = weight.astype(jnp.bfloat16).astype(jnp.float32)
            parts.append(jnp.where(member, weight, 0.0).astype(jnp.bfloat16))
        spread.append(jnp.concatenate(parts, axis=1))
    for i in range(R_OWN):
        lanes = slice(i * A, i * A + A)
        sums = jnp.dot(spread[0], own[:, lanes], preferred_element_type=jnp.float32)
        sums = sums + jnp.dot(spread[1], other[:, lanes], preferred_element_type=jnp.float32)
        out[:, lanes] = sums.astype(jnp.bfloat16)
    ones = jnp.ones((NY * P_DEV, P_DEV), jnp.bfloat16)
    sums = jnp.dot(spread[0], ones, preferred_element_type=jnp.float32)
    sums = sums + jnp.dot(spread[1], ones, preferred_element_type=jnp.float32)
    high = sums.astype(jnp.bfloat16).astype(jnp.float32)
    sums = jnp.where(iota((P_DEV, P_DEV), 1) < 64, high, sums - high)
    out[:, WIDE:] = sums.astype(jnp.bfloat16)


def finish_kernel(got, out, out_weights):
    odd = (iota((2 * NZ, FULL), 0) & 1) == 1
    for r in range(NY):
        part = got[r * 2 * NZ : (r + 1) * 2 * NZ, :].astype(jnp.float32)
        for j in range(2):
            total = jnp.sum(jnp.where(odd == (j == 1), part, 0.0), axis=0, keepdims=True)
            for i in range(R_OWN):
                out[j, r * R_OWN + i : r * R_OWN + i + 1, :] = total[:, i * A : i * A + A]
            if r == 0:
                out_weights[j] = jnp.sum(total[:, WIDE:]) * (1.0 / 64.0)


VMEM = pl.BlockSpec(memory_space=pltpu.VMEM)
SMEM = pl.BlockSpec(memory_space=pltpu.SMEM)
HBM = pl.BlockSpec(memory_space=pltpu.HBM)


def call(kernel, name, outs, scratch, flops, nbytes, in_specs, out_specs):
    return pl.pallas_call(
        kernel,
        out_shape=outs,
        in_specs=in_specs,
        out_specs=out_specs,
        scratch_shapes=scratch,
        compiler_params=pltpu.CompilerParams(vmem_limit_bytes=VMEM_LIMIT),
        cost_estimate=pl.CostEstimate(flops=flops, bytes_accessed=nbytes, transcendentals=0),
        name=name,
    )


def body(images, references, sharpness, classes, rotations, shifts, shift_phase):
    y = lax.axis_index("y").astype(jnp.int32)
    core = lax.axis_index("core").astype(jnp.int32)
    shape = jax.ShapeDtypeStruct

    block = shape((P_DEV, FULL), jnp.bfloat16)
    pieces, *dealt = call(
        deal_kernel,
        "deal",
        [shape((NY * NZ, 2, FULL), jnp.bfloat16)] + [block] * NY,
        [
            pltpu.VMEM((P_DEV * R_DEV, A), jnp.bfloat16),
            pltpu.VMEM((2, R_DEV, A), jnp.bfloat16),
            pltpu.VMEM((8, P_DEV), jnp.int32),
            pltpu.VMEM((1, 2), jnp.bfloat16),
            pltpu.VMEM((2 * NY, FULL), jnp.float32),
            pltpu.VMEM((R_DEV, P_DEV, A), jnp.bfloat16),
            pltpu.SemaphoreType.DMA((7,)),
        ],
        300_000_000,
        3_000_000,
        [SMEM] + [HBM] * 6,
        [VMEM] * (1 + NY),
    )(
        y[None],
        *[
            pltpu.with_memory_space_constraint(x, pltpu.HBM)
            for x in (
                images.reshape(P_DEV * R_DEV, A),
                references,
                classes.reshape(1, P_DEV),
                rotations.reshape(1, P_DEV),
                shifts.reshape(1, P_DEV),
                sharpness.reshape(1, 2),
            )
        ],
    )
    blocks = [dealt[0]]
    for d in range(1, NY):
        pairs = [(i, (i + STEPS[d]) % NY) for i in range(NY)]
        blocks.append(lax.ppermute(dealt[d], "y", pairs))
    pieces, blocks[1] = lax.optimization_barrier((pieces, blocks[1]))
    panel = lax.all_to_all(
        pieces, ("y", "z"), split_axis=0, concat_axis=0, tiled=True
    )
    phases = lax.dynamic_slice_in_dim(shift_phase, y * R_OWN, R_OWN, 1).transpose(1, 0, 2)
    phases = jnp.pad(phases, ((0, 0), (0, SHIFT_ROWS - 25), (0, 0)))
    rows = call(
        align_kernel,
        "align",
        shape((NY * P_DEV, FULL), jnp.bfloat16),
        [pltpu.VMEM((2 * SHIFT_ROWS, WIDE), jnp.bfloat16)],
        800_000_000,
        4_000_000,
        [VMEM] * 6,
        VMEM,
    )(*blocks, spectral_table(A), phases)

    other = lax.ppermute(rows, "core", [(0, 1), (1, 0)])
    at = jnp.stack([y, core])
    panel = panel.reshape(NY * NZ * 2, FULL)
    norm = call(
        norm_kernel,
        "norms",
        shape((P_DEV, P_DEV), jnp.float32),
        [],
        300_000,
        300_000,
        [VMEM],
        VMEM,
    )(panel)
    payload = call(
        score_kernel,
        "score",
        shape((NX * NY, 2, FULL), jnp.float32),
        [pltpu.VMEM((2, FULL), jnp.float32)],
        600_000_000,
        2_000_000,
        [SMEM] + [VMEM] * 4,
        VMEM,
    )(at, rows, other, panel, norm)
    got = lax.all_to_all(payload, ("x", "y"), split_axis=0, concat_axis=0, tiled=True)
    sums = call(
        sum_kernel,
        "sum",
        shape((P_DEV, FULL), jnp.bfloat16),
        [pltpu.VMEM((2, FULL), jnp.float32)],
        300_000_000,
        3_000_000,
        [SMEM] + [VMEM] * 3,
        VMEM,
    )(at, got, rows, other)
    sums = lax.all_to_all(
        sums.reshape(NY * NZ, 2, FULL), ("y", "z"), split_axis=0, concat_axis=0, tiled=True
    )
    class_sums, class_weights = call(
        finish_kernel,
        "finish",
        [shape((2, R_DEV, A), jnp.float32), shape((2,), jnp.float32)],
        [],
        1_000_000,
        400_000,
        [VMEM],
        [VMEM, SMEM],
    )(sums.reshape(NY * NZ * 2, FULL))
    return class_sums, class_weights


def solution(mesh):
    whole = Mesh(mesh.devices.reshape(NY, NZ, 2, NX), ("y", "z", "core", "x"))
    dom = ("y", "z", "core")
    return jax.shard_map(
        body,
        mesh=whole,
        in_specs=(
            P(dom, "x", None),
            P(dom, "x", None),
            P(dom),
            P(dom, None),
            P(dom),
            P(dom),
            P(None, "x", None),
        ),
        out_specs=(P(dom, "x", None), P(dom)),
        check_vma=False,
    )
```

```python
import math

import jax
import jax.numpy as jnp
from jax import lax
from jax.experimental import pallas as pl
from jax.experimental.pallas import tpu as pltpu
from jax.sharding import Mesh
from jax.sharding import PartitionSpec as P

C = 256
EPSILON = 1e-06
NY, NZ, NX = 4, 16, 4
P_DEV = 128
R_DEV = 16
A = 256
FREQS = 128
R_OWN = R_DEV // NY
WIDE = R_OWN * A
FULL = WIDE + 128
TILES = WIDE // 128
DEALT = TILES * P_DEV + 16
SHIFT_ROWS = 32
STEPS = (0, 1, 3, 2)
VMEM_LIMIT = 40 * 1024 * 1024


def spectral_table(length):
    half_len = length // 2
    angle_index = jnp.arange(length, dtype=jnp.int32)
    freq_index = jnp.arange(half_len, dtype=jnp.int32)
    turn_count = angle_index[:, None] * freq_index[None, :] % length
    radians = turn_count.astype(jnp.float32) * (2.0 * math.pi / length)
    norm_scale = 1.0 / math.sqrt(length)
    both = jnp.concatenate([jnp.cos(radians), -jnp.sin(radians)], 1) * norm_scale
    return both.astype(jnp.bfloat16)


def iota(shape, axis):
    return lax.broadcasted_iota(jnp.int32, shape, axis)


def deal_kernel(
    y_ref,
    images_hbm,
    refs_hbm,
    label_hbm,
    rot_hbm,
    shift_hbm,
    sharp_hbm,
    pieces,
    out0,
    out1,
    out2,
    out3,
    images,
    refs,
    ints,
    sharp,
    row_of,
    grid,
    sems,
):
    y = y_ref[0]
    copies = [
        pltpu.make_async_copy(source, target, sems.at[at])
        for at, (source, target) in enumerate(
            (
                (refs_hbm, refs),
                (label_hbm, ints.at[pl.ds(0, 1)]),
                (rot_hbm, ints.at[pl.ds(1, 1)]),
                (shift_hbm, ints.at[pl.ds(2, 1)]),
                (sharp_hbm, sharp),
            )
        )
    ]
    half = P_DEV * R_DEV // 2
    for i in range(2):
        rows = pl.ds(i * half, half)
        copies.append(pltpu.make_async_copy(images_hbm.at[rows], images.at[rows], sems.at[5 + i]))
    for copy in copies:
        copy.start()
    for copy in copies[:5]:
        copy.wait()
    for j in range(2):
        wide = refs[j].astype(jnp.float32)
        for r in range(R_DEV):
            at = r // R_OWN * 2 + j
            lanes = slice(r % R_OWN * A, r % R_OWN * A + A)
            row_of[at : at + 1, lanes] = wide[r : r + 1]
        tile = jnp.broadcast_to(sharp[...].astype(jnp.float32)[0:1, j : j + 1], (1, 128))
        for r in range(NY):
            row_of[2 * r + j : 2 * r + j + 1, WIDE:] = tile
    for r in range(NY):
        pair = row_of[2 * r : 2 * r + 2, :].astype(jnp.bfloat16)
        for z in range(NZ):
            pieces[r * NZ + z] = pair
    row, col = iota((A, A), 0), iota((A, A), 1)
    swap = (col == ((row & 15) * 16 + (row >> 4))).astype(jnp.float32).astype(jnp.bfloat16)
    for b in range(P_DEV // 16):
        if b % 4 == 0:
            copies[5 + b // 4].wait()
        x = jnp.dot(swap, images[b * A : b * A + A, :], preferred_element_type=jnp.float32)
        x = x.astype(jnp.bfloat16)
        for r in range(R_DEV):
            grid[r, b * 16 : b * 16 + 16, :] = x[r * 16 : r * 16 + 16]
    label = ints[0:1, :]
    label = ((label >> 1) & 1) * 128 + (label >> 2) * 2 + (label & 1)
    at = iota((16, P_DEV), 0)
    tail = jnp.where(at == 0, label, jnp.where(at == 1, ints[1:2, :], ints[2:3, :]))
    tail = tail.astype(jnp.float32).astype(jnp.bfloat16)
    for step, out in zip(STEPS, (out0, out1, out2, out3)):
        first = ((y + step) & (NY - 1)) * R_OWN
        for t in range(TILES):
            out[t * P_DEV : t * P_DEV + P_DEV, :] = grid[first + t // 2, :, t % 2 * 128 : t % 2 * 128 + 128]
        out[TILES * P_DEV :, :] = tail


def align_kernel(in0, in1, in2, in3, table, phases, out, parts):
    for r in range(R_OWN):
        phase = phases[r]
        for at, value in ((0, jnp.cos(phase)), (FREQS, jnp.sin(phase))):
            high = value.astype(jnp.bfloat16)
            low = (value - high.astype(jnp.float32)).astype(jnp.bfloat16)
            lanes = slice(r * A + at, r * A + at + FREQS)
            parts[0:SHIFT_ROWS, lanes] = high
            parts[SHIFT_ROWS : 2 * SHIFT_ROWS, lanes] = low
    dft = table[...]
    diagonal = iota((P_DEV, P_DEV), 0) == iota((P_DEV, P_DEV), 1)
    row, lane = iota((P_DEV, P_DEV), 0), iota((P_DEV, P_DEV), 1)
    for d, block in enumerate((in0, in1, in2, in3)):
        rows = slice(d * P_DEV, d * P_DEV + P_DEV)
        tail = block[TILES * P_DEV :, :].astype(jnp.float32)
        rot = jnp.sum(jnp.where(diagonal, tail[1:2], 0.0), axis=1, keepdims=True)
        shift = jnp.sum(jnp.where(diagonal, tail[2:3], 0.0), axis=1, keepdims=True)
        angle = ((rot.astype(jnp.int32) * lane) & (A - 1)).astype(jnp.float32) * (2.0 * math.pi / A)
        cos_rot, sin_rot = jnp.cos(angle), jnp.sin(angle)
        pick = (lane[:, : 2 * SHIFT_ROWS] & (SHIFT_ROWS - 1)) == shift.astype(jnp.int32)
        pick = pick.astype(jnp.float32).astype(jnp.bfloat16)
        for i in range(R_OWN):
            lanes = slice(i * A, i * A + A)
            turn = jnp.dot(pick, parts[:, lanes], preferred_element_type=jnp.float32)
            pair = [block[t * P_DEV : t * P_DEV + P_DEV, :] for t in (2 * i, 2 * i + 1)]
            angles = jnp.concatenate(pair, axis=1)
            spectra = jnp.dot(angles, dft, preferred_element_type=jnp.float32)
            cosine = turn[:, :FREQS] * cos_rot - turn[:, FREQS:] * sin_rot
            sine = turn[:, FREQS:] * cos_rot + turn[:, :FREQS] * sin_rot
            real, imag = spectra[:, :FREQS], spectra[:, FREQS:]
            out[rows, i * A : i * A + FREQS] = (real * cosine - imag * sine).astype(jnp.bfloat16)
            out[rows, i * A + FREQS : i * A + A] = (real * sine + imag * cosine).astype(jnp.bfloat16)
        flat = out[rows, :WIDE]
        gram = lax.dot_general(
            flat, flat, (((1,), (1,)), ((), ())), preferred_element_type=jnp.float32
        )
        power = jnp.sum(jnp.where(diagonal, gram, 0.0), axis=0, keepdims=True)
        high = power.astype(jnp.bfloat16).astype(jnp.float32)
        tail = jnp.where(row[:16] == 3, high, jnp.where(row[:16] == 4, power - high, tail))
        out[d * P_DEV : d * P_DEV + 16, WIDE:] = tail.astype(jnp.bfloat16)
        out[d * P_DEV + 16 : d * P_DEV + P_DEV, WIDE:] = jnp.zeros((P_DEV - 16, 128), jnp.bfloat16)


def norm_kernel(refs, out):
    wide = refs[:, :WIDE].astype(jnp.float32)
    norm = jnp.sum(wide * wide, axis=1, keepdims=True)
    out[...] = jnp.broadcast_to(norm, (P_DEV, P_DEV))


def tail_of(rows, d, core):
    tail = rows[d * P_DEV : d * P_DEV + 16, WIDE:].astype(jnp.float32)
    return tail[0:1].astype(jnp.int32) ^ (core * P_DEV), tail[3:4] + tail[4:5]


def lanes_of(side, source):
    return pl.ds(pl.multiple_of((side * NY + source) * P_DEV, P_DEV), P_DEV)


def score_kernel(at_ref, own, other, refs, norm, out, stats):
    y, core = at_ref[0], at_ref[1]
    flat_refs = refs[:, :WIDE]
    sharp = refs[:, WIDE:].astype(jnp.float32)
    class_of = iota((P_DEV, P_DEV), 0)
    diagonal = class_of == iota((P_DEV, P_DEV), 1)
    for side, rows in enumerate((own, other)):
        for d in range(NY):
            lanes = lanes_of(side, (y - STEPS[d]) & (NY - 1))
            label, power = tail_of(rows, d, core)
            scores = lax.dot_general(
                flat_refs,
                rows[d * P_DEV : d * P_DEV + P_DEV, :WIDE],
                (((1,), (1,)), ((), ())),
                preferred_element_type=jnp.float32,
            )
            inner = jnp.where(class_of == label, scores * sharp, 0.0)
            stats[0:1, lanes] = jnp.sum(inner, axis=0, keepdims=True)
            stats[1:2, lanes] = power
    norm_row = jnp.sum(jnp.where(diagonal, norm[...], 0.0), axis=0, keepdims=True)
    stats[0:1, WIDE:] = norm_row
    stats[1:2, WIDE:] = norm_row
    value = stats[...]
    for i in range(NX * NY):
        out[i] = value


def sum_kernel(at_ref, got, own, other, out, stats):
    y, core = at_ref[0], at_ref[1]
    total = got[0]
    for i in range(1, NX * NY):
        total = total + got[i]
    stats[...] = total
    class_of = iota((P_DEV, P_DEV), 0)
    diagonal = class_of == iota((P_DEV, P_DEV), 1)
    norm = jnp.sum(jnp.where(diagonal, stats[0:1, WIDE:], 0.0), axis=1, keepdims=True)
    spread = []
    for side, rows in enumerate((own, other)):
        parts = []
        for d in range(NY):
            lanes = lanes_of(side, (y - STEPS[d]) & (NY - 1))
            member = class_of == tail_of(rows, d, core)[0]
            ref_power = jnp.sum(jnp.where(member, norm, 0.0), axis=0, keepdims=True)
            inner, power = stats[0:1, lanes], stats[1:2, lanes]
            weight = jax.nn.sigmoid(inner / jnp.sqrt((power + EPSILON) * (ref_power + EPSILON)))
            weight = weight.astype(jnp.bfloat16).astype(jnp.float32)
            parts.append(jnp.where(member, weight, 0.0).astype(jnp.bfloat16))
        spread.append(jnp.concatenate(parts, axis=1))
    for i in range(R_OWN):
        lanes = slice(i * A, i * A + A)
        sums = jnp.dot(spread[0], own[:, lanes], preferred_element_type=jnp.float32)
        sums = sums + jnp.dot(spread[1], other[:, lanes], preferred_element_type=jnp.float32)
        out[:, lanes] = sums.astype(jnp.bfloat16)
    ones = jnp.ones((NY * P_DEV, P_DEV), jnp.bfloat16)
    sums = jnp.dot(spread[0], ones, preferred_element_type=jnp.float32)
    sums = sums + jnp.dot(spread[1], ones, preferred_element_type=jnp.float32)
    high = sums.astype(jnp.bfloat16).astype(jnp.float32)
    sums = jnp.where(iota((P_DEV, P_DEV), 1) < 64, high, sums - high)
    out[:, WIDE:] = sums.astype(jnp.bfloat16)


def finish_kernel(got, out, out_weights):
    odd = (iota((2 * NZ, FULL), 0) & 1) == 1
    for r in range(NY):
        part = got[r * 2 * NZ : (r + 1) * 2 * NZ, :].astype(jnp.float32)
        for j in range(2):
            total = jnp.sum(jnp.where(odd == (j == 1), part, 0.0), axis=0, keepdims=True)
            for i in range(R_OWN):
                out[j, r * R_OWN + i : r * R_OWN + i + 1, :] = total[:, i * A : i * A + A]
            if r == 0:
                out_weights[j] = jnp.sum(total[:, WIDE:]) * (1.0 / 64.0)


VMEM = pl.BlockSpec(memory_space=pltpu.VMEM)
SMEM = pl.BlockSpec(memory_space=pltpu.SMEM)
HBM = pl.BlockSpec(memory_space=pltpu.HBM)


def call(kernel, name, outs, scratch, flops, nbytes, in_specs, out_specs):
    return pl.pallas_call(
        kernel,
        out_shape=outs,
        in_specs=in_specs,
        out_specs=out_specs,
        scratch_shapes=scratch,
        compiler_params=pltpu.CompilerParams(vmem_limit_bytes=VMEM_LIMIT),
        cost_estimate=pl.CostEstimate(flops=flops, bytes_accessed=nbytes, transcendentals=0),
        name=name,
    )


def body(images, references, sharpness, classes, rotations, shifts, shift_phase):
    y = lax.axis_index("y").astype(jnp.int32)
    core = lax.axis_index("core").astype(jnp.int32)
    shape = jax.ShapeDtypeStruct

    block = shape((DEALT, 128), jnp.bfloat16)
    pieces, *dealt = call(
        deal_kernel,
        "deal",
        [shape((NY * NZ, 2, FULL), jnp.bfloat16)] + [block] * NY,
        [
            pltpu.VMEM((P_DEV * R_DEV, A), jnp.bfloat16),
            pltpu.VMEM((2, R_DEV, A), jnp.bfloat16),
            pltpu.VMEM((8, P_DEV), jnp.int32),
            pltpu.VMEM((1, 2), jnp.bfloat16),
            pltpu.VMEM((2 * NY, FULL), jnp.float32),
            pltpu.VMEM((R_DEV, P_DEV, A), jnp.bfloat16),
            pltpu.SemaphoreType.DMA((7,)),
        ],
        300_000_000,
        3_000_000,
        [SMEM] + [HBM] * 6,
        [VMEM] * (1 + NY),
    )(
        y[None],
        *[
            pltpu.with_memory_space_constraint(x, pltpu.HBM)
            for x in (
                images.reshape(P_DEV * R_DEV, A),
                references,
                classes.reshape(1, P_DEV),
                rotations.reshape(1, P_DEV),
                shifts.reshape(1, P_DEV),
                sharpness.reshape(1, 2),
            )
        ],
    )
    blocks = [dealt[0]]
    for d in range(1, NY):
        pairs = [(i, (i + STEPS[d]) % NY) for i in range(NY)]
        blocks.append(lax.ppermute(dealt[d], "y", pairs))
    pieces, blocks[1] = lax.optimization_barrier((pieces, blocks[1]))
    panel = lax.all_to_all(
        pieces, ("y", "z"), split_axis=0, concat_axis=0, tiled=True
    )
    phases = lax.dynamic_slice_in_dim(shift_phase, y * R_OWN, R_OWN, 1).transpose(1, 0, 2)
    phases = jnp.pad(phases, ((0, 0), (0, SHIFT_ROWS - 25), (0, 0)))
    rows = call(
        align_kernel,
        "align",
        shape((NY * P_DEV, FULL), jnp.bfloat16),
        [pltpu.VMEM((2 * SHIFT_ROWS, WIDE), jnp.bfloat16)],
        800_000_000,
        4_000_000,
        [VMEM] * 6,
        VMEM,
    )(*blocks, spectral_table(A), phases)

    other = lax.ppermute(rows, "core", [(0, 1), (1, 0)])
    at = jnp.stack([y, core])
    panel = panel.reshape(NY * NZ * 2, FULL)
    norm = call(
        norm_kernel,
        "norms",
        shape((P_DEV, P_DEV), jnp.float32),
        [],
        300_000,
        300_000,
        [VMEM],
        VMEM,
    )(panel)
    payload = call(
        score_kernel,
        "score",
        shape((NX * NY, 2, FULL), jnp.float32),
        [pltpu.VMEM((2, FULL), jnp.float32)],
        600_000_000,
        2_000_000,
        [SMEM] + [VMEM] * 4,
        VMEM,
    )(at, rows, other, panel, norm)
    got = lax.all_to_all(payload, ("x", "y"), split_axis=0, concat_axis=0, tiled=True)
    sums = call(
        sum_kernel,
        "sum",
        shape((P_DEV, FULL), jnp.bfloat16),
        [pltpu.VMEM((2, FULL), jnp.float32)],
        300_000_000,
        3_000_000,
        [SMEM] + [VMEM] * 3,
        VMEM,
    )(at, got, rows, other)
    sums = lax.all_to_all(
        sums.reshape(NY * NZ, 2, FULL), ("y", "z"), split_axis=0, concat_axis=0, tiled=True
    )
    class_sums, class_weights = call(
        finish_kernel,
        "finish",
        [shape((2, R_DEV, A), jnp.float32), shape((2,), jnp.float32)],
        [],
        1_000_000,
        400_000,
        [VMEM],
        [VMEM, SMEM],
    )(sums.reshape(NY * NZ * 2, FULL))
    return class_sums, class_weights


def solution(mesh):
    whole = Mesh(mesh.devices.reshape(NY, NZ, 2, NX), ("y", "z", "core", "x"))
    dom = ("y", "z", "core")
    return jax.shard_map(
        body,
        mesh=whole,
        in_specs=(
            P(dom, "x", None),
            P(dom, "x", None),
            P(dom),
            P(dom, None),
            P(dom),
            P(dom),
            P(None, "x", None),
        ),
        out_specs=(P(dom, "x", None), P(dom)),
        check_vma=False,
    )
```

```python
import math

import jax
import jax.numpy as jnp
from jax import lax
from jax.experimental import pallas as pl
from jax.experimental.pallas import tpu as pltpu
from jax.sharding import Mesh
from jax.sharding import PartitionSpec as P

C = 256
EPSILON = 1e-06
NY, NZ, NX = 4, 16, 4
P_DEV = 128
R_DEV = 16
A = 256
FREQS = 128
R_OWN = R_DEV // NY
WIDE = R_OWN * A
FULL = WIDE + 128
TILES = WIDE // 128
DEALT = TILES * P_DEV + 16
SHIFT_ROWS = 32
STEPS = (0, 1, 3, 2)
VMEM_LIMIT = 40 * 1024 * 1024


def spectral_table(length):
    half_len = length // 2
    angle_index = jnp.arange(length, dtype=jnp.int32)
    freq_index = jnp.arange(half_len, dtype=jnp.int32)
    turn_count = angle_index[:, None] * freq_index[None, :] % length
    radians = turn_count.astype(jnp.float32) * (2.0 * math.pi / length)
    norm_scale = 1.0 / math.sqrt(length)
    both = jnp.concatenate([jnp.cos(radians), -jnp.sin(radians)], 1) * norm_scale
    return both.astype(jnp.bfloat16)


def iota(shape, axis):
    return lax.broadcasted_iota(jnp.int32, shape, axis)


def deal_kernel(
    y_ref,
    images_hbm,
    refs_hbm,
    label_hbm,
    rot_hbm,
    shift_hbm,
    sharp_hbm,
    pieces,
    out0,
    out1,
    out2,
    out3,
    images,
    refs,
    ints,
    sharp,
    row_of,
    grid,
    sems,
):
    y = y_ref[0]
    copies = [
        pltpu.make_async_copy(source, target, sems.at[at])
        for at, (source, target) in enumerate(
            (
                (refs_hbm, refs),
                (label_hbm, ints.at[pl.ds(0, 1)]),
                (rot_hbm, ints.at[pl.ds(1, 1)]),
                (shift_hbm, ints.at[pl.ds(2, 1)]),
                (sharp_hbm, sharp),
            )
        )
    ]
    half = P_DEV * R_DEV // 2
    for i in range(2):
        rows = pl.ds(i * half, half)
        copies.append(pltpu.make_async_copy(images_hbm.at[rows], images.at[rows], sems.at[5 + i]))
    for copy in copies:
        copy.start()
    for copy in copies[:5]:
        copy.wait()
    for j in range(2):
        wide = refs[j].astype(jnp.float32)
        for r in range(R_DEV):
            at = r // R_OWN * 2 + j
            lanes = slice(r % R_OWN * A, r % R_OWN * A + A)
            row_of[at : at + 1, lanes] = wide[r : r + 1]
        tile = jnp.broadcast_to(sharp[...].astype(jnp.float32)[0:1, j : j + 1], (1, 128))
        for r in range(NY):
            row_of[2 * r + j : 2 * r + j + 1, WIDE:] = tile
    for r in range(NY):
        pair = row_of[2 * r : 2 * r + 2, :].astype(jnp.bfloat16)
        for z in range(NZ):
            pieces[r * NZ + z] = pair
    row, col = iota((A, A), 0), iota((A, A), 1)
    swap = (col == ((row & 15) * 16 + (row >> 4))).astype(jnp.float32).astype(jnp.bfloat16)
    for b in range(P_DEV // 16):
        if b % 4 == 0:
            copies[5 + b // 4].wait()
        x = jnp.dot(swap, images[b * A : b * A + A, :], preferred_element_type=jnp.float32)
        x = x.astype(jnp.bfloat16)
        for r in range(R_DEV):
            grid[r, b * 16 : b * 16 + 16, :] = x[r * 16 : r * 16 + 16]
    label = ints[0:1, :]
    label = ((label >> 1) & 1) * 128 + (label >> 2) * 2 + (label & 1)
    at = iota((16, P_DEV), 0)
    tail = jnp.where(at == 0, label, jnp.where(at == 1, ints[1:2, :], ints[2:3, :]))
    tail = tail.astype(jnp.float32).astype(jnp.bfloat16)
    for step, out in zip(STEPS, (out0, out1, out2, out3)):
        first = ((y + step) & (NY - 1)) * R_OWN
        for t in range(TILES):
            out[t * P_DEV : t * P_DEV + P_DEV, :] = grid[first + t // 2, :, t % 2 * 128 : t % 2 * 128 + 128]
        out[TILES * P_DEV :, :] = tail


def align_kernel(in0, in1, in2, in3, table, phases, out, parts):
    for r in range(R_OWN):
        phase = phases[r]
        for at, value in ((0, jnp.cos(phase)), (FREQS, jnp.sin(phase))):
            high = value.astype(jnp.bfloat16)
            low = (value - high.astype(jnp.float32)).astype(jnp.bfloat16)
            lanes = slice(r * A + at, r * A + at + FREQS)
            parts[0:SHIFT_ROWS, lanes] = high
            parts[SHIFT_ROWS : 2 * SHIFT_ROWS, lanes] = low
    dft = table[...]
    diagonal = iota((P_DEV, P_DEV), 0) == iota((P_DEV, P_DEV), 1)
    row, lane = iota((P_DEV, P_DEV), 0), iota((P_DEV, P_DEV), 1)
    for d, block in enumerate((in0, in1, in2, in3)):
        rows = slice(d * P_DEV, d * P_DEV + P_DEV)
        tail = block[TILES * P_DEV :, :].astype(jnp.float32)
        rot = jnp.sum(jnp.where(diagonal, tail[1:2], 0.0), axis=1, keepdims=True)
        shift = jnp.sum(jnp.where(diagonal, tail[2:3], 0.0), axis=1, keepdims=True)
        angle = ((rot.astype(jnp.int32) * lane) & (A - 1)).astype(jnp.float32) * (2.0 * math.pi / A)
        cos_rot, sin_rot = jnp.cos(angle), jnp.sin(angle)
        pick = (lane[:, : 2 * SHIFT_ROWS] & (SHIFT_ROWS - 1)) == shift.astype(jnp.int32)
        pick = pick.astype(jnp.float32).astype(jnp.bfloat16)
        for i in range(R_OWN):
            lanes = slice(i * A, i * A + A)
            turn = jnp.dot(pick, parts[:, lanes], preferred_element_type=jnp.float32)
            pair = [block[t * P_DEV : t * P_DEV + P_DEV, :] for t in (2 * i, 2 * i + 1)]
            angles = jnp.concatenate(pair, axis=1)
            spectra = jnp.dot(angles, dft, preferred_element_type=jnp.float32)
            cosine = turn[:, :FREQS] * cos_rot - turn[:, FREQS:] * sin_rot
            sine = turn[:, FREQS:] * cos_rot + turn[:, :FREQS] * sin_rot
            real, imag = spectra[:, :FREQS], spectra[:, FREQS:]
            out[rows, i * A : i * A + FREQS] = (real * cosine - imag * sine).astype(jnp.bfloat16)
            out[rows, i * A + FREQS : i * A + A] = (real * sine + imag * cosine).astype(jnp.bfloat16)
        flat = out[rows, :WIDE]
        gram = lax.dot_general(
            flat, flat, (((1,), (1,)), ((), ())), preferred_element_type=jnp.float32
        )
        power = jnp.sum(jnp.where(diagonal, gram, 0.0), axis=0, keepdims=True)
        high = power.astype(jnp.bfloat16).astype(jnp.float32)
        tail = jnp.where(row[:16] == 3, high, jnp.where(row[:16] == 4, power - high, tail))
        out[d * P_DEV : d * P_DEV + 16, WIDE:] = tail.astype(jnp.bfloat16)
        out[d * P_DEV + 16 : d * P_DEV + P_DEV, WIDE:] = jnp.zeros((P_DEV - 16, 128), jnp.bfloat16)


def norm_kernel(refs, out):
    wide = refs[:, :WIDE].astype(jnp.float32)
    norm = jnp.sum(wide * wide, axis=1, keepdims=True)
    out[...] = jnp.broadcast_to(norm, (P_DEV, P_DEV))


def tail_of(rows, d, core):
    tail = rows[d * P_DEV : d * P_DEV + 16, WIDE:].astype(jnp.float32)
    return tail[0:1].astype(jnp.int32) ^ (core * P_DEV), tail[3:4] + tail[4:5]


def lanes_of(side, source):
    return pl.ds(pl.multiple_of((side * NY + source) * P_DEV, P_DEV), P_DEV)


def score_kernel(at_ref, own, other, refs, norm, out, stats):
    y, core = at_ref[0], at_ref[1]
    flat_refs = refs[:, :WIDE]
    sharp = refs[:, WIDE:].astype(jnp.float32)
    class_of = iota((P_DEV, P_DEV), 0)
    diagonal = class_of == iota((P_DEV, P_DEV), 1)
    for side, rows in enumerate((own, other)):
        for d in range(NY):
            lanes = lanes_of(side, (y - STEPS[d]) & (NY - 1))
            label, power = tail_of(rows, d, core)
            scores = lax.dot_general(
                flat_refs,
                rows[d * P_DEV : d * P_DEV + P_DEV, :WIDE],
                (((1,), (1,)), ((), ())),
                preferred_element_type=jnp.float32,
            )
            inner = jnp.where(class_of == label, scores * sharp, 0.0)
            stats[0:1, lanes] = jnp.sum(inner, axis=0, keepdims=True)
            stats[1:2, lanes] = power
    norm_row = jnp.sum(jnp.where(diagonal, norm[...], 0.0), axis=0, keepdims=True)
    stats[0:1, WIDE:] = norm_row
    stats[1:2, WIDE:] = norm_row
    value = stats[...]
    for i in range(NX * NY):
        out[i] = value


def sum_kernel(at_ref, got, own, other, out, stats):
    y, core = at_ref[0], at_ref[1]
    total = got[0]
    for i in range(1, NX * NY):
        total = total + got[i]
    stats[...] = total
    class_of = iota((P_DEV, P_DEV), 0)
    diagonal = class_of == iota((P_DEV, P_DEV), 1)
    norm = jnp.sum(jnp.where(diagonal, stats[0:1, WIDE:], 0.0), axis=1, keepdims=True)
    spread = []
    for side, rows in enumerate((own, other)):
        parts = []
        for d in range(NY):
            lanes = lanes_of(side, (y - STEPS[d]) & (NY - 1))
            member = class_of == tail_of(rows, d, core)[0]
            ref_power = jnp.sum(jnp.where(member, norm, 0.0), axis=0, keepdims=True)
            inner, power = stats[0:1, lanes], stats[1:2, lanes]
            weight = jax.nn.sigmoid(inner / jnp.sqrt((power + EPSILON) * (ref_power + EPSILON)))
            weight = weight.astype(jnp.bfloat16).astype(jnp.float32)
            parts.append(jnp.where(member, weight, 0.0).astype(jnp.bfloat16))
        spread.append(jnp.concatenate(parts, axis=1))
    for i in range(R_OWN):
        lanes = slice(i * A, i * A + A)
        sums = jnp.dot(spread[0], own[:, lanes], preferred_element_type=jnp.float32)
        sums = sums + jnp.dot(spread[1], other[:, lanes], preferred_element_type=jnp.float32)
        out[:, lanes] = sums.astype(jnp.bfloat16)
    ones = jnp.ones((NY * P_DEV, P_DEV), jnp.bfloat16)
    sums = jnp.dot(spread[0], ones, preferred_element_type=jnp.float32)
    sums = sums + jnp.dot(spread[1], ones, preferred_element_type=jnp.float32)
    high = sums.astype(jnp.bfloat16).astype(jnp.float32)
    sums = jnp.where(iota((P_DEV, P_DEV), 1) < 64, high, sums - high)
    out[:, WIDE:] = sums.astype(jnp.bfloat16)


def finish_kernel(got, out, out_weights):
    odd = (iota((2 * NZ, FULL), 0) & 1) == 1
    for r in range(NY):
        part = got[r * 2 * NZ : (r + 1) * 2 * NZ, :].astype(jnp.float32)
        for j in range(2):
            total = jnp.sum(jnp.where(odd == (j == 1), part, 0.0), axis=0, keepdims=True)
            for i in range(R_OWN):
                out[j, r * R_OWN + i : r * R_OWN + i + 1, :] = total[:, i * A : i * A + A]
            if r == 0:
                out_weights[j] = jnp.sum(total[:, WIDE:]) * (1.0 / 64.0)


VMEM = pl.BlockSpec(memory_space=pltpu.VMEM)
SMEM = pl.BlockSpec(memory_space=pltpu.SMEM)
HBM = pl.BlockSpec(memory_space=pltpu.HBM)


def call(kernel, name, outs, scratch, flops, nbytes, in_specs, out_specs):
    return pl.pallas_call(
        kernel,
        out_shape=outs,
        in_specs=in_specs,
        out_specs=out_specs,
        scratch_shapes=scratch,
        compiler_params=pltpu.CompilerParams(vmem_limit_bytes=VMEM_LIMIT),
        cost_estimate=pl.CostEstimate(flops=flops, bytes_accessed=nbytes, transcendentals=0),
        name=name,
    )


def body(images, references, sharpness, classes, rotations, shifts, shift_phase):
    y = lax.axis_index("y").astype(jnp.int32)
    core = lax.axis_index("core").astype(jnp.int32)
    shape = jax.ShapeDtypeStruct

    block = shape((DEALT, 128), jnp.bfloat16)
    pieces, *dealt = call(
        deal_kernel,
        "deal",
        [shape((NY * NZ, 2, FULL), jnp.bfloat16)] + [block] * NY,
        [
            pltpu.VMEM((P_DEV * R_DEV, A), jnp.bfloat16),
            pltpu.VMEM((2, R_DEV, A), jnp.bfloat16),
            pltpu.VMEM((8, P_DEV), jnp.int32),
            pltpu.VMEM((1, 2), jnp.bfloat16),
            pltpu.VMEM((2 * NY, FULL), jnp.float32),
            pltpu.VMEM((R_DEV, P_DEV, A), jnp.bfloat16),
            pltpu.SemaphoreType.DMA((7,)),
        ],
        300_000_000,
        3_000_000,
        [SMEM] + [HBM] * 6,
        [VMEM] * (1 + NY),
    )(
        y[None],
        *[
            pltpu.with_memory_space_constraint(x, pltpu.HBM)
            for x in (
                images.reshape(P_DEV * R_DEV, A),
                references,
                classes.reshape(1, P_DEV),
                rotations.reshape(1, P_DEV),
                shifts.reshape(1, P_DEV),
                sharpness.reshape(1, 2),
            )
        ],
    )
    def permuted(block, steps):
        return lax.ppermute(block, "y", [(i, (i + steps) % NY) for i in range(NY)])

    near = [permuted(dealt[d], STEPS[d]) for d in (1, 2)]
    pieces, near[0] = lax.optimization_barrier((pieces, near[0]))
    far, near[1] = lax.optimization_barrier((dealt[3], near[1]))
    blocks = [dealt[0], *near, permuted(far, STEPS[3])]
    panel = lax.all_to_all(
        pieces, ("y", "z"), split_axis=0, concat_axis=0, tiled=True
    )
    phases = lax.dynamic_slice_in_dim(shift_phase, y * R_OWN, R_OWN, 1).transpose(1, 0, 2)
    phases = jnp.pad(phases, ((0, 0), (0, SHIFT_ROWS - 25), (0, 0)))
    rows = call(
        align_kernel,
        "align",
        shape((NY * P_DEV, FULL), jnp.bfloat16),
        [pltpu.VMEM((2 * SHIFT_ROWS, WIDE), jnp.bfloat16)],
        800_000_000,
        4_000_000,
        [VMEM] * 6,
        VMEM,
    )(*blocks, spectral_table(A), phases)

    other = lax.ppermute(rows, "core", [(0, 1), (1, 0)])
    at = jnp.stack([y, core])
    panel = panel.reshape(NY * NZ * 2, FULL)
    norm = call(
        norm_kernel,
        "norms",
        shape((P_DEV, P_DEV), jnp.float32),
        [],
        5_000_000_000,
        300_000,
        [VMEM],
        VMEM,
    )(panel)
    payload = call(
        score_kernel,
        "score",
        shape((NX * NY, 2, FULL), jnp.float32),
        [pltpu.VMEM((2, FULL), jnp.float32)],
        600_000_000,
        2_000_000,
        [SMEM] + [VMEM] * 4,
        VMEM,
    )(at, rows, other, panel, norm)
    got = lax.all_to_all(payload, ("x", "y"), split_axis=0, concat_axis=0, tiled=True)
    sums = call(
        sum_kernel,
        "sum",
        shape((P_DEV, FULL), jnp.bfloat16),
        [pltpu.VMEM((2, FULL), jnp.float32)],
        300_000_000,
        3_000_000,
        [SMEM] + [VMEM] * 3,
        VMEM,
    )(at, got, rows, other)
    sums = lax.all_to_all(
        sums.reshape(NY * NZ, 2, FULL), ("y", "z"), split_axis=0, concat_axis=0, tiled=True
    )
    class_sums, class_weights = call(
        finish_kernel,
        "finish",
        [shape((2, R_DEV, A), jnp.float32), shape((2,), jnp.float32)],
        [],
        1_000_000,
        400_000,
        [VMEM],
        [VMEM, SMEM],
    )(sums.reshape(NY * NZ * 2, FULL))
    return class_sums, class_weights


def solution(mesh):
    whole = Mesh(mesh.devices.reshape(NY, NZ, 2, NX), ("y", "z", "core", "x"))
    dom = ("y", "z", "core")
    return jax.shard_map(
        body,
        mesh=whole,
        in_specs=(
            P(dom, "x", None),
            P(dom, "x", None),
            P(dom),
            P(dom, None),
            P(dom),
            P(dom),
            P(None, "x", None),
        ),
        out_specs=(P(dom, "x", None), P(dom)),
        check_vma=False,
    )
```
